32 devices in a mesh: graph: 8 (over z, y), leaf: 4 (over x, core).
Axes of the slice: x: 2, y: 2, z: 4, core: 2. Of those that a mesh axis runs over, the one named last changes fastest.
Arguments:
- weights: float32 [2, 1171200], P(None, ('graph', 'leaf'))
- first_moment: float32 [2, 1171200], P(None, ('graph', 'leaf'))
- second_moment: float32 [2, 1171200], P(None, ('graph', 'leaf'))
- centers: bfloat16 [8, 80, 300], P('graph'), may hold values from -6 to 6
- leaves: bfloat16 [8, 4096, 300], P('graph', 'leaf'), may hold values from -6 to 6
- edge_feats: bfloat16 [8, 4096, 300], P('graph', 'leaf'), may hold values from -6 to 6
- center_cot: bfloat16 [8, 80, 300], P('graph'), may hold values from -6 to 6
- leaf_cot: bfloat16 [8, 4096, 300], P('graph', 'leaf'), may hold values from -6 to 6
- edge_cot: bfloat16 [8, 4096, 300], P('graph', 'leaf'), may hold values from -6 to 6
- graph_ids: int32 [8, 4096], P('graph', 'leaf'), may hold values from 0 to 79, never falling along the last dimension, each value on 1 to 100 neighbouring positions
- star_sizes: int32 [8, 80], P('graph'), may hold values from 5 to 100
- leaf_mask: int32 [8, 4096], P('graph', 'leaf'), may hold values 0 or 1
- owner_list: int32 [32], replicated, may hold values from 0 to 31, as said below
Outputs:
- centers_out: bfloat16 [8, 80, 300], P('graph')
- leaves_out: bfloat16 [8, 4096, 300], P('graph', 'leaf')
- edges_out: bfloat16 [8, 4096, 300], P('graph', 'leaf')
- grad_centers: float32 [8, 80, 300], P('graph')
- grad_leaves: float32 [8, 4096, 300], P('graph', 'leaf')
- grad_edges: float32 [8, 4096, 300], P('graph', 'leaf')
- first_new: float32 [2, 1171200], P(None, ('graph', 'leaf'))
- second_new: float32 [2, 1171200], P(None, ('graph', 'leaf'))
- weights_new: float32 [2, 1171200], P(None, ('graph', 'leaf'))
- weights_low: bfloat16 [2, 1171200], P(None, ('graph', 'leaf'))
- weight_grads: float32 [2, 1171200], P(None, ('graph', 'leaf'))
The draws below stay inside these ranges and needn't reach their ends.
Inputs may be any that keep to these rules, and one draw needn't show every extreme that they name: `graph_ids`: star numbers never fall along a group's slots; each star has 1 to 100 slots, one exactly 100. `owner_list`: a permutation of the holders.
All inputs are finite; a program needn't handle non-finite values. No bound on the sum of `leaf_mask` on one device may be relied on, other than what follows from the above.
Results may differ from the reference program's by a relative error of at most 0.04.
Values may be sent and summed in bfloat16 or wider, within the bound.
No kernel may reach another device: no remote copies, remote signals or barrier semaphores. Data moves between devices by JAX's collectives and lax.ppermute only.
A program may use at most 192 MiB of HBM per device.

```python
import math
import jax
import jax.numpy as jnp
import numpy as np
from jax import lax

D = 300
HEADS = 12
HEAD = 25
FF = 1200
LAYERS = 2
MOST = 100
STEP = 5
STARS_DEV = 80
LEAF_SLOTS = 4096
HOLDERS = 32
PARAMS_LAYER = 1171200
BLOCK = 36600
ROWS = 33408
N_GRAPH = 8


def holder_order(key):
    return jax.random.permutation(jax.random.fold_in(key, 101), HOLDERS).astype(jnp.int32)


def pieces(square_values, one_value, two_value, gain_value, shift_value):
    parts = [jnp.full((D * D,), v, jnp.float32) for v in square_values]
    parts = parts + [jnp.full((D * FF,), one_value, jnp.float32), jnp.full((FF * D,), two_value, jnp.float32)]
    parts = parts + [jnp.full((D,), gain_value, jnp.float32), jnp.full((D,), shift_value, jnp.float32)]
    parts = parts + [jnp.full((D,), gain_value, jnp.float32), jnp.full((D,), shift_value, jnp.float32)]
    return jnp.concatenate(parts)


def to_stored(flat_all, key):
    holder_idx = holder_order(key)
    blocks = flat_all.reshape(LAYERS, HOLDERS, BLOCK)
    return jnp.zeros_like(blocks).at[:, holder_idx].set(blocks).reshape(LAYERS, PARAMS_LAYER)


def base_noise(key, salt):
    subkey = jax.random.fold_in(key, salt)
    return jax.random.normal(subkey, (LAYERS, PARAMS_LAYER), jnp.float32)


def grad_size():
    return pieces([0.05, 0.1, 0.3, 0.4, 0.3], 0.3, 0.5, 1.0, 1.0) * math.sqrt(ROWS)


def draw_owner_list(key, part):
    return holder_order(key)


def draw_weights(key, part):
    inner = D ** (-0.5)
    spread_vec = pieces([inner, inner, inner, (D // 2) ** (-0.5), inner], inner, FF ** (-0.5), 0.1, 0.3)
    middle = pieces([0.0, 0.0, 0.0, 0.0, 0.0], 0.0, 0.0, 1.0, 0.0)
    return to_stored(middle[None, :] + spread_vec[None, :] * base_noise(key, 1), key)


def draw_first_moment(key, part):
    return to_stored(0.1 / 0.9 * grad_size()[None, :] * base_noise(key, 2), key)


def draw_second_moment(key, part):
    factor = jnp.exp(jax.random.uniform(jax.random.fold_in(key, 3), (LAYERS, PARAMS_LAYER), jnp.float32, math.log(0.5), math.log(8.0)))
    size_sq = grad_size() * grad_size()
    return to_stored(0.001 / 0.999 * size_sq[None, :] * factor, key)


def plant(values, rng, smallest, high):
    extent = values.shape
    index_at = [jax.random.randint(jax.random.fold_in(rng, axis), (), 0, extent[axis]) for axis in range(len(extent))]
    values = values.at[tuple(index_at)].set(smallest)
    longest = extent.index(max(extent))
    index_at[longest] = (index_at[longest] + 1) % extent[longest]
    return values.at[tuple(index_at)].set(high)


def shard_levels(rng, shape, split, least, largest):
    factor_of, own = 1.0, jax.random.fold_in(rng, 6)
    for position, blocks in split:
        draws = jnp.exp(jax.random.uniform(jax.random.fold_in(own, position), (blocks,), jnp.float32, least / len(split), largest / len(split)))
        factor_of = factor_of * jnp.repeat(draws, shape[position] // blocks).reshape([-1 if axis == position else 1 for axis in range(len(shape))])
    return factor_of


def length_profile(amount, total, limit, slope):
    loads = [(1 << 20) // math.isqrt(grade ** slope) + 1 for grade in range(2, amount + 1)]
    spare, holding = total - limit - (amount - 1), [1] * (amount - 1)
    while spare > 0:
        free = [i for i in range(amount - 1) if holding[i] < limit]
        pool, left = sum([loads[i] for i in free]), spare
        for i in free:
            more = min(limit - holding[i], max(1, left * loads[i] // pool), spare)
            holding[i] = holding[i] + more
            spare = spare - more
    return np.array([limit] + holding)


def uneven_parts(rng, count, total, reach, slope):
    if count == 2:
        one = jax.random.randint(rng, (), max(1, total - reach), min(reach, total - 1) + 1)
        return jnp.stack([one, total - one])
    lengths = jnp.asarray(length_profile(count, total, reach, slope), jnp.int32)
    couples = (count - 1) // 2
    source_of, receiver = lengths[1:1 + 2 * couples:2], lengths[2:2 + 2 * couples:2]
    slack = jnp.minimum(source_of - 1, reach - receiver)
    moved = jax.random.randint(jax.random.fold_in(rng, 1), (couples,), 0, 1 << 20) % (slack + 1)
    lengths = lengths.at[1:1 + 2 * couples:2].set(source_of - moved).at[2:2 + 2 * couples:2].set(receiver + moved)
    return lengths[jax.random.permutation(jax.random.fold_in(rng, 2), count)]


def noise(key, shape, scale, most, cuts=(), held_as=jnp.bfloat16):
    drawn = jax.random.normal(key, shape, jnp.float32) * scale
    if len(cuts) > 0:
        drawn = shard_levels(key, shape, cuts, -0.22, 0.18) * drawn
    return jnp.clip(drawn, min=-most, max=most).astype(held_as)


def setup_inputs(seed: int = 0) -> dict:
    key_list = jax.random.split(jax.random.key(seed), 14)
    return {
        "weights": draw_weights(jax.random.fold_in(key_list[13], 71), 0),
        "first_moment": draw_first_moment(jax.random.fold_in(key_list[13], 71), 0),
        "second_moment": draw_second_moment(jax.random.fold_in(key_list[13], 71), 0),
        "centers": noise(key_list[3], (N_GRAPH, STARS_DEV, D), 1.0, 6.0, ((0, 8),)),
        "leaves": noise(key_list[4], (N_GRAPH, LEAF_SLOTS, D), 1.0, 6.0, ((0, 8), (1, 4))),
        "edge_feats": noise(key_list[5], (N_GRAPH, LEAF_SLOTS, D), 1.0, 6.0, ((0, 8), (1, 4))),
        "center_cot": noise(key_list[6], (N_GRAPH, STARS_DEV, D), 1.0, 6.0, ((0, 8),)),
        "leaf_cot": noise(key_list[7], (N_GRAPH, LEAF_SLOTS, D), 1.0, 6.0, ((0, 8), (1, 4))),
        "edge_cot": noise(key_list[8], (N_GRAPH, LEAF_SLOTS, D), 1.0, 6.0, ((0, 8), (1, 4))),
        "graph_ids": jax.vmap(lambda own: jnp.searchsorted(jnp.cumsum(uneven_parts(own, STARS_DEV, LEAF_SLOTS, MOST, 2)), jnp.arange(LEAF_SLOTS), side="right"))(jax.random.split(key_list[9], N_GRAPH)).reshape((N_GRAPH, LEAF_SLOTS)).astype(jnp.int32),
        "star_sizes": plant(jax.random.randint(key_list[10], (N_GRAPH, STARS_DEV), 5, 101), jax.random.fold_in(key_list[10], 1), 5, 100).astype(jnp.int32),
        "leaf_mask": plant((jax.random.randint(key_list[11], (N_GRAPH, LEAF_SLOTS), 0, 8) < 7).astype(jnp.int32), jax.random.fold_in(key_list[11], 1), 0, 1),
        "owner_list": draw_owner_list(jax.random.fold_in(key_list[13], 71), 0),
    }


@jax.custom_vjp
def low(v):
    return lax.optimization_barrier(v.astype(jnp.bfloat16)).astype(jnp.float32)

@jax.custom_vjp
def low_back(v):
    return v

def low_keep(v):
    return (low(v), None)

def low_pass(kept, grad):
    return (grad,)

def back_keep(v):
    return (v, None)

def back_low(kept, grad):
    return (low(grad),)
low.defvjp(low_keep, low_pass)
low_back.defvjp(back_keep, back_low)
NEG = -1e+30
EPS_NORM = 1e-05
BETA_ONE = 0.9
BETA_TWO = 0.999
RATE = 0.05
DECAY = 0.01
EPS_ADAM = 1e-08

def product(left, right):
    return jnp.dot(left, right, precision=lax.Precision.HIGHEST, preferred_element_type=jnp.float32)

def split_params(flat_vec, model_width, hidden_width):
    square = model_width * model_width
    matrices = [flat_vec[i * square:(i + 1) * square].reshape(model_width, model_width) for i in range(5)]
    offset = 5 * square
    w_one = flat_vec[offset:offset + model_width * hidden_width].reshape(model_width, hidden_width)
    offset = offset + model_width * hidden_width
    w_two = flat_vec[offset:offset + hidden_width * model_width].reshape(hidden_width, model_width)
    offset = offset + hidden_width * model_width
    norm_rows = flat_vec[offset:offset + 4 * model_width].reshape(4, model_width)
    return matrices + [w_one, w_two, norm_rows]

def head_sum(values):
    return lax.optimization_barrier(jnp.sum(values.reshape(values.shape[0], HEADS, HEAD), axis=2))

def spread(values):
    return jnp.repeat(values, HEAD, axis=1)

def normalize(inputs, gain_row, shift_row):
    center_mean = lax.optimization_barrier(jnp.mean(inputs, axis=-1, keepdims=True))
    deviation = inputs - center_mean
    variance = lax.optimization_barrier(jnp.mean(deviation * deviation, axis=-1, keepdims=True))
    return deviation * lax.rsqrt(variance + EPS_NORM) * gain_row + shift_row

def ref_layer(params, center_in, leaf_in, edge_in, onehot, live_mask, star_scale, star_ids):
    w_query, w_key, w_value, w_out, w_edge, w_one, w_two, norm_rows = params
    star_count = center_in.shape[0]
    edge_low = low(edge_in)
    edge_next = low_back(product(edge_low, w_edge))
    message = low(leaf_in * edge_low)
    center_low = low(center_in)
    keys = low_back(product(message, w_key))
    values = low_back(product(message, w_value))
    query = low_back(product(center_low, w_query))
    self_key = low_back(product(center_low, w_key))
    self_value = low_back(product(center_low, w_value))
    leaf_message = low(jnp.take(center_in, star_ids, axis=0) * edge_low)
    leaf_out = low_back(product(leaf_message, w_value))
    scores = jnp.take(star_scale, star_ids)[:, None] * head_sum(jnp.take(query, star_ids, axis=0) * keys)
    self_scores = star_scale[:, None] * head_sum(query * self_key)
    member = onehot[:, :, None] * live_mask[:, None, None] > 0.5
    top_score = jnp.maximum(lax.optimization_barrier(jnp.max(jnp.where(member, scores[:, None, :], NEG), axis=0)), self_scores)
    shifted = jnp.where(live_mask[:, None] > 0.5, scores - jnp.take(top_score, star_ids, axis=0), NEG)
    weights_leaf = jnp.exp(shifted)
    self_weight = jnp.exp(self_scores - top_score)
    denominator = product(onehot.T, weights_leaf) + self_weight
    numerator = product(onehot.T, spread(weights_leaf) * values) + spread(self_weight) * self_value
    attended = numerator / spread(denominator)
    attn_center = low_back(product(low(attended), w_out))
    attn_leaf = low_back(product(low(leaf_out), w_out))
    joined = jnp.concatenate([center_in + attn_center, leaf_in + attn_leaf], axis=0)
    normed = normalize(joined, norm_rows[0], norm_rows[1])
    hidden_pre = low_back(product(low(normed), w_one))
    active = jax.nn.gelu(hidden_pre, approximate=False)
    branch = low_back(product(low(active), w_two))
    output = normalize(normed + branch, norm_rows[2], norm_rows[3])
    return (output[:star_count], output[star_count:], edge_next)

def forward_graph(flat_w, center_in, leaf_in, edge_in, star_ids, live_mask, star_scale):
    low_w = low(flat_w)
    onehot = (star_ids[:, None] == jnp.arange(center_in.shape[0], dtype=jnp.int32)[None, :]).astype(jnp.float32)
    carried = (center_in, leaf_in, edge_in)
    for i in range(LAYERS):
        carried = ref_layer(split_params(low_w[i], D, FF), carried[0], carried[1], carried[2], onehot, live_mask, star_scale, star_ids)
    return carried

def reference(weights, first_moment, second_moment, centers, leaves, edge_feats, center_cot, leaf_cot, edge_cot, graph_ids, star_sizes, leaf_mask, owner_list):
    holders = owner_list.shape[0]
    block_len = weights.shape[1] // holders

    def unstore(stored):
        return jnp.take(stored.reshape(LAYERS, holders, block_len), owner_list, axis=1).reshape(LAYERS, -1)

    def restore(flat_vec):
        blocks = flat_vec.reshape(LAYERS, holders, block_len)
        return jnp.zeros_like(blocks).at[:, owner_list].set(blocks).reshape(LAYERS, -1)
    flat_w = unstore(weights)
    scales = jnp.log(star_sizes.astype(jnp.float32)) / (math.log(32.0) * math.sqrt(HEAD))

    def one_graph(grad_sum, items):
        center_in, leaf_in, edge_in, cot_center, cot_leaf, cot_edge, star_ids, mask_row, scale_row = items
        live_mask = mask_row.astype(jnp.float32)

        def run(w_in, c_in, l_in, e_in):
            return forward_graph(w_in, c_in, l_in, e_in, star_ids, live_mask, scale_row)
        primal, pullback = jax.vjp(run, flat_w, center_in.astype(jnp.float32), leaf_in.astype(jnp.float32), edge_in.astype(jnp.float32))
        grad_w, grad_c, grad_l, grad_e = pullback((cot_center.astype(jnp.float32), cot_leaf.astype(jnp.float32), cot_edge.astype(jnp.float32)))
        return (grad_sum + grad_w, (primal[0].astype(jnp.bfloat16), primal[1].astype(jnp.bfloat16), primal[2].astype(jnp.bfloat16), grad_c, grad_l, grad_e))
    grad_total, outputs = lax.scan(one_graph, jnp.zeros_like(flat_w), (centers, leaves, edge_feats, center_cot, leaf_cot, edge_cot, graph_ids, leaf_mask, scales))
    first_new = BETA_ONE * unstore(first_moment) + (1.0 - BETA_ONE) * grad_total
    second_new = BETA_TWO * unstore(second_moment) + (1.0 - BETA_TWO) * grad_total * grad_total
    step_one = first_new / (1.0 - BETA_ONE ** STEP)
    step_two = second_new / (1.0 - BETA_TWO ** STEP)
    weights_new = flat_w - RATE * (step_one / (jnp.sqrt(step_two) + EPS_ADAM) + DECAY * flat_w)
    stored_new = restore(weights_new)
    return (outputs[0], outputs[1], outputs[2], outputs[3], outputs[4], outputs[5], restore(first_new), restore(second_new), stored_new, stored_new.astype(jnp.bfloat16), restore(grad_total))
```

```python
import math

import jax
import jax.numpy as jnp
from jax import lax
from jax.experimental import pallas as pl
from jax.experimental.pallas import tpu as pltpu
from jax.sharding import PartitionSpec as P

D = 300
HEADS = 12
HEAD = 25
FF = 1200
LAYERS = 2
STEP = 5
ROWS_LAYER = 5 * D + 2 * FF + 4

NEG = -1e30
EPS_NORM = 1e-05
BETA_ONE = 0.9
BETA_TWO = 0.999
RATE = 0.05
DECAY = 0.01
EPS_ADAM = 1e-08
INV_ROOT_TWO = 0.7071067811865476
INV_ROOT_TWO_PI = 0.3989422804014327

HALO = 128
TILE = 256
HP = 16
PACK = 320
CHUNKS = tuple((i, min(i + 256, FF)) for i in range(0, FF, 256))
VMEM = 56 << 20
F32 = jnp.float32
BF = jnp.bfloat16

WEIGHTS = ("wq", "wk", "wv", "wo", "we", "w1", "w2", "norm")
WEIGHT_SHAPES = tuple([((D, D), BF)] * 5 + [((D, FF), BF), ((FF, D), BF), ((8, D), F32)])


def nn(a, b):
    return lax.dot_general(a, b, (((1,), (0,)), ((), ())), preferred_element_type=F32)


def nt(a, b):
    return lax.dot_general(a, b, (((1,), (1,)), ((), ())), preferred_element_type=F32)


def tn(a, b):
    return lax.dot_general(a, b, (((0,), (0,)), ((), ())), preferred_element_type=F32)


def halves(x):
    high = x.astype(BF)
    return high, (x - high.astype(F32)).astype(BF)


def thirds(x):
    high = x.astype(BF)
    rest = x - high.astype(F32)
    mid = rest.astype(BF)
    return high, mid, (rest - mid.astype(F32)).astype(BF)


def stacked(parts, axis=0):
    return jnp.concatenate([p.astype(F32) for p in parts], axis=axis).astype(BF)


def table(rows, repeat=1):
    head = lax.broadcasted_iota(jnp.int32, (repeat * rows, D), 0) % rows
    feature = lax.broadcasted_iota(jnp.int32, (repeat * rows, D), 1)
    low = head * HEAD
    return jnp.where((feature >= low) & (feature < low + HEAD), 1.0, 0.0).astype(BF)


def head_sum(values):
    high, low = halves(values)
    tab = table(HP)
    return nt(high, tab) + nt(low, tab)


def head_sum_t(values):
    high, low = halves(values)
    tab = table(HP)
    return nt(tab, high) + nt(tab, low)


def spread(values):
    high, low = halves(values)
    tab = table(HP)
    return nn(high, tab) + nn(low, tab)


def spread_t(values):
    return tn(stacked(halves(values)), table(HP, 2))


def onehot_col(ids, stars, repeat):
    lane = lax.broadcasted_iota(jnp.int32, (ids.shape[0], repeat * stars), 1)
    hit = lane == ids
    for i in range(1, repeat):
        hit = hit | (lane == ids + i * stars) & (ids >= 0)
    return jnp.where(hit, 1.0, 0.0).astype(BF)


def onehot_row(ids, stars, repeat):
    sub = lax.broadcasted_iota(jnp.int32, (repeat * stars, ids.shape[1]), 0)
    hit = sub == ids
    for i in range(1, repeat):
        hit = hit | (sub == ids + i * stars) & (ids >= 0)
    return jnp.where(hit, 1.0, 0.0).astype(BF)


def row_mean(x):
    return jnp.sum(x, axis=-1, keepdims=True) * (1.0 / D)


def normalized(x):
    dev = x - row_mean(x)
    inverse = lax.rsqrt(row_mean(dev * dev) + EPS_NORM)
    return dev * inverse, inverse


def norm_back(grad, scaled, inverse):
    return inverse * (grad - row_mean(grad) - scaled * row_mean(grad * scaled))


def ffn_forward(r, z, rows):
    norm = r["norm"]
    g1, b1, g2, b2 = (norm[i : i + 1, :] for i in range(4))
    xh1, inv1 = normalized(z)
    h = xh1 * g1 + b1
    hb = h.astype(BF)
    r["hb"][rows, :] = hb
    r["xh1"][rows, :] = xh1.astype(BF)
    r["inv1"][rows, :] = inv1
    total = h
    for lo, hi in CHUNKS:
        pre = nn(hb, r["w1"][:, lo:hi])
        cdf = 0.5 * (1.0 + lax.erf(pre * INV_ROOT_TWO))
        act = (pre * cdf).astype(BF)
        r["act"][rows, lo:hi] = act
        r["slope"][rows, lo:hi] = (
            cdf + pre * jnp.exp(-0.5 * pre * pre) * INV_ROOT_TWO_PI
        ).astype(BF)
        total = total + nn(act, r["w2"][lo:hi, :])
    xh2, inv2 = normalized(total)
    r["xh2"][rows, :] = xh2.astype(BF)
    r["inv2"][rows, :] = inv2
    return xh2 * g2 + b2


def fold(x):
    return jnp.sum(x.reshape(x.shape[0] // 8, 8, x.shape[1]), axis=0)


def ffn_backward(r, gy, rows, weight):
    norm = r["norm"]
    g1, g2 = norm[0:1, :], norm[2:3, :]
    xh2 = r["xh2"][rows, :].astype(F32)
    gw = gy * weight
    r["dn"][2] += fold(gw * xh2)
    r["dn"][3] += fold(gw)
    mid = norm_back(gy * g2, xh2, r["inv2"][rows, :])
    branch = mid.astype(BF)
    r["dbr"][rows, :] = (mid * weight).astype(BF)
    total = mid
    for lo, hi in CHUNKS:
        dact = nt(branch, r["w2"][lo:hi, :])
        dpre = dact * r["slope"][rows, lo:hi].astype(F32)
        low = dpre.astype(BF)
        r["dpre"][rows, lo:hi] = (dpre * weight).astype(BF)
        total = total + nt(low, r["w1"][:, lo:hi])
    xh1 = r["xh1"][rows, :].astype(F32)
    gw = total * weight
    r["dn"][0] += fold(gw * xh1)
    r["dn"][1] += fold(gw)
    return norm_back(total * g1, xh1, r["inv1"][rows, :])


def forward(r, stars, leaf_rows):
    centers = pl.ds(leaf_rows, stars)
    xc = r["xc"][...].astype(F32)
    low = xc.astype(BF)
    qs = nn(low, r["wq"][...]) * r["scale"][...]
    kc = nn(low, r["wk"][...])
    vc = nn(low, r["wv"][...])
    own_score = head_sum(qs * kc)
    r["qs"][...] = qs
    r["kc"][...] = kc
    r["vc"][...] = vc
    r["self"][...] = own_score
    r["qcat"][...] = stacked(halves(qs))
    r["xcat"][...] = stacked(halves(xc))

    def tile(t, carry):
        start = pl.multiple_of(t * TILE, TILE)
        rows = pl.ds(start, TILE)
        el = r["el"][rows, :]
        ew = el.astype(F32)
        xl = r["xl"][rows, :].astype(F32)
        r["en"][rows, :] = nn(el, r["we"][...]).astype(BF)
        hot = onehot_col(r["idc"][rows, :], stars, 2)
        m = (xl * ew).astype(BF)
        k = nn(m, r["wk"][...])
        r["k"][rows, :] = k.astype(BF)
        r["v"][rows, :] = nn(m, r["wv"][...]).astype(BF)
        r["s"][:, rows] = head_sum_t(nn(hot, r["qcat"][...]) * k)
        mc = (nn(hot, r["xcat"][...]) * ew).astype(BF)
        ub = nn(mc, r["wv"][...]).astype(BF)
        r["ub"][rows, :] = ub
        r["yl"][rows, :] = ffn_forward(r, xl + nn(ub, r["wo"][...]), rows)
        return carry

    lax.fori_loop(0, leaf_rows // TILE, tile, 0)

    ids = r["idr"][...]
    live = r["live"][...] > 0.5
    score = r["s"][...]
    top = jnp.where(live, score, NEG)
    lane = lax.broadcasted_iota(jnp.int32, (1, leaf_rows), 1)
    shift = 1
    while shift < 128:
        same = (pltpu.roll(ids, shift, 1) == ids) & (lane >= shift)
        top = jnp.maximum(top, jnp.where(same, pltpu.roll(top, shift, 1), NEG))
        shift *= 2
    hot_row = onehot_row(ids, stars, 1)
    last = hot_row.astype(F32) * r["last"][...]
    present = jnp.sum(last, axis=1, keepdims=True) > 0.5
    last = last.astype(BF)
    star_top = sum(nt(last, part) for part in thirds(top))
    peak = jnp.where(present, jnp.maximum(star_top, own_score), own_score)
    peak_row = tn(stacked(thirds(peak)), onehot_row(ids, stars, 3))
    e = jnp.where(live, jnp.exp(jnp.where(live, score - peak_row, 0.0)), 0.0)
    self_weight = jnp.exp(own_score - peak)
    total = self_weight + sum(nt(hot_row, part) for part in halves(e))
    r["logt"][...] = peak + jnp.log(total)
    weighted = (spread_t(e) * r["v"][...].astype(F32)).astype(BF)
    o = (nn(hot_row, weighted) + spread(self_weight) * vc) / spread(total)
    r["o"][...] = o
    z = xc + nn(o.astype(BF), r["wo"][...])
    r["yc"][...] = ffn_forward(r, z, centers)


def backward(r, stars, leaf_rows, own_rows):
    centers = pl.ds(leaf_rows, stars)
    own = r["cown"][...]
    r["dn"][...] = jnp.zeros_like(r["dn"])
    r["dq"][...] = jnp.zeros_like(r["dq"])
    r["dx"][...] = jnp.zeros_like(r["dx"])
    dz_c = ffn_backward(r, r["gyc"][...].astype(F32), centers, own)
    dac = dz_c.astype(BF)
    do = nt(dac, r["wo"][...])
    r["docat"][...] = stacked(halves(do))
    o = r["o"][...]
    vc = r["vc"][...]
    kc = r["kc"][...]
    qs = r["qs"][...]
    xc = r["xc"][...].astype(F32)
    r["qcat"][...] = stacked(halves(qs))
    r["xcat"][...] = stacked(halves(xc))
    delta = head_sum(do * o)
    self_p = jnp.exp(r["self"][...] - r["logt"][...])
    d_self = self_p * (head_sum(do * vc) - delta)
    coef_c = spread(d_self)
    dvc = spread(self_p) * do
    dkc = coef_c * qs
    logt_parts = stacked(thirds(r["logt"][...]))
    delta_parts = stacked(thirds(delta))

    def tile(t, carry):
        start = pl.multiple_of(t * TILE, TILE)
        rows = pl.ds(start, TILE)
        row = lax.broadcasted_iota(jnp.int32, (TILE, 1), 0) + start
        mine = jnp.where((row >= HALO) & (row < HALO + own_rows), 1.0, 0.0)
        dz = ffn_backward(r, r["gyl"][rows, :].astype(F32), rows, mine)
        dal = dz.astype(BF)
        r["dal"][rows, :] = dal
        du = nt(dal, r["wo"][...]).astype(BF)
        r["du"][rows, :] = du
        dmc = nt(du, r["wv"][...])
        el = r["el"][rows, :].astype(F32)
        xl = r["xl"][rows, :].astype(F32)
        hot = onehot_col(r["idc"][rows, :], stars, 2)
        ids_row = r["idr"][:, rows]
        hot_row = onehot_row(ids_row, stars, 1)
        hot3 = onehot_row(ids_row, stars, 3)
        xr = nn(hot, r["xcat"][...])
        r["mc"][rows, :] = (xr * el).astype(BF)
        r["dx"][...] += nn(hot_row, (dmc * el).astype(BF))
        de = dmc * xr
        live = r["live"][:, rows] > 0.5
        score = r["s"][:, rows] - tn(logt_parts, hot3)
        p = jnp.where(live, jnp.exp(jnp.where(live, score, 0.0)), 0.0)
        dor = nn(hot, r["docat"][...])
        v = r["v"][rows, :].astype(F32)
        ds = p * (head_sum_t(dor * v) - tn(delta_parts, hot3))
        dv = (spread_t(p) * dor).astype(BF)
        r["dv"][rows, :] = dv
        coef = spread_t(ds)
        r["dq"][...] += nn(hot_row, (coef * r["k"][rows, :].astype(F32)).astype(BF))
        dk = (coef * nn(hot, r["qcat"][...])).astype(BF)
        r["dk"][rows, :] = dk
        r["m"][rows, :] = (xl * el).astype(BF)
        dm = nt(dk, r["wk"][...]) + nt(dv, r["wv"][...])
        r["gxl"][rows, :] = dz + dm * el
        de = de + dm * xl + nt(r["ge"][rows, :], r["we"][...])
        r["gel"][rows, :] = de.astype(r["gel"].dtype)
        return carry

    lax.fori_loop(0, leaf_rows // TILE, tile, 0)

    dq = (r["dq"][...] + coef_c * kc) * r["scale"][...]
    dq_low = dq.astype(BF)
    dkc_low = dkc.astype(BF)
    dvc_low = dvc.astype(BF)
    r["gxc"][...] = (
        dz_c
        + nt(dq_low, r["wq"][...])
        + nt(dkc_low, r["wk"][...])
        + nt(dvc_low, r["wv"][...])
        + r["dx"][...]
    )

    own_leaf = slice(HALO, HALO + own_rows)
    nat = r["nat"]
    xb = xc.astype(BF)
    nat_store(nat, pl.ds(0, D), tn(xb, (dq * own).astype(BF)))
    m = r["m"][own_leaf, :]
    nat_store(
        nat, pl.ds(D, D), tn(m, r["dk"][own_leaf, :]) + tn(xb, (dkc * own).astype(BF))
    )
    nat_store(
        nat,
        pl.ds(2 * D, D),
        tn(m, r["dv"][own_leaf, :])
        + tn(r["mc"][own_leaf, :], r["du"][own_leaf, :])
        + tn(xb, (dvc * own).astype(BF)),
    )
    nat_store(
        nat,
        pl.ds(3 * D, D),
        tn(r["ub"][own_leaf, :], r["dal"][own_leaf, :]) + tn(o.astype(BF), (dz_c * own).astype(BF)),
    )
    nat_store(nat, pl.ds(4 * D, D), tn(r["el"][own_leaf, :], r["ge"][own_leaf, :]))
    base = 5 * D
    for j in range(FF // D):
        columns = slice(j * D, (j + 1) * D)
        part = tn(r["hb"][own_leaf, :], r["dpre"][own_leaf, columns]) + tn(
            r["hb"][leaf_rows:, :], r["dpre"][leaf_rows:, columns]
        )
        nat_store(nat, pl.ds(base + j, D, stride=FF // D), part)
    base = base + FF
    for lo, hi in CHUNKS:
        part = tn(r["act"][own_leaf, lo:hi], r["dbr"][own_leaf, :]) + tn(
            r["act"][leaf_rows:, lo:hi], r["dbr"][leaf_rows:, :]
        )
        nat_store(nat, pl.ds(base + lo, hi - lo), part)
    base = base + FF
    sums = [jnp.sum(r["dn"][i], axis=0, keepdims=True) for i in range(4)]
    nat_store(nat, pl.ds(base, 4), jnp.concatenate(sums, axis=0))


def nat_load(nat, at):
    return jnp.concatenate([nat[c, at, :] for c in range(3)], axis=1)[:, :D]


def nat_store(nat, at, value):
    nat[0, at, :] = value[:, 0:128]
    nat[1, at, :] = value[:, 128:256]
    rest = jnp.zeros((value.shape[0], 384 - D), F32)
    nat[2, at, :] = jnp.concatenate([value[:, 256:D], rest], axis=1)


def pack_blocks(r, holders, rows):
    nat = r["nat"]
    lane = lax.broadcasted_iota(jnp.int32, (64, 128), 1)
    for b in range(holders):
        at = r["slot"][b]
        top = b * rows
        r["out"][at, 0:128, :] = nat[0, top : top + 128, :].astype(BF)
        r["out"][at, 128:256, :] = nat[1, top : top + 128, :].astype(BF)
        high = pltpu.roll(nat[2, top + 64 : top + 128, :], 64, 1)
        tail = jnp.where(lane < 64, nat[2, top : top + 64, :], high)
        r["out"][at, 256:320, :] = tail.astype(BF)


def unpack_blocks(r, holders, rows):
    nat = r["nat"]
    for b in range(holders):
        at = r["slot"][b]
        top = b * rows
        nat[0, top : top + rows, :] = r["got"][at, 0:128, :].astype(F32)[:rows]
        nat[1, top : top + rows, :] = r["got"][at, 128:256, :].astype(F32)[:rows]
        tail = r["got"][at, 256:320, :].astype(F32)
        nat[2, top : top + 64, :] = tail
        nat[2, top + 64 : top + rows, :] = pltpu.roll(tail, 64, 1)[: rows - 64]
    for i, name in enumerate(WEIGHTS[:5]):
        r[name][...] = nat_load(nat, pl.ds(i * D, D)).astype(BF)
    base = 5 * D
    for j in range(FF // D):
        part = nat_load(nat, pl.ds(base + j, D, stride=FF // D))
        r["w1"][:, j * D : (j + 1) * D] = part.astype(BF)
    base = base + FF
    r["w2"][...] = nat_load(nat, pl.ds(base, FF)).astype(BF)
    base = base + FF
    r["norm"][...] = nat_load(nat, pl.ds(base, 8))


def call(body, inputs, outputs, scratch, in_smem=(), name=None):
    names = list(inputs) + list(outputs) + list(scratch)

    def kernel(*refs):
        body(dict(zip(names, refs, strict=True)))

    vmem = pl.BlockSpec(memory_space=pltpu.VMEM)
    smem = pl.BlockSpec(memory_space=pltpu.SMEM)
    results = pl.pallas_call(
        kernel,
        out_shape=[jax.ShapeDtypeStruct(s, d) for s, d in outputs.values()],
        in_specs=[smem if k in in_smem else vmem for k in inputs],
        out_specs=[vmem] * len(outputs),
        scratch_shapes=[pltpu.VMEM(s, d) for s, d in scratch.values()],
        compiler_params=pltpu.CompilerParams(vmem_limit_bytes=VMEM),
        name=name,
    )(*inputs.values())
    return dict(zip(outputs, results, strict=True))


def saved_shapes(stars, leaf_rows):
    rows = leaf_rows + stars
    return {
        "k": ((leaf_rows, D), BF),
        "v": ((leaf_rows, D), BF),
        "ub": ((leaf_rows, D), BF),
        "hb": ((rows, D), BF),
        "xh1": ((rows, D), BF),
        "xh2": ((rows, D), BF),
        "act": ((rows, FF), BF),
        "slope": ((rows, FF), BF),
        "inv1": ((rows, 1), F32),
        "inv2": ((rows, 1), F32),
        "s": ((HP, leaf_rows), F32),
        "qs": ((stars, D), F32),
        "kc": ((stars, D), F32),
        "vc": ((stars, D), F32),
        "o": ((stars, D), F32),
        "self": ((stars, HP), F32),
        "logt": ((stars, HP), F32),
    }


def forward_scratch(stars):
    return {"qcat": ((2 * stars, D), BF), "xcat": ((2 * stars, D), BF)}


def backward_scratch(stars, leaf_rows):
    rows = leaf_rows + stars
    return {
        "docat": ((2 * stars, D), BF),
        "dn": ((4, 8, D), F32),
        "dq": ((stars, D), F32),
        "dx": ((stars, D), F32),
        "dbr": ((rows, D), BF),
        "dpre": ((rows, FF), BF),
        "dal": ((leaf_rows, D), BF),
        "du": ((leaf_rows, D), BF),
        "mc": ((leaf_rows, D), BF),
        "dv": ((leaf_rows, D), BF),
        "dk": ((leaf_rows, D), BF),
        "m": ((leaf_rows, D), BF),
    }


def tree_stages(graph_size, leaf_size):
    stages = [("leaf", 0, 1)]
    for axis, size, first in (("leaf", leaf_size, 1), ("graph", graph_size, 0)):
        bit = first
        while (1 << bit) < size:
            bits = 1 if axis == "graph" and bit == 0 else min(2, size.bit_length() - 1 - bit)
            stages.append((axis, bit, bits))
            bit += bits
    return stages


def exchange(x, stage, value, sizes):
    axis, shift, bits = stage
    return lax.ppermute(x, axis, [(i, i ^ (value << shift)) for i in range(sizes[axis])])


def gather_tree(x, stages, sizes):
    held = x[None]
    for stage in stages[::-1]:
        held = jnp.concatenate(
            [held] + [exchange(held, stage, v, sizes) for v in range(1, 1 << stage[2])], axis=0
        )
    return held


def reduce_tree(x, stages, sizes):
    held = x
    for n, stage in enumerate(stages):
        count = held.shape[0] >> stage[2]
        total = held[:count].astype(F32)
        for v in range(1, 1 << stage[2]):
            total = total + exchange(held[v * count : (v + 1) * count], stage, v, sizes).astype(F32)
        held = total if n == len(stages) - 1 else total.astype(BF)
    return held[0]


def tree_slot(relative, stages, leaf_bits):
    slot = jnp.zeros_like(relative)
    for axis, shift, bits in stages:
        shift = shift + (leaf_bits if axis == "graph" else 0)
        slot = (slot << bits) | ((relative >> shift) & ((1 << bits) - 1))
    return slot


def to_rows(flat, rows):
    block = jnp.pad(flat.reshape(rows, D), ((0, 128 - rows), (0, 0)))
    tail = jnp.pad(block[:, 256:], ((0, 0), (0, 320 - D)))
    return jnp.concatenate(
        [block[:, :128], block[:, 128:256], jnp.concatenate([tail[:64], tail[64:]], axis=1)], axis=0
    )


def from_rows(packed, rows):
    tail = jnp.concatenate([packed[256:, : D - 256], packed[256:, 64 : D - 192]], axis=0)
    block = jnp.concatenate([packed[:128], packed[128:256], tail], axis=1)
    return block[:rows].reshape(-1)


def split_flat(vec):
    square = D * D
    mats = [vec[i * square : (i + 1) * square].reshape(D, D) for i in range(5)]
    at = 5 * square
    w1 = vec[at : at + D * FF].reshape(D, FF)
    at = at + D * FF
    w2 = vec[at : at + FF * D].reshape(FF, D)
    at = at + FF * D
    norm = jnp.pad(vec[at : at + 4 * D].reshape(4, D).astype(F32), ((0, 4), (0, 0)))
    return dict(zip(WEIGHTS, mats + [w1, w2, norm], strict=True))


def with_halo(x):
    size = lax.axis_size("leaf")
    left = lax.ppermute(x[:, -HALO:], "leaf", [(i, i + 1) for i in range(size - 1)])
    right = lax.ppermute(x[:, :HALO], "leaf", [(i + 1, i) for i in range(size - 1)])
    return jnp.concatenate([left, x, right], axis=1)


def local(
    weights,
    first_moment,
    second_moment,
    centers,
    leaves,
    edge_feats,
    center_cot,
    leaf_cot,
    edge_cot,
    graph_ids,
    star_sizes,
    leaf_mask,
    owner_list,
):
    sizes = {"graph": lax.axis_size("graph"), "leaf": lax.axis_size("leaf")}
    holders = sizes["graph"] * sizes["leaf"]
    block_len = weights.shape[1]
    block_rows = block_len // D
    in_rows = block_len % D == 0 and 64 < block_rows <= 128
    stars = centers.shape[1]
    own_rows = leaves.shape[1]
    leaf_rows = own_rows + 2 * HALO

    stages = tree_stages(sizes["graph"], sizes["leaf"])
    me = lax.axis_index(("graph", "leaf"))
    slot = tree_slot(owner_list ^ me, stages, sizes["leaf"].bit_length() - 1)
    nat_rows = ROWS_LAYER + 12
    weights_low = weights.astype(BF)
    params = []
    for i in range(LAYERS):
        if in_rows:
            got = gather_tree(to_rows(weights_low[i], block_rows), stages, sizes)
            params.append(
                call(
                    lambda r: unpack_blocks(r, holders, block_rows),
                    {"slot": slot, "got": got},
                    dict(zip(WEIGHTS, WEIGHT_SHAPES, strict=True)),
                    {"nat": ((3, nat_rows, 128), F32)},
                    in_smem=("slot",),
                    name="unpack",
                )
            )
        else:
            got = gather_tree(weights_low[i], stages, sizes)
            params.append(split_flat(jnp.take(got, slot, axis=0).reshape(-1)))

    ext = with_halo(jnp.concatenate([leaves, edge_feats, leaf_cot, edge_cot], axis=0))
    code = with_halo(graph_ids * 2 + leaf_mask + 1) - 1
    ids = jnp.where(code < 0, -1, code >> 1)
    live = jnp.where(code < 0, 0, code & 1).astype(F32)
    edge_id = jnp.full((1, 1), -1, jnp.int32)
    last = (ids != jnp.concatenate([ids[:, 1:], edge_id], axis=1)).astype(F32)
    first = graph_ids[0] != ids[0, HALO - 1 : HALO - 1 + own_rows]
    star_index = jnp.arange(stars, dtype=jnp.int32)
    star_own = jnp.any((star_index[:, None] == graph_ids) & first[None, :], axis=1)[:, None]
    scale = (jnp.log(star_sizes[0].astype(F32)) / (math.log(32.0) * math.sqrt(HEAD)))[:, None]
    base = {
        "idc": ids.reshape(-1, 1),
        "idr": ids,
        "live": live,
        "last": last,
        "scale": scale,
        "cown": star_own.astype(F32),
    }
    saved = saved_shapes(stars, leaf_rows)
    f_scratch = forward_scratch(stars)
    b_scratch = backward_scratch(stars, leaf_rows)
    nat = {"nat": ((3, nat_rows, 128), F32)}
    blocks = {"out": ((holders, PACK, 128), BF)}
    grads_out = blocks if in_rows else nat
    grads_scratch = nat if in_rows else {}

    one = call(
        lambda r: forward(r, stars, leaf_rows),
        {**base, **params[0], "xc": centers[0], "xl": ext[0], "el": ext[1]},
        {
            "yc": ((stars, D), F32),
            "yl": ((leaf_rows, D), F32),
            "en": ((leaf_rows, D), BF),
            **saved,
        },
        f_scratch,
        name="forward",
    )

    def both(r):
        forward(r, stars, leaf_rows)
        backward(r, stars, leaf_rows, own_rows)
        if in_rows:
            pack_blocks(r, holders, block_rows)

    two = call(
        both,
        {
            **base,
            "slot": slot,
            **params[1],
            "xc": one["yc"],
            "xl": one["yl"],
            "el": one["en"],
            "gyc": center_cot[0],
            "gyl": ext[2],
            "ge": ext[3],
        },
        {
            "yc": ((stars, D), F32),
            "yl": ((leaf_rows, D), F32),
            "en": ((leaf_rows, D), BF),
            "gxc": ((stars, D), F32),
            "gxl": ((leaf_rows, D), F32),
            "gel": ((leaf_rows, D), BF),
            **grads_out,
        },
        {**f_scratch, **saved, **b_scratch, **grads_scratch},
        in_smem=("slot",),
        name="last",
    )

    def back(r):
        backward(r, stars, leaf_rows, own_rows)
        if in_rows:
            pack_blocks(r, holders, block_rows)

    three = call(
        back,
        {
            **base,
            "slot": slot,
            **params[0],
            "xc": centers[0],
            "xl": ext[0],
            "el": ext[1],
            "gyc": two["gxc"],
            "gyl": two["gxl"],
            "ge": two["gel"],
            **{k: one[k] for k in saved},
        },
        {
            "gxc": ((stars, D), F32),
            "gxl": ((leaf_rows, D), F32),
            "gel": ((leaf_rows, D), F32),
            **grads_out,
        },
        {**f_scratch, **b_scratch, **grads_scratch},
        in_smem=("slot",),
        name="first",
    )

    totals = []
    for grads in (three, two):
        if in_rows:
            totals.append(from_rows(reduce_tree(grads["out"], stages, sizes), block_rows))
        else:
            flat = jnp.swapaxes(grads["nat"][:, :ROWS_LAYER], 0, 1).reshape(ROWS_LAYER, 384)
            flat = flat[:, :D].reshape(holders, block_len)
            placed = jnp.zeros_like(flat).at[slot].set(flat).astype(BF)
            totals.append(reduce_tree(placed, stages, sizes))
    grad_total = jnp.stack(totals)

    own_leaf = slice(HALO, HALO + own_rows)
    centers_out = lax.psum(jnp.where(star_own, two["yc"], 0.0).astype(BF), "leaf")
    grad_centers = lax.psum(jnp.where(star_own, three["gxc"], 0.0), "leaf")
    first_new = BETA_ONE * first_moment + (1.0 - BETA_ONE) * grad_total
    second_new = BETA_TWO * second_moment + (1.0 - BETA_TWO) * grad_total * grad_total
    step_one = first_new / (1.0 - BETA_ONE**STEP)
    step_two = second_new / (1.0 - BETA_TWO**STEP)
    weights_new = weights - RATE * (step_one / (jnp.sqrt(step_two) + EPS_ADAM) + DECAY * weights)
    return (
        centers_out[None],
        two["yl"][own_leaf].astype(BF)[None],
        two["en"][own_leaf][None],
        grad_centers[None],
        three["gxl"][own_leaf][None],
        three["gel"][own_leaf][None],
        first_new,
        second_new,
        weights_new,
        weights_new.astype(BF),
        grad_total,
    )


def solution(mesh):
    both = ("graph", "leaf")
    return jax.shard_map(
        local,
        mesh=mesh,
        in_specs=(
            P(None, both),
            P(None, both),
            P(None, both),
            P("graph", None, None),
            P("graph", "leaf", None),
            P("graph", "leaf", None),
            P("graph", None, None),
            P("graph", "leaf", None),
            P("graph", "leaf", None),
            P("graph", "leaf"),
            P("graph", None),
            P("graph", "leaf"),
            P(),
        ),
        out_specs=(
            P("graph", None, None),
            P("graph", "leaf", None),
            P("graph", "leaf", None),
            P("graph", None, None),
            P("graph", "leaf", None),
            P("graph", "leaf", None),
            P(None, both),
            P(None, both),
            P(None, both),
            P(None, both),
            P(None, both),
        ),
        check_vma=False,
    )
```

```python
import math

import jax
import jax.numpy as jnp
from jax import lax
from jax.experimental import pallas as pl
from jax.experimental.pallas import tpu as pltpu
from jax.sharding import PartitionSpec as P

D = 300
HEADS = 12
HEAD = 25
FF = 1200
LAYERS = 2
STEP = 5
ROWS_LAYER = 5 * D + 2 * FF + 4

NEG = -1e30
EPS_NORM = 1e-05
BETA_ONE = 0.9
BETA_TWO = 0.999
RATE = 0.05
DECAY = 0.01
EPS_ADAM = 1e-08
INV_ROOT_TWO = 0.7071067811865476
INV_ROOT_TWO_PI = 0.3989422804014327

HALO = 128
TILE = 256
HP = 16
PACK = 320
CHUNKS = tuple((i, min(i + 256, FF)) for i in range(0, FF, 256))
VMEM = 56 << 20
F32 = jnp.float32
BF = jnp.bfloat16

WEIGHTS = ("wq", "wk", "wv", "wo", "we", "w1", "w2", "norm")
WEIGHT_SHAPES = tuple([((D, D), BF)] * 5 + [((D, FF), BF), ((FF, D), BF), ((8, D), F32)])


def nn(a, b):
    return lax.dot_general(a, b, (((1,), (0,)), ((), ())), preferred_element_type=F32)


def nt(a, b):
    return lax.dot_general(a, b, (((1,), (1,)), ((), ())), preferred_element_type=F32)


def tn(a, b):
    return lax.dot_general(a, b, (((0,), (0,)), ((), ())), preferred_element_type=F32)


def halves(x):
    high = x.astype(BF)
    return high, (x - high.astype(F32)).astype(BF)


def thirds(x):
    high = x.astype(BF)
    rest = x - high.astype(F32)
    mid = rest.astype(BF)
    return high, mid, (rest - mid.astype(F32)).astype(BF)


def stacked(parts, axis=0):
    return jnp.concatenate([p.astype(F32) for p in parts], axis=axis).astype(BF)


def table(rows, repeat=1):
    head = lax.broadcasted_iota(jnp.int32, (repeat * rows, D), 0) % rows
    feature = lax.broadcasted_iota(jnp.int32, (repeat * rows, D), 1)
    low = head * HEAD
    return jnp.where((feature >= low) & (feature < low + HEAD), 1.0, 0.0).astype(BF)


def head_sum(values):
    high, low = halves(values)
    tab = table(HP)
    return nt(high, tab) + nt(low, tab)


def head_sum_t(values):
    high, low = halves(values)
    tab = table(HP)
    return nt(tab, high) + nt(tab, low)


def spread(values):
    high, low = halves(values)
    tab = table(HP)
    return nn(high, tab) + nn(low, tab)


def spread_t(values):
    return tn(stacked(halves(values)), table(HP, 2))


def onehot_col(ids, stars, repeat):
    lane = lax.broadcasted_iota(jnp.int32, (ids.shape[0], repeat * stars), 1)
    hit = lane == ids
    for i in range(1, repeat):
        hit = hit | (lane == ids + i * stars) & (ids >= 0)
    return jnp.where(hit, 1.0, 0.0).astype(BF)


def onehot_row(ids, stars, repeat):
    sub = lax.broadcasted_iota(jnp.int32, (repeat * stars, ids.shape[1]), 0)
    hit = sub == ids
    for i in range(1, repeat):
        hit = hit | (sub == ids + i * stars) & (ids >= 0)
    return jnp.where(hit, 1.0, 0.0).astype(BF)


def row_mean(x):
    return jnp.sum(x, axis=-1, keepdims=True) * (1.0 / D)


def normalized(x):
    dev = x - row_mean(x)
    inverse = lax.rsqrt(row_mean(dev * dev) + EPS_NORM)
    return dev * inverse, inverse


def norm_back(grad, scaled, inverse):
    return inverse * (grad - row_mean(grad) - scaled * row_mean(grad * scaled))


def ffn_forward(r, z, rows):
    norm = r["norm"]
    g1, b1, g2, b2 = (norm[i : i + 1, :] for i in range(4))
    xh1, inv1 = normalized(z)
    h = xh1 * g1 + b1
    hb = h.astype(BF)
    r["hb"][rows, :] = hb
    r["xh1"][rows, :] = xh1.astype(BF)
    r["inv"][rows, 0:1] = inv1
    total = h
    for lo, hi in CHUNKS:
        pre = nn(hb, r["w1"][:, lo:hi])
        cdf = 0.5 * (1.0 + lax.erf(pre * INV_ROOT_TWO))
        act = (pre * cdf).astype(BF)
        r["act"][rows, lo:hi] = act
        r["slope"][rows, lo:hi] = (
            cdf + pre * jnp.exp(-0.5 * pre * pre) * INV_ROOT_TWO_PI
        ).astype(BF)
        total = total + nn(act, r["w2"][lo:hi, :])
    xh2, inv2 = normalized(total)
    r["xh2"][rows, :] = xh2.astype(BF)
    r["inv"][rows, 1:2] = inv2
    return xh2 * g2 + b2


def fold(x):
    return jnp.sum(x.reshape(x.shape[0] // 8, 8, x.shape[1]), axis=0)


def ffn_backward(r, gy, rows, weight):
    norm = r["norm"]
    g1, g2 = norm[0:1, :], norm[2:3, :]
    xh2 = r["xh2"][rows, :].astype(F32)
    gw = gy * weight
    r["dn"][2] += fold(gw * xh2)
    r["dn"][3] += fold(gw)
    mid = norm_back(gy * g2, xh2, r["inv"][rows, 1:2])
    branch = mid.astype(BF)
    r["dbr"][rows, :] = (mid * weight).astype(BF)
    total = mid
    for lo, hi in CHUNKS:
        dact = nt(branch, r["w2"][lo:hi, :])
        dpre = dact * r["slope"][rows, lo:hi].astype(F32)
        low = dpre.astype(BF)
        r["dpre"][rows, lo:hi] = (dpre * weight).astype(BF)
        total = total + nt(low, r["w1"][:, lo:hi])
    xh1 = r["xh1"][rows, :].astype(F32)
    gw = total * weight
    r["dn"][0] += fold(gw * xh1)
    r["dn"][1] += fold(gw)
    return norm_back(total * g1, xh1, r["inv"][rows, 0:1])


def forward(r, stars, leaf_rows):
    centers = pl.ds(leaf_rows, stars)
    xc = r["xc"][...].astype(F32)
    low = xc.astype(BF)
    r.wait("wq", "wk", "wv", "wo", "we", "w1", "w2")
    qs = nn(low, r["wq"][...]) * r["scale"][...]
    kc = nn(low, r["wk"][...])
    vc = nn(low, r["wv"][...])
    own_score = head_sum(qs * kc)
    r["qs"][...] = qs
    r["kc"][...] = kc
    r["vc"][...] = vc
    r["self"][...] = own_score
    r["qcat"][...] = stacked(halves(qs))
    r["xcat"][...] = stacked(halves(xc))

    def tile(start, rows, carry):
        el = r["el"][rows, :]
        ew = el.astype(F32)
        xl = r["xl"][rows, :].astype(F32)
        r["en"][rows, :] = nn(el, r["we"][...]).astype(BF)
        hot = onehot_col(r["idc"][rows, :], stars, 2)
        m = (xl * ew).astype(BF)
        k = nn(m, r["wk"][...])
        r["k"][rows, :] = k.astype(BF)
        r["v"][rows, :] = nn(m, r["wv"][...]).astype(BF)
        r["s"][:, rows] = head_sum_t(nn(hot, r["qcat"][...]) * k)
        mc = (nn(hot, r["xcat"][...]) * ew).astype(BF)
        ub = nn(mc, r["wv"][...]).astype(BF)
        r["ub"][rows, :] = ub
        y = ffn_forward(r, xl + nn(ub, r["wo"][...]), rows)
        r["yl"][rows, :] = y.astype(r["yl"].dtype)
        return carry

    made = ("yl", "en", "k", "v", "ub", "hb", "xh1", "xh2", "inv", "act", "slope")
    r.loop(("xl", "el"), made, tile, 0)

    ids = r["idr"][...]
    live = r["live"][...] > 0.5
    score = r["s"][...]
    top = jnp.where(live, score, NEG)
    lane = lax.broadcasted_iota(jnp.int32, (1, leaf_rows), 1)
    shift = 1
    while shift < 128:
        same = (pltpu.roll(ids, shift, 1) == ids) & (lane >= shift)
        top = jnp.maximum(top, jnp.where(same, pltpu.roll(top, shift, 1), NEG))
        shift *= 2
    hot_row = onehot_row(ids, stars, 1)
    last = hot_row.astype(F32) * r["last"][...]
    present = jnp.sum(last, axis=1, keepdims=True) > 0.5
    last = last.astype(BF)
    star_top = sum(nt(last, part) for part in thirds(top))
    peak = jnp.where(present, jnp.maximum(star_top, own_score), own_score)
    peak_row = tn(stacked(thirds(peak)), onehot_row(ids, stars, 3))
    e = jnp.where(live, jnp.exp(jnp.where(live, score - peak_row, 0.0)), 0.0)
    self_weight = jnp.exp(own_score - peak)
    total = self_weight + sum(nt(hot_row, part) for part in halves(e))
    r["logt"][...] = peak + jnp.log(total)
    weighted = (spread_t(e) * r["v"][...].astype(F32)).astype(BF)
    o = (nn(hot_row, weighted) + spread(self_weight) * vc) / spread(total)
    r["o"][...] = o
    z = xc + nn(o.astype(BF), r["wo"][...])
    r["yc"][...] = ffn_forward(r, z, centers)
    r.finish(*made)


def backward_ffn(r, stars, leaf_rows, own_rows):
    centers = pl.ds(leaf_rows, stars)
    r["dn"][...] = jnp.zeros_like(r["dn"])
    r.wait("w2", "w1")

    def tile(start, rows, carry):
        row = lax.broadcasted_iota(jnp.int32, (TILE, 1), 0) + start
        mine = jnp.where((row >= HALO) & (row < HALO + own_rows), 1.0, 0.0)
        r["dz"][rows, :] = ffn_backward(r, r["gyl"][rows, :].astype(F32), rows, mine)
        return carry

    r.loop(("gyl", "xh2", "inv", "slope", "xh1"), ("dz",), tile, 0)
    r.arrive("xh2", "inv", "slope", "xh1")
    r["dz"][centers, :] = ffn_backward(r, r["gyc"][...].astype(F32), centers, r["cown"][...])
    r.finish("dz")


def backward_attention(r, stars, leaf_rows):
    centers = pl.ds(leaf_rows, stars)
    r.wait("wv", "wo")
    dac = r["dz"][centers, :].astype(BF)
    do = nt(dac, r["wo"][...])
    docat = stacked(halves(do))
    vc = r["vc"][...]
    kc = r["kc"][...]
    qs = r["qs"][...]
    xc = r["xc"][...].astype(F32)
    r["docat"][...] = docat
    r["qcat"][...] = stacked(halves(qs))
    r["xcat"][...] = stacked(halves(xc))
    delta = head_sum(do * r["o"][...])
    self_p = jnp.exp(r["self"][...] - r["logt"][...])
    d_self = self_p * (head_sum(do * vc) - delta)
    coef_c = spread(d_self)
    r["dvc"][...] = (spread(self_p) * do).astype(BF)
    r["dkc"][...] = (coef_c * qs).astype(BF)
    logt_parts = stacked(thirds(r["logt"][...]))
    delta_parts = stacked(thirds(delta))

    def tile(start, rows, total):
        dal = r["dz"][rows, :].astype(BF)
        r["dal"][rows, :] = dal
        r["du"][rows, :] = nt(dal, r["wo"][...]).astype(BF)
        el = r["el"][rows, :].astype(F32)
        hot = onehot_col(r["idc"][rows, :], stars, 2)
        ids_row = r["idr"][:, rows]
        hot3 = onehot_row(ids_row, stars, 3)
        r["mc"][rows, :] = (nn(hot, r["xcat"][...]) * el).astype(BF)
        live = r["live"][:, rows] > 0.5
        score = r["s"][:, rows] - tn(logt_parts, hot3)
        p = jnp.where(live, jnp.exp(jnp.where(live, score, 0.0)), 0.0)
        dor = nn(hot, r["docat"][...])
        ds = p * (head_sum_t(dor * r["v"][rows, :].astype(F32)) - tn(delta_parts, hot3))
        r["dv"][rows, :] = (spread_t(p) * dor).astype(BF)
        coef = spread_t(ds)
        r["dk"][rows, :] = (coef * nn(hot, r["qcat"][...])).astype(BF)
        r["m"][rows, :] = (r["xl"][rows, :].astype(F32) * el).astype(BF)
        part = (coef * r["k"][rows, :].astype(F32)).astype(BF)
        return total + nn(onehot_row(ids_row, stars, 1), part)

    zero = jnp.zeros((stars, D), F32)
    total = r.loop(("el", "v", "xl", "k"), ("du", "dk", "dv"), tile, zero)
    r["dq"][...] = ((total + coef_c * kc) * r["scale"][...]).astype(BF)
    r.finish("du", "dk", "dv")


def weight_grads(r, stars, leaf_rows, own_rows):
    own = r["cown"][...]
    own_leaf = slice(HALO, HALO + own_rows)
    r.arrive("ub", "hb", "act", "ge")
    nat = r["nat"]
    xb = r["xc"][...].astype(BF)
    dq, dkc, dvc, dac = (
        (x.astype(F32) * own).astype(BF)
        for x in (r["dq"][...], r["dkc"][...], r["dvc"][...], r["dz"][leaf_rows:, :])
    )
    nat_store(nat, pl.ds(0, D), tn(xb, dq))
    m = r["m"][own_leaf, :]
    nat_store(nat, pl.ds(D, D), tn(m, r["dk"][own_leaf, :]) + tn(xb, dkc))
    nat_store(
        nat,
        pl.ds(2 * D, D),
        tn(m, r["dv"][own_leaf, :])
        + tn(r["mc"][own_leaf, :], r["du"][own_leaf, :])
        + tn(xb, dvc),
    )
    nat_store(
        nat,
        pl.ds(3 * D, D),
        tn(r["ub"][own_leaf, :], r["dal"][own_leaf, :]) + tn(r["o"][...].astype(BF), dac),
    )
    nat_store(nat, pl.ds(4 * D, D), tn(r["el"][own_leaf, :], r["ge"][own_leaf, :]))
    base = 5 * D
    for j in range(FF // D):
        columns = slice(j * D, (j + 1) * D)
        part = tn(r["hb"][own_leaf, :], r["dpre"][own_leaf, columns]) + tn(
            r["hb"][leaf_rows:, :], r["dpre"][leaf_rows:, columns]
        )
        nat_store(nat, pl.ds(base + j, D, stride=FF // D), part)
    base = base + FF
    for lo, hi in CHUNKS:
        part = tn(r["act"][own_leaf, lo:hi], r["dbr"][own_leaf, :]) + tn(
            r["act"][leaf_rows:, lo:hi], r["dbr"][leaf_rows:, :]
        )
        nat_store(nat, pl.ds(base + lo, hi - lo), part)
    base = base + FF
    sums = [jnp.sum(r["dn"][i], axis=0, keepdims=True) for i in range(4)]
    nat_store(nat, pl.ds(base, 4), jnp.concatenate(sums, axis=0))


def backward_inputs(r, stars, leaf_rows):
    r.wait("wq", "wk", "wv", "we")
    r["xcat"][...] = stacked(halves(r["xc"][...].astype(F32)))

    def tile(start, rows, total):
        dmc = nt(r["du"][rows, :], r["wv"][...])
        el = r["el"][rows, :].astype(F32)
        hot = onehot_col(r["idc"][rows, :], stars, 2)
        dm = nt(r["dk"][rows, :], r["wk"][...]) + nt(r["dv"][rows, :], r["wv"][...])
        r["gxl"][rows, :] = r["dz"][rows, :] + dm * el
        de = dmc * nn(hot, r["xcat"][...]) + dm * r["xl"][rows, :].astype(F32)
        de = de + nt(r["ge"][rows, :], r["we"][...])
        r["gel"][rows, :] = de.astype(r["gel"].dtype)
        return total + nn(onehot_row(r["idr"][:, rows], stars, 1), (dmc * el).astype(BF))

    zero = jnp.zeros((stars, D), F32)
    total = r.loop(("du", "el", "dk", "dv", "xl", "ge", "dz"), ("gxl", "gel"), tile, zero)
    r.arrive("dz")
    r["gxc"][...] = (
        r["dz"][leaf_rows:, :]
        + nt(r["dq"][...], r["wq"][...])
        + nt(r["dkc"][...], r["wk"][...])
        + nt(r["dvc"][...], r["wv"][...])
        + total
    )
    r.finish("gxl", "gel")


def nat_load(nat, at):
    return jnp.concatenate([nat[c, at, :] for c in range(3)], axis=1)[:, :D]


def nat_store(nat, at, value):
    nat[0, at, :] = value[:, 0:128]
    nat[1, at, :] = value[:, 128:256]
    rest = jnp.zeros((value.shape[0], 384 - D), F32)
    nat[2, at, :] = jnp.concatenate([value[:, 256:D], rest], axis=1)


def pack_blocks(r, holders, rows):
    nat = r["nat"]
    lane = lax.broadcasted_iota(jnp.int32, (64, 128), 1)
    half = holders // 2
    for b in range(holders):
        top = b * rows
        at = r["slot"][0, b]
        r["all_a"][at, 0:128, :] = nat[0, top : top + 128, :].astype(BF)
        r["all_a"][at, 128:160, :] = nat[1, top : top + 32, :].astype(BF)
        at = r["slot"][1, b]
        r["all_b"][at, 0:96, :] = nat[1, top + 32 : top + 128, :].astype(BF)
        high = pltpu.roll(nat[2, top + 64 : top + 128, :], 64, 1)
        tail = jnp.where(lane < 64, nat[2, top : top + 64, :], high)
        r["all_b"][at, 96:160, :] = tail.astype(BF)
    for i, name in enumerate(("all_a", "all_b")):
        r["keep"][i * half : (i + 1) * half] = r[name][:half]
        r["send"][i * half : (i + 1) * half] = r[name][half:]


def unpack_blocks(r, holders, rows):
    nat = r["nat"]
    half = holders // 2

    def block(name, slot):
        near, far = r["near_" + name], r["far_" + name]
        at = jnp.where(slot >= half, slot - half, slot)
        flag = jnp.full((PACK // 2, 128), jnp.where(slot >= half, 1.0, 0.0), F32)
        return jnp.where(flag > 0.5, far[at].astype(F32), near[at].astype(F32))

    for b in range(holders):
        top = b * rows
        one = block("a", r["slot"][0, b])
        two = block("b", r["slot"][1, b])
        nat[0, top : top + rows, :] = one[:rows]
        nat[1, top : top + 32, :] = one[128:]
        nat[1, top + 32 : top + rows, :] = two[: rows - 32]
        tail = two[96:]
        nat[2, top : top + 64, :] = tail
        nat[2, top + 64 : top + rows, :] = pltpu.roll(tail, 64, 1)[: rows - 64]
    for i, name in enumerate(WEIGHTS[:5]):
        r[name][...] = nat_load(nat, pl.ds(i * D, D)).astype(BF)
    base = 5 * D
    for j in range(FF // D):
        part = nat_load(nat, pl.ds(base + j, D, stride=FF // D))
        r["w1"][:, j * D : (j + 1) * D] = part.astype(BF)
    base = base + FF
    r["w2"][...] = nat_load(nat, pl.ds(base, FF)).astype(BF)
    base = base + FF
    r["norm"][...] = nat_load(nat, pl.ds(base, 8))


class Refs(dict):
    def __init__(self, refs, leaf_rows):
        super().__init__(refs)
        self.tiles = leaf_rows // TILE
        self.coming, self.going, self.pending = {}, {}, []

    def wait(self, *names):
        for name in names:
            for copy in self.coming.pop(name, ()):
                copy.wait()

    def arrive(self, *names):
        for name in names:
            if name in self.coming:
                for copy in self.coming.pop(name)["all"]():
                    copy.wait()

    def loop(self, names, made, body, init):
        coming = [self.coming[k] for k in names if k in self.coming and "tile" in self.coming[k]]
        going = [self.going[k] for k in made if k in self.going]

        def step(t, carry):
            start = pl.multiple_of(t * TILE, TILE)
            for k in coming:
                k["tile"](t, start).wait()
            carry = body(start, pl.ds(start, TILE), carry)
            for k in going:
                k["tile"](t, start)
            return carry

        result = lax.fori_loop(0, self.tiles, step, init)
        for k in coming:
            k["all"] = k["rest"]
            del k["tile"]
        return result

    def finish(self, *names):
        for name in names:
            if name in self.going:
                self.pending.extend(self.going.pop(name)["rest"]())


def call(body, inputs, outputs, scratch, micros, leaf_rows=TILE, lazy=(), joins=(), own=(), in_smem=(), name=None):
    joins = dict(joins)
    tiles = leaf_rows // TILE
    raw = {k for k, _ in joins.values()} | ({"halo_l", "halo_r"} if joins else set())
    lazy_in = [k for k in inputs if k in lazy] + list(joins)
    buffers = {}
    for k in lazy_in:
        source = inputs[joins[k][0]] if k in joins else inputs[k]
        rows = leaf_rows if k in joins else source.shape[0]
        buffers[k] = ((rows,) + source.shape[1:], source.dtype)
    lazy_out = [k for k in outputs if k in lazy]
    for k in lazy_out:
        shape, dtype = outputs[k]
        buffers[k] = ((leaf_rows,) + shape[1:] if k in own else shape, dtype)
    names = list(inputs) + list(outputs) + list(scratch)

    def kernel(*refs):
        outer = dict(zip(names, refs, strict=False))
        rest = refs[len(names) :]
        held = dict(zip(buffers, rest, strict=False))
        sems = rest[-1] if buffers else None
        r = Refs({**outer, **held}, leaf_rows)
        copy = pltpu.make_async_copy
        for i, k in enumerate(buffers):
            inner, total = held[k], buffers[k][0][0]
            if k in lazy_out:
                target = outer[k]
                if k in own:
                    cut = pl.ds(HALO, leaf_rows - 2 * HALO)

                    def last(inner=inner, target=target, cut=cut, i=i):
                        one = copy(inner.at[cut], target, sems.at[i, tiles])
                        one.start()
                        return [one]

                    def per_tile(t, start):
                        return None

                else:

                    def per_tile(t, start, inner=inner, target=target, i=i):
                        rows = pl.ds(start, TILE)
                        copy(inner.at[rows], target.at[rows], sems.at[i, t]).start()

                    def last(inner=inner, target=target, i=i, total=total):
                        done = [
                            copy(inner.at[pl.ds(t * TILE, TILE)], target.at[pl.ds(t * TILE, TILE)], sems.at[i, t])
                            for t in range(tiles)
                        ]
                        if total > leaf_rows:
                            rows = pl.ds(leaf_rows, total - leaf_rows)
                            done.append(copy(inner.at[rows], target.at[rows], sems.at[i, tiles]))
                            done[-1].start()
                        return done

                r.going[k] = {"tile": per_tile, "rest": last}
            elif total < leaf_rows or k in WEIGHTS:
                one = copy(outer[k], inner, sems.at[i, 0])
                one.start()
                r.coming[k] = [one]
            else:

                def wait_for(t, start, inner=inner, i=i):
                    rows = inner.at[pl.ds(start, TILE)]
                    return copy(rows, rows, sems.at[i, t])

                def behind(inner=inner, i=i, total=total):
                    if total == leaf_rows:
                        return []
                    rows = inner.at[pl.ds(leaf_rows, total - leaf_rows)]
                    return [copy(rows, rows, sems.at[i, tiles])]

                def every(wait_for=wait_for, behind=behind):
                    return [wait_for(t, t * TILE) for t in range(tiles)] + behind()

                r.coming[k] = {"tile": wait_for, "rest": behind, "all": every}
        for t in range(tiles + 1):
            for i, k in enumerate(buffers):
                if k in lazy_out or not isinstance(r.coming.get(k), dict):
                    continue
                inner, total = held[k], buffers[k][0][0]
                low, high = t * TILE, min((t + 1) * TILE, leaf_rows)
                if t == tiles:
                    high = total
                if k in joins:
                    source, place = joins[k]
                    stop = leaf_rows - HALO
                    pieces = [
                        (outer["halo_l"], place * HALO, 0, HALO),
                        (outer[source], 0, HALO, stop),
                        (outer["halo_r"], place * HALO, stop, leaf_rows),
                    ]
                else:
                    pieces = [(outer[k], 0, 0, total)]
                for ref, offset, first, stop in pieces:
                    a, b = max(first, low), min(stop, high)
                    if a < b:
                        piece = ref.at[pl.ds(a - first + offset, b - a)]
                        copy(piece, inner.at[pl.ds(a, b - a)], sems.at[i, t]).start()
        body(r)
        for k in list(r.coming):
            if isinstance(r.coming[k], dict):
                r.arrive(k)
            else:
                r.wait(k)
        r.finish(*list(r.going))
        for one in r.pending:
            one.wait()

    vmem = pl.BlockSpec(memory_space=pltpu.VMEM)
    smem = pl.BlockSpec(memory_space=pltpu.SMEM)
    anywhere = pl.BlockSpec(memory_space=pl.ANY)

    def place(k):
        return smem if k in in_smem else anywhere if k in lazy or k in raw else vmem

    results = pl.pallas_call(
        kernel,
        out_shape=[jax.ShapeDtypeStruct(s, d) for s, d in outputs.values()],
        in_specs=[place(k) for k in inputs],
        out_specs=[place(k) for k in outputs],
        scratch_shapes=[pltpu.VMEM(s, d) for s, d in scratch.values()]
        + [pltpu.VMEM(s, d) for s, d in buffers.values()]
        + ([pltpu.SemaphoreType.DMA((len(buffers), tiles + 1))] if buffers else []),
        compiler_params=pltpu.CompilerParams(vmem_limit_bytes=VMEM),
        cost_estimate=pl.CostEstimate(
            flops=int(micros * 1e9), bytes_accessed=int(micros * 1e6), transcendentals=0
        ),
        name=name,
    )(*inputs.values())
    return dict(zip(outputs, results, strict=True))


def saved_shapes(stars, leaf_rows):
    rows = leaf_rows + stars
    return {
        "k": ((leaf_rows, D), BF),
        "v": ((leaf_rows, D), BF),
        "ub": ((leaf_rows, D), BF),
        "hb": ((rows, D), BF),
        "xh1": ((rows, D), BF),
        "xh2": ((rows, D), BF),
        "act": ((rows, FF), BF),
        "slope": ((rows, FF), BF),
        "inv": ((rows, 128), F32),
        "s": ((HP, leaf_rows), F32),
        "qs": ((stars, D), F32),
        "kc": ((stars, D), F32),
        "vc": ((stars, D), F32),
        "o": ((stars, D), F32),
        "self": ((stars, HP), F32),
        "logt": ((stars, HP), F32),
    }


def pair_shapes(stars, *names):
    return {k: ((2 * stars, D), BF) for k in names}


def leaf_shapes(leaf_rows, *names):
    return {k: ((leaf_rows, D), BF) for k in names}


def star_shapes(stars, *names):
    return {k: ((stars, D), BF) for k in names}


def ffn_scratch(stars, leaf_rows):
    rows = leaf_rows + stars
    return {"dn": ((4, 8, D), F32), "dbr": ((rows, D), BF), "dpre": ((rows, FF), BF)}


def exchange(x, stage, value, sizes):
    axis, shift, bits = stage
    return lax.ppermute(x, axis, [(i, i ^ (value << shift)) for i in range(sizes[axis])])


def tree_stages(sizes, swap):
    bits = {axis: size.bit_length() - 1 for axis, size in sizes.items()}

    def cut(axis, start, stop):
        return [(axis, i, min(2, stop - i)) for i in range(start, stop, 2)]

    middle = [cut("leaf", 1, bits["leaf"]), cut("graph", 0, 1)]
    if swap:
        middle = middle[::-1]
    return [("leaf", 0, 1)] + middle[0] + middle[1] + cut("graph", 1, bits["graph"])


def tree_slot(relative, stages, leaf_bits):
    slot = jnp.zeros_like(relative)
    for axis, shift, bits in stages:
        shift = shift + (leaf_bits if axis == "graph" else 0)
        slot = (slot << bits) | ((relative >> shift) & ((1 << bits) - 1))
    return slot


def gather_step(held, stage, sizes):
    parts = [held] + [exchange(held, stage, v, sizes) for v in range(1, 1 << stage[2])]
    return jnp.concatenate(parts, axis=0)


def reduce_step(held, stage, sizes, final):
    count = held.shape[0] >> stage[2]
    total = held[:count].astype(F32)
    for v in range(1, 1 << stage[2]):
        total = total + exchange(held[v * count : (v + 1) * count], stage, v, sizes).astype(F32)
    return total if final else total.astype(BF)


def star_total(x, sizes):
    for bit in range(sizes["leaf"].bit_length() - 1):
        x = x + exchange(x, ("leaf", bit, 1), 1, sizes)
    return x


def after(x, *first):
    return lax.optimization_barrier((x, *first))[0]


def to_rows(flat, rows):
    block = jnp.pad(flat.reshape(rows, D), ((0, 128 - rows), (0, 0)))
    tail = jnp.pad(block[:, 256:], ((0, 0), (0, 320 - D)))
    return jnp.concatenate(
        [block[:, :128], block[:, 128:256], jnp.concatenate([tail[:64], tail[64:]], axis=1)], axis=0
    )


def from_rows(packed, rows):
    tail = jnp.concatenate([packed[256:, : D - 256], packed[256:, 64 : D - 192]], axis=0)
    block = jnp.concatenate([packed[:128], packed[128:256], tail], axis=1)
    return block[:rows].reshape(-1)


def split_flat(vec):
    square = D * D
    mats = [vec[i * square : (i + 1) * square].reshape(D, D) for i in range(5)]
    at = 5 * square
    w1 = vec[at : at + D * FF].reshape(D, FF)
    at = at + D * FF
    w2 = vec[at : at + FF * D].reshape(FF, D)
    at = at + FF * D
    norm = jnp.pad(vec[at : at + 4 * D].reshape(4, D).astype(F32), ((0, 4), (0, 0)))
    return dict(zip(WEIGHTS, mats + [w1, w2, norm], strict=True))


def halo(x):
    size = lax.axis_size("leaf")
    last, first = x
    left = lax.ppermute(last, "leaf", [(i, i + 1) for i in range(size - 1)])
    right = lax.ppermute(first, "leaf", [(i + 1, i) for i in range(size - 1)])
    return left, right


def local(
    weights,
    first_moment,
    second_moment,
    centers,
    leaves,
    edge_feats,
    center_cot,
    leaf_cot,
    edge_cot,
    graph_ids,
    star_sizes,
    leaf_mask,
    owner_list,
):
    sizes = {"graph": lax.axis_size("graph"), "leaf": lax.axis_size("leaf")}
    holders = sizes["graph"] * sizes["leaf"]
    block_len = weights.shape[1]
    block_rows = block_len // D
    in_rows = block_len % D == 0 and 64 < block_rows <= 128
    stars = centers.shape[1]
    own_rows = leaves.shape[1]
    leaf_rows = own_rows + 2 * HALO

    orders = [tree_stages(sizes, swap) for swap in (False, True)]
    me = lax.axis_index(("graph", "leaf"))
    leaf_bits = sizes["leaf"].bit_length() - 1
    slot = jnp.stack([tree_slot(owner_list ^ me, stages, leaf_bits) for stages in orders])
    nat_rows = ROWS_LAYER + 12
    half = PACK // 2
    n_steps = len(orders[0])
    weights_low = weights.astype(BF)

    def gather_begin(i):
        if not in_rows:
            return [gather_step(weights_low[i][None], orders[0][-1], sizes)]
        held = gather_step(to_rows(weights_low[i], block_rows)[None], orders[0][-1], sizes)
        return [held[:, :half], held[:, half:]]

    def gather_more(held, n):
        return [gather_step(h, o[n], sizes) for h, o in zip(held, orders, strict=False)]

    def gather_end(held):
        if not in_rows:
            return gather_step(held[0], orders[0][0], sizes)
        far = [exchange(h, orders[0][0], 1, sizes) for h in held]
        return dict(zip(("near_a", "near_b", "far_a", "far_b"), held + far, strict=True))

    def unpack(got):
        if not in_rows:
            return split_flat(jnp.take(got, slot[0], axis=0).reshape(-1))
        return call(
            lambda r: unpack_blocks(r, holders, block_rows),
            {"slot": slot, **got},
            dict(zip(WEIGHTS, WEIGHT_SHAPES, strict=True)),
            {"nat": ((3, nat_rows, 128), F32)},
            4,
            in_smem=("slot",),
            name="unpack",
        )

    raw = {"leaves": leaves[0], "edges": edge_feats[0], "lcot": leaf_cot[0], "ecot": edge_cot[0]}
    marks = jnp.pad((graph_ids + 1).astype(BF), ((0, 15), (0, 0)))
    marks = jnp.concatenate([marks[:8], jnp.broadcast_to(leaf_mask.astype(BF), (8, own_rows))], axis=0)

    def edge(cut):
        note = jnp.pad(marks[:, cut], ((0, 0), (0, D - HALO)))
        return jnp.concatenate([x[cut] for x in raw.values()] + [note], axis=0)

    held_zero = gather_begin(0)
    left, right = halo((edge(slice(own_rows - HALO, own_rows)), edge(slice(0, HALO))))
    raw = {**raw, "halo_l": left, "halo_r": right}
    at = len(raw) - 2

    def with_marks(line, mine):
        sides = [x[at * HALO + line, :HALO].astype(jnp.int32)[None] for x in (left, right)]
        return jnp.concatenate([sides[0], mine, sides[1]], axis=1)

    ids = with_marks(0, graph_ids + 1) - 1
    live = with_marks(8, leaf_mask).astype(F32)
    edge_id = jnp.full((1, 1), -1, jnp.int32)
    last = (ids != jnp.concatenate([ids[:, 1:], edge_id], axis=1)).astype(F32)
    first = graph_ids[0] != ids[0, HALO - 1 : HALO - 1 + own_rows]
    star_index = jnp.arange(stars, dtype=jnp.int32)
    star_own = jnp.any((star_index[:, None] == graph_ids) & first[None, :], axis=1)[:, None]
    scale = (jnp.log(star_sizes[0].astype(F32)) / (math.log(32.0) * math.sqrt(HEAD)))[:, None]
    base = {
        "idc": ids.reshape(-1, 1),
        "idr": ids,
        "live": live,
        "last": last,
        "scale": scale,
        "cown": star_own.astype(F32),
    }
    saved = saved_shapes(stars, leaf_rows)
    rows = leaf_rows + stars
    nat = {"nat": ((3, nat_rows, 128), F32)}
    if in_rows:
        grads_out = {k: ((holders, half, 128), BF) for k in ("keep", "send")}
        grads_scratch = {k: ((holders, half, 128), BF) for k in ("all_a", "all_b")} | nat
    else:
        grads_out, grads_scratch = nat, {}
    lazy = ("w1", "w2", "wq", "wk", "wv", "wo", "we", "xl", "el", "gyl", "ge", "yl", "en", "inv") + (
        "k", "v", "ub", "hb", "xh1", "xh2", "act", "slope", "dz", "du", "dk", "dv", "gxl", "gel",
    )
    f_scratch = pair_shapes(stars, "qcat", "xcat")
    a_scratch = pair_shapes(stars, "qcat", "xcat", "docat") | leaf_shapes(leaf_rows, "dal", "mc", "m")
    handed = (
        {"dz": ((rows, D), F32)}
        | leaf_shapes(leaf_rows, "du", "dk", "dv")
        | star_shapes(stars, "dq", "dkc", "dvc")
    )
    squares = ("wq", "wk", "wv", "wo", "we")

    def halves_of(*names):
        return {k: raw[k] for k in (*names, "halo_l", "halo_r")}

    join = {"xl": ("leaves", 0), "el": ("edges", 1), "gyl": ("lcot", 2), "ge": ("ecot", 3)}

    def joined(*names):
        return {k: join[k] for k in names}

    held_one = None
    for n in range(n_steps - 2, 0, -1):
        held_zero = gather_more(held_zero, n)
        if held_one is None:
            weights_low = after(weights_low, *held_zero) if n == 1 else weights_low
            held_one = gather_begin(1)
    held_one = list(lax.optimization_barrier((held_one, held_zero))[0])
    params = [unpack(gather_end(held_zero))]
    held_one = gather_more(held_one, n_steps - 2)
    centers_in, held_one = lax.optimization_barrier((centers[0], held_one))
    for n in range(n_steps - 3, 0, -1):
        held_one = gather_more(list(held_one), n)
    one = call(
        lambda r: forward(r, stars, leaf_rows),
        {**{k: params[0][k] for k in squares}, **halves_of("leaves", "edges"), **base}
        | {**{k: params[0][k] for k in ("w1", "w2", "norm")}, "xc": centers_in},
        {"yc": ((stars, D), F32), "yl": ((leaf_rows, D), F32), "en": ((leaf_rows, D), BF), **saved},
        f_scratch,
        25,
        leaf_rows,
        lazy=lazy,
        joins=joined("xl", "el"),
        name="forward",
    )
    held_one = list(lax.optimization_barrier((held_one, one["yc"]))[0])
    params.append(unpack(gather_end(held_one)))

    def grads_of(r):
        backward_ffn(r, stars, leaf_rows, own_rows)
        backward_attention(r, stars, leaf_rows)
        weight_grads(r, stars, leaf_rows, own_rows)
        if in_rows:
            pack_blocks(r, holders, block_rows)

    def both(r):
        forward(r, stars, leaf_rows)
        grads_of(r)

    two_in = {"xc": one["yc"], "xl": one["yl"], "el": one["en"], **halves_of("ecot")}
    own_out = {"yl": ((own_rows, D), BF), "en": ((own_rows, D), BF)}
    two = call(
        both,
        {**{k: params[1][k] for k in squares}, **two_in, **base, "slot": slot}
        | {k: params[1][k] for k in ("w1", "w2", "norm")}
        | {"gyc": center_cot[0], **halves_of("lcot")},
        {"yc": ((stars, D), F32), **own_out, **handed, **grads_out},
        {**a_scratch, **saved, **ffn_scratch(stars, leaf_rows), **grads_scratch},
        45,
        leaf_rows,
        in_smem=("slot",),
        lazy=lazy,
        joins=joined("gyl", "ge"),
        own=("yl", "en"),
        name="last",
    )

    def inputs_of(params, given, made, joins, out_rows, dtype, name):
        return call(
            lambda r: backward_inputs(r, stars, leaf_rows),
            {
                **{k: params[k] for k in ("wv", "wk", "we", "wq")},
                **{k: base[k] for k in ("idc", "idr")},
                **given,
                **{k: made[k] for k in handed},
            },
            {"gxc": ((stars, D), F32), "gxl": ((out_rows, D), F32), "gel": ((out_rows, D), dtype)},
            pair_shapes(stars, "xcat"),
            9,
            leaf_rows,
            lazy=lazy,
            joins=joins,
            own=("gxl", "gel") if out_rows == own_rows else (),
            name=name,
        )

    def begin(made):
        if not in_rows:
            flat = jnp.swapaxes(made["nat"][:, :ROWS_LAYER], 0, 1).reshape(ROWS_LAYER, 384)
            flat = flat[:, :D].reshape(holders, block_len)
            placed = jnp.zeros_like(flat).at[slot[0]].set(flat).astype(BF)
            return [reduce_step(placed, orders[0][0], sizes, False)]
        got = exchange(made["send"], orders[0][0], 1, sizes)
        count = holders // 2
        return [
            (made["keep"][i : i + count].astype(F32) + got[i : i + count].astype(F32)).astype(BF)
            for i in (0, count)
        ]

    def advance(held, n):
        if n == n_steps - 1:
            return [reduce_step(jnp.concatenate(held, axis=1), orders[0][n], sizes, True)]
        return [reduce_step(h, o[n], sizes, False) for h, o in zip(held, orders, strict=False)]

    def end(held):
        return from_rows(held[0][0], block_rows) if in_rows else held[0][0]

    held_two = begin(two)
    two_grads = inputs_of(params[1], two_in, two, joined("ge"), leaf_rows, BF, "last_inputs")
    gyc, held_two = lax.optimization_barrier((two_grads["gxc"], held_two))
    held_two = advance(held_two, 1)
    three = call(
        grads_of,
        {
            "w2": params[0]["w2"],
            "gyl": two_grads["gxl"],
            **{k: one[k] for k in ("xh2", "inv", "slope")},
            "w1": params[0]["w1"],
            "xh1": one["xh1"],
            **{k: params[0][k] for k in ("wo", "wv", "norm")},
            **{k: one[k] for k in saved if k not in ("xh2", "inv", "slope", "xh1")},
            **halves_of("leaves", "edges"),
            **base,
            "slot": slot,
            "xc": centers[0],
            "ge": two_grads["gel"],
            "gyc": gyc,
        },
        {**handed, **grads_out},
        {**a_scratch, **ffn_scratch(stars, leaf_rows), **grads_scratch},
        28,
        leaf_rows,
        in_smem=("slot",),
        lazy=lazy,
        joins=joined("xl", "el"),
        name="first",
    )
    handed_three = {k: three[k] for k in handed}
    if n_steps > 2:
        handed_three["dq"], held_two = lax.optimization_barrier((three["dq"], held_two))
        held_two = advance(list(held_two), 2)
    held_three = begin(three)
    three_in = {"xc": centers[0], "ge": two_grads["gel"], **halves_of("leaves", "edges")}
    three_grads = inputs_of(
        params[0], three_in, handed_three, joined("xl", "el"), own_rows, F32, "first_inputs"
    )
    for n in range(1, n_steps):
        if n + 2 < n_steps:
            held_two = advance(held_two, n + 2)
        held_three = advance(held_three, n)
    grad_total = jnp.stack([end(held_three), end(held_two)])

    centers_out = star_total(jnp.where(star_own, two["yc"], 0.0).astype(BF), sizes)
    grad_centers = star_total(jnp.where(star_own, three_grads["gxc"], 0.0), sizes)
    first_new = BETA_ONE * first_moment + (1.0 - BETA_ONE) * grad_total
    second_new = BETA_TWO * second_moment + (1.0 - BETA_TWO) * grad_total * grad_total
    step_one = first_new / (1.0 - BETA_ONE**STEP)
    step_two = second_new / (1.0 - BETA_TWO**STEP)
    weights_new = weights - RATE * (step_one / (jnp.sqrt(step_two) + EPS_ADAM) + DECAY * weights)
    return (
        centers_out[None],
        two["yl"][None],
        two["en"][None],
        grad_centers[None],
        three_grads["gxl"][None],
        three_grads["gel"][None],
        first_new,
        second_new,
        weights_new,
        weights_new.astype(BF),
        grad_total,
    )


def solution(mesh):
    both = ("graph", "leaf")
    return jax.shard_map(
        local,
        mesh=mesh,
        in_specs=(
            P(None, both),
            P(None, both),
            P(None, both),
            P("graph", None, None),
            P("graph", "leaf", None),
            P("graph", "leaf", None),
            P("graph", None, None),
            P("graph", "leaf", None),
            P("graph", "leaf", None),
            P("graph", "leaf"),
            P("graph", None),
            P("graph", "leaf"),
            P(),
        ),
        out_specs=(
            P("graph", None, None),
            P("graph", "leaf", None),
            P("graph", "leaf", None),
            P("graph", None, None),
            P("graph", "leaf", None),
            P("graph", "leaf", None),
            P(None, both),
            P(None, both),
            P(None, both),
            P(None, both),
            P(None, both),
        ),
        check_vma=False,
    )
```

```python
import math

import jax
import jax.numpy as jnp
from jax import lax
from jax.experimental import pallas as pl
from jax.experimental.pallas import tpu as pltpu
from jax.sharding import PartitionSpec as P

D = 300
HEADS = 12
HEAD = 25
FF = 1200
LAYERS = 2
STEP = 5
ROWS_LAYER = 5 * D + 2 * FF + 4

NEG = -1e30
EPS_NORM = 1e-05
BETA_ONE = 0.9
BETA_TWO = 0.999
RATE = 0.05
DECAY = 0.01
EPS_ADAM = 1e-08
INV_ROOT_TWO = 0.7071067811865476
INV_ROOT_TWO_PI = 0.3989422804014327

HALO = 128
TILE = 256
HP = 16
PACK = 320
CHUNKS = tuple((i, min(i + 256, FF)) for i in range(0, FF, 256))
VMEM = 56 << 20
F32 = jnp.float32
BF = jnp.bfloat16

WEIGHTS = ("wq", "wk", "wv", "wo", "we", "w1", "w2", "norm")
WEIGHT_SHAPES = tuple([((D, D), BF)] * 5 + [((D, FF), BF), ((FF, D), BF), ((8, D), F32)])


def nn(a, b):
    return lax.dot_general(a, b, (((1,), (0,)), ((), ())), preferred_element_type=F32)


def nt(a, b):
    return lax.dot_general(a, b, (((1,), (1,)), ((), ())), preferred_element_type=F32)


def tn(a, b):
    return lax.dot_general(a, b, (((0,), (0,)), ((), ())), preferred_element_type=F32)


def halves(x):
    high = x.astype(BF)
    return high, (x - high.astype(F32)).astype(BF)


def thirds(x):
    high = x.astype(BF)
    rest = x - high.astype(F32)
    mid = rest.astype(BF)
    return high, mid, (rest - mid.astype(F32)).astype(BF)


def stacked(parts, axis=0):
    return jnp.concatenate([p.astype(F32) for p in parts], axis=axis).astype(BF)


def table(rows, repeat=1):
    head = lax.broadcasted_iota(jnp.int32, (repeat * rows, D), 0) % rows
    feature = lax.broadcasted_iota(jnp.int32, (repeat * rows, D), 1)
    low = head * HEAD
    return jnp.where((feature >= low) & (feature < low + HEAD), 1.0, 0.0).astype(BF)


def head_sum(values):
    high, low = halves(values)
    tab = table(HP)
    return nt(high, tab) + nt(low, tab)


def head_sum_t(values):
    high, low = halves(values)
    tab = table(HP)
    return nt(tab, high) + nt(tab, low)


def spread(values):
    high, low = halves(values)
    tab = table(HP)
    return nn(high, tab) + nn(low, tab)


def spread_t(values):
    return tn(stacked(halves(values)), table(HP, 2))


def onehot_col(ids, stars, repeat):
    lane = lax.broadcasted_iota(jnp.int32, (ids.shape[0], repeat * stars), 1)
    hit = lane == ids
    for i in range(1, repeat):
        hit = hit | (lane == ids + i * stars) & (ids >= 0)
    return jnp.where(hit, 1.0, 0.0).astype(BF)


def onehot_row(ids, stars, repeat):
    sub = lax.broadcasted_iota(jnp.int32, (repeat * stars, ids.shape[1]), 0)
    hit = sub == ids
    for i in range(1, repeat):
        hit = hit | (sub == ids + i * stars) & (ids >= 0)
    return jnp.where(hit, 1.0, 0.0).astype(BF)


def row_mean(x):
    return jnp.sum(x, axis=-1, keepdims=True) * (1.0 / D)


def normalized(x):
    dev = x - row_mean(x)
    inverse = lax.rsqrt(row_mean(dev * dev) + EPS_NORM)
    return dev * inverse, inverse


def norm_back(grad, scaled, inverse):
    return inverse * (grad - row_mean(grad) - scaled * row_mean(grad * scaled))


def ffn_forward(r, z, rows):
    norm = r.norm
    g1, b1, g2, b2 = (norm[i : i + 1, :] for i in range(4))
    xh1, inv1 = normalized(z)
    h = xh1 * g1 + b1
    hb = h.astype(BF)
    r.hb[rows, :] = hb
    r.xh1[rows, :] = xh1.astype(BF)
    r.inv[rows, 0:1] = inv1
    total = h
    for lo, hi in CHUNKS:
        pre = nn(hb, r.w1[:, lo:hi])
        cdf = 0.5 * (1.0 + lax.erf(pre * INV_ROOT_TWO))
        act = (pre * cdf).astype(BF)
        r.act[rows, lo:hi] = act
        r.slope[rows, lo:hi] = (
            cdf + pre * jnp.exp(-0.5 * pre * pre) * INV_ROOT_TWO_PI
        ).astype(BF)
        total = total + nn(act, r.w2[lo:hi, :])
    xh2, inv2 = normalized(total)
    r.xh2[rows, :] = xh2.astype(BF)
    r.inv[rows, 1:2] = inv2
    return xh2 * g2 + b2


def fold(x):
    return jnp.sum(x.reshape(x.shape[0] // 8, 8, x.shape[1]), axis=0)


def ffn_backward(r, gy, rows, weight):
    norm = r.norm
    g1, g2 = norm[0:1, :], norm[2:3, :]
    xh2 = r.xh2[rows, :].astype(F32)
    gw = gy * weight
    r.dn[2] += fold(gw * xh2)
    r.dn[3] += fold(gw)
    mid = norm_back(gy * g2, xh2, r.inv[rows, 1:2])
    branch = mid.astype(BF)
    r.dbr[rows, :] = (mid * weight).astype(BF)
    total = mid
    for lo, hi in CHUNKS:
        dact = nt(branch, r.w2[lo:hi, :])
        dpre = dact * r.slope[rows, lo:hi].astype(F32)
        low = dpre.astype(BF)
        r.dpre[rows, lo:hi] = (dpre * weight).astype(BF)
        total = total + nt(low, r.w1[:, lo:hi])
    xh1 = r.xh1[rows, :].astype(F32)
    gw = total * weight
    r.dn[0] += fold(gw * xh1)
    r.dn[1] += fold(gw)
    return norm_back(total * g1, xh1, r.inv[rows, 0:1])


def forward(r, stars, leaf_rows):
    centers = pl.ds(leaf_rows, stars)
    xc = r.xc[...].astype(F32)
    low = xc.astype(BF)
    r.wait("wq", "wk", "wv", "wo", "we", "w1", "w2")
    qs = nn(low, r.wq[...]) * r.scale[...]
    kc = nn(low, r.wk[...])
    vc = nn(low, r.wv[...])
    own_score = head_sum(qs * kc)
    r.qs[...] = qs
    r.kc[...] = kc
    r.vc[...] = vc
    r.self[...] = own_score
    r.qcat[...] = stacked(halves(qs))
    r.xcat[...] = stacked(halves(xc))

    def tile(start, rows, carry):
        el = r.el[rows, :]
        ew = el.astype(F32)
        xl = r.xl[rows, :].astype(F32)
        r.en[rows, :] = nn(el, r.we[...]).astype(BF)
        hot = onehot_col(r.idc[rows, :], stars, 2)
        m = (xl * ew).astype(BF)
        k = nn(m, r.wk[...])
        r.k[rows, :] = k.astype(BF)
        r.v[rows, :] = nn(m, r.wv[...]).astype(BF)
        r.s[:, rows] = head_sum_t(nn(hot, r.qcat[...]) * k)
        mc = (nn(hot, r.xcat[...]) * ew).astype(BF)
        ub = nn(mc, r.wv[...]).astype(BF)
        r.ub[rows, :] = ub
        y = ffn_forward(r, xl + nn(ub, r.wo[...]), rows)
        r.yl[rows, :] = y.astype(r.yl.dtype)
        return carry

    made = ("yl", "en", "k", "v", "ub", "hb", "xh1", "xh2", "inv", "act", "slope")
    r.loop(("xl", "el"), made, tile, 0)

    ids = r.idr[...]
    live = r.live[...] > 0.5
    score = r.s[...]
    top = jnp.where(live, score, NEG)
    lane = lax.broadcasted_iota(jnp.int32, (1, leaf_rows), 1)
    shift = 1
    while shift < 128:
        same = (pltpu.roll(ids, shift, 1) == ids) & (lane >= shift)
        top = jnp.maximum(top, jnp.where(same, pltpu.roll(top, shift, 1), NEG))
        shift *= 2
    hot_row = onehot_row(ids, stars, 1)
    last = hot_row.astype(F32) * r.last[...]
    present = jnp.sum(last, axis=1, keepdims=True) > 0.5
    last = last.astype(BF)
    star_top = sum(nt(last, part) for part in thirds(top))
    peak = jnp.where(present, jnp.maximum(star_top, own_score), own_score)
    peak_row = tn(stacked(thirds(peak)), onehot_row(ids, stars, 3))
    e = jnp.where(live, jnp.exp(jnp.where(live, score - peak_row, 0.0)), 0.0)
    self_weight = jnp.exp(own_score - peak)
    total = self_weight + sum(nt(hot_row, part) for part in halves(e))
    r.logt[...] = peak + jnp.log(total)
    weighted = (spread_t(e) * r.v[...].astype(F32)).astype(BF)
    o = (nn(hot_row, weighted) + spread(self_weight) * vc) / spread(total)
    r.o[...] = o
    z = xc + nn(o.astype(BF), r.wo[...])
    r.yc[...] = ffn_forward(r, z, centers)
    r.finish(*made)


def backward_ffn(r, stars, leaf_rows, own_rows):
    centers = pl.ds(leaf_rows, stars)
    r.dn[...] = jnp.zeros_like(r.dn)
    r.wait("w2", "w1")

    def tile(start, rows, carry):
        row = lax.broadcasted_iota(jnp.int32, (TILE, 1), 0) + start
        mine = jnp.where((row >= HALO) & (row < HALO + own_rows), 1.0, 0.0)
        r.dz[rows, :] = ffn_backward(r, r.gyl[rows, :].astype(F32), rows, mine)
        return carry

    r.loop(("gyl", "xh2", "inv", "slope", "xh1"), ("dz", "dbr", "dpre"), tile, 0)
    r.arrive("xh2", "inv", "slope", "xh1")
    r.dz[centers, :] = ffn_backward(r, r.gyc[...].astype(F32), centers, r.cown[...])
    r.finish("dz", "dbr", "dpre")


def backward_attention(r, stars, leaf_rows):
    centers = pl.ds(leaf_rows, stars)
    r.wait("wv", "wo")
    r.arrive_rest("dz")
    dac = r.dz[centers, :].astype(BF)
    do = nt(dac, r.wo[...])
    docat = stacked(halves(do))
    vc = r.vc[...]
    kc = r.kc[...]
    qs = r.qs[...]
    xc = r.xc[...].astype(F32)
    r.docat[...] = docat
    r.qcat[...] = stacked(halves(qs))
    r.xcat[...] = stacked(halves(xc))
    delta = head_sum(do * r.o[...])
    self_p = jnp.exp(r.self[...] - r.logt[...])
    d_self = self_p * (head_sum(do * vc) - delta)
    coef_c = spread(d_self)
    r.dvc[...] = (spread(self_p) * do).astype(BF)
    r.dkc[...] = (coef_c * qs).astype(BF)
    logt_parts = stacked(thirds(r.logt[...]))
    delta_parts = stacked(thirds(delta))

    def tile(start, rows, total):
        dal = r.dz[rows, :].astype(BF)
        r.dal[rows, :] = dal
        r.du[rows, :] = nt(dal, r.wo[...]).astype(BF)
        el = r.el[rows, :].astype(F32)
        hot = onehot_col(r.idc[rows, :], stars, 2)
        ids_row = r.idr[:, rows]
        hot3 = onehot_row(ids_row, stars, 3)
        r.mc[rows, :] = (nn(hot, r.xcat[...]) * el).astype(BF)
        live = r.live[:, rows] > 0.5
        score = r.s[:, rows] - tn(logt_parts, hot3)
        p = jnp.where(live, jnp.exp(jnp.where(live, score, 0.0)), 0.0)
        dor = nn(hot, r.docat[...])
        ds = p * (head_sum_t(dor * r.v[rows, :].astype(F32)) - tn(delta_parts, hot3))
        r.dv[rows, :] = (spread_t(p) * dor).astype(BF)
        coef = spread_t(ds)
        r.dk[rows, :] = (coef * nn(hot, r.qcat[...])).astype(BF)
        r.m[rows, :] = (r.xl[rows, :].astype(F32) * el).astype(BF)
        part = (coef * r.k[rows, :].astype(F32)).astype(BF)
        return total + nn(onehot_row(ids_row, stars, 1), part)

    zero = jnp.zeros((stars, D), F32)
    total = r.loop(("dz", "el", "v", "xl", "k"), ("du", "dk", "dv"), tile, zero)
    r.dq[...] = ((total + coef_c * kc) * r.scale[...]).astype(BF)
    r.finish("du", "dk", "dv")


def weight_grads(r, stars, leaf_rows, own_rows):
    own = r.cown[...]
    own_leaf = slice(HALO, HALO + own_rows)
    r.arrive("dz", "ub", "ge", "hb", "dpre", "act", "dbr")
    nat = r.nat
    xb = r.xc[...].astype(BF)
    dq, dkc, dvc, dac = (
        (x.astype(F32) * own).astype(BF)
        for x in (r.dq[...], r.dkc[...], r.dvc[...], r.dz[leaf_rows:, :])
    )
    nat_store(nat, pl.ds(0, D), tn(xb, dq))
    m = r.m[own_leaf, :]
    nat_store(nat, pl.ds(D, D), tn(m, r.dk[own_leaf, :]) + tn(xb, dkc))
    nat_store(
        nat,
        pl.ds(2 * D, D),
        tn(m, r.dv[own_leaf, :])
        + tn(r.mc[own_leaf, :], r.du[own_leaf, :])
        + tn(xb, dvc),
    )
    nat_store(
        nat,
        pl.ds(3 * D, D),
        tn(r.ub[own_leaf, :], r.dal[own_leaf, :]) + tn(r.o[...].astype(BF), dac),
    )
    nat_store(nat, pl.ds(4 * D, D), tn(r.el[own_leaf, :], r.ge[own_leaf, :]))
    base = 5 * D
    for j in range(FF // D):
        columns = slice(j * D, (j + 1) * D)
        part = tn(r.hb[own_leaf, :], r.dpre[own_leaf, columns]) + tn(
            r.hb[leaf_rows:, :], r.dpre[leaf_rows:, columns]
        )
        nat_store(nat, pl.ds(base + j, D, stride=FF // D), part)
    base = base + FF
    for lo, hi in CHUNKS:
        part = tn(r.act[own_leaf, lo:hi], r.dbr[own_leaf, :]) + tn(
            r.act[leaf_rows:, lo:hi], r.dbr[leaf_rows:, :]
        )
        nat_store(nat, pl.ds(base + lo, hi - lo), part)
    base = base + FF
    sums = [jnp.sum(r.dn[i], axis=0, keepdims=True) for i in range(4)]
    nat_store(nat, pl.ds(base, 4), jnp.concatenate(sums, axis=0))


def backward_inputs(r, stars, leaf_rows):
    r.wait("wq", "wk", "wv", "we")
    r.xcat[...] = stacked(halves(r.xc[...].astype(F32)))

    def tile(start, rows, total):
        dmc = nt(r.du[rows, :], r.wv[...])
        el = r.el[rows, :].astype(F32)
        hot = onehot_col(r.idc[rows, :], stars, 2)
        dm = nt(r.dk[rows, :], r.wk[...]) + nt(r.dv[rows, :], r.wv[...])
        r.gxl[rows, :] = r.dz[rows, :] + dm * el
        de = dmc * nn(hot, r.xcat[...]) + dm * r.xl[rows, :].astype(F32)
        de = de + nt(r.ge[rows, :], r.we[...])
        r.gel[rows, :] = de.astype(r.gel.dtype)
        return total + nn(onehot_row(r.idr[:, rows], stars, 1), (dmc * el).astype(BF))

    zero = jnp.zeros((stars, D), F32)
    total = r.loop(("du", "el", "dk", "dv", "xl", "ge", "dz"), ("gxl", "gel"), tile, zero)
    r.arrive("dz")
    r.gxc[...] = (
        r.dz[leaf_rows:, :]
        + nt(r.dq[...], r.wq[...])
        + nt(r.dkc[...], r.wk[...])
        + nt(r.dvc[...], r.wv[...])
        + total
    )
    r.finish("gxl", "gel")


def nat_load(nat, at):
    return jnp.concatenate([nat[c, at, :] for c in range(3)], axis=1)[:, :D]


def nat_store(nat, at, value):
    nat[0, at, :] = value[:, 0:128]
    nat[1, at, :] = value[:, 128:256]
    rest = jnp.zeros((value.shape[0], 384 - D), F32)
    nat[2, at, :] = jnp.concatenate([value[:, 256:D], rest], axis=1)


def pack_blocks(r, holders, rows):
    nat = r.nat
    lane = lax.broadcasted_iota(jnp.int32, (64, 128), 1)
    half = holders // 2
    for b in range(holders):
        top = b * rows
        at = r.slot[0, b]
        r.all_a[at, 0:128, :] = nat[0, top : top + 128, :].astype(BF)
        r.all_a[at, 128:160, :] = nat[1, top : top + 32, :].astype(BF)
        at = r.slot[1, b]
        r.all_b[at, 0:96, :] = nat[1, top + 32 : top + 128, :].astype(BF)
        high = pltpu.roll(nat[2, top + 64 : top + 128, :], 64, 1)
        tail = jnp.where(lane < 64, nat[2, top : top + 64, :], high)
        r.all_b[at, 96:160, :] = tail.astype(BF)
    for i, name in enumerate(("all_a", "all_b")):
        r.keep[i * half : (i + 1) * half] = r[name][:half]
        r.send[i * half : (i + 1) * half] = r[name][half:]


def unpack_blocks(r, holders, rows):
    nat = r.nat
    half = holders // 2

    for b in range(holders):
        top = b * rows
        slot = r.slot[0, b]
        at = jnp.where(slot >= half, slot - half, slot)
        flag = jnp.full((PACK, 128), jnp.where(slot >= half, 1.0, 0.0), F32)
        got = jnp.where(flag > 0.5, r.far[at].astype(F32), r.near[at].astype(F32))
        nat[0, top : top + rows, :] = got[:rows]
        nat[1, top : top + rows, :] = got[128 : 128 + rows]
        tail = got[256:]
        nat[2, top : top + 64, :] = tail
        nat[2, top + 64 : top + rows, :] = pltpu.roll(tail, 64, 1)[: rows - 64]
    for i, name in enumerate(WEIGHTS[:5]):
        r[name][...] = nat_load(nat, pl.ds(i * D, D)).astype(BF)
    base = 5 * D
    for j in range(FF // D):
        part = nat_load(nat, pl.ds(base + j, D, stride=FF // D))
        r.w1[:, j * D : (j + 1) * D] = part.astype(BF)
    base = base + FF
    r.w2[...] = nat_load(nat, pl.ds(base, FF)).astype(BF)
    base = base + FF
    r.norm[...] = nat_load(nat, pl.ds(base, 8))


class Bag(dict):
    def __getattr__(self, name):
        return self[name]


class Refs(Bag):
    def __init__(self, refs, leaf_rows):
        super().__init__(refs)
        self.tiles = leaf_rows // TILE
        self.coming, self.going, self.pending = {}, {}, []

    def wait(self, *names):
        for name in names:
            for copy in self.coming.pop(name, ()):
                copy.wait()

    def arrive(self, *names):
        for name in names:
            if name in self.coming:
                for copy in self.coming.pop(name)["all"]():
                    copy.wait()

    def arrive_rest(self, name):
        if name in self.coming:
            for copy in self.coming[name]["rest"]():
                copy.wait()
            every = self.coming[name]["every"]
            self.coming[name]["all"] = every
            self.coming[name]["rest"] = list

    def loop(self, names, made, body, init):
        coming = [self.coming[k] for k in names if k in self.coming and "tile" in self.coming[k]]
        going = [self.going[k] for k in made if k in self.going]

        def step(t, carry):
            start = pl.multiple_of(t * TILE, TILE)
            for k in coming:
                k["tile"](t, start).wait()
            carry = body(start, pl.ds(start, TILE), carry)
            for k in going:
                k["tile"](t, start)
            return carry

        result = lax.fori_loop(0, self.tiles, step, init)
        for k in coming:
            k["all"] = k["rest"]
            del k["tile"]
        return result

    def finish(self, *names):
        for name in names:
            if name in self.going:
                self.pending.extend(self.going.pop(name)["rest"]())


def call(body, inputs, outputs, scratch, micros, leaf_rows=TILE, lazy=(), joins=(), own=(), in_smem=(), name=None):
    joins = dict(joins)
    tiles = leaf_rows // TILE
    raw = {k for k, _ in joins.values()} | ({"halo_l", "halo_r"} if joins else set())
    lazy_in = [k for k in inputs if k in lazy] + list(joins)
    buffers = {}
    for k in lazy_in:
        source = inputs[joins[k][0]] if k in joins else inputs[k]
        rows = leaf_rows if k in joins else source.shape[0]
        buffers[k] = ((rows,) + source.shape[1:], source.dtype)
    lazy_out = [k for k in outputs if k in lazy]
    for k in lazy_out:
        shape, dtype = outputs[k]
        buffers[k] = ((leaf_rows,) + shape[1:] if k in own else shape, dtype)
    names = list(inputs) + list(outputs) + list(scratch)

    def kernel(*refs):
        outer = dict(zip(names, refs, strict=False))
        rest = refs[len(names) :]
        held = dict(zip(buffers, rest, strict=False))
        sems = rest[-1] if buffers else None
        r = Refs({**outer, **held}, leaf_rows)
        copy = pltpu.make_async_copy
        for i, k in enumerate(buffers):
            inner, total = held[k], buffers[k][0][0]
            if k in lazy_out:
                target = outer[k]
                if k in own:
                    cut = pl.ds(HALO, leaf_rows - 2 * HALO)

                    def last(inner=inner, target=target, cut=cut, i=i):
                        one = copy(inner.at[cut], target, sems.at[i, tiles])
                        one.start()
                        return [one]

                    def per_tile(t, start):
                        return None

                else:

                    def per_tile(t, start, inner=inner, target=target, i=i):
                        rows = pl.ds(start, TILE)
                        copy(inner.at[rows], target.at[rows], sems.at[i, t]).start()

                    def last(inner=inner, target=target, i=i, total=total):
                        done = [
                            copy(inner.at[pl.ds(t * TILE, TILE)], target.at[pl.ds(t * TILE, TILE)], sems.at[i, t])
                            for t in range(tiles)
                        ]
                        if total > leaf_rows:
                            rows = pl.ds(leaf_rows, total - leaf_rows)
                            done.append(copy(inner.at[rows], target.at[rows], sems.at[i, tiles]))
                            done[-1].start()
                        return done

                r.going[k] = {"tile": per_tile, "rest": last}
            elif total < leaf_rows or k in WEIGHTS:
                one = copy(outer[k], inner, sems.at[i, 0])
                one.start()
                r.coming[k] = [one]
            else:

                def wait_for(t, start, inner=inner, i=i):
                    rows = inner.at[pl.ds(start, TILE)]
                    return copy(rows, rows, sems.at[i, t])

                def behind(inner=inner, i=i, total=total):
                    if total == leaf_rows:
                        return []
                    rows = inner.at[pl.ds(leaf_rows, total - leaf_rows)]
                    return [copy(rows, rows, sems.at[i, tiles])]

                def every(wait_for=wait_for):
                    return [wait_for(t, t * TILE) for t in range(tiles)]

                def whole(every=every, behind=behind):
                    return every() + behind()

                r.coming[k] = {"tile": wait_for, "rest": behind, "every": every, "all": whole}
        for t in [tiles] + list(range(tiles)):
            for i, k in enumerate(buffers):
                if k in lazy_out or not isinstance(r.coming.get(k), dict):
                    continue
                inner, total = held[k], buffers[k][0][0]
                low, high = t * TILE, min((t + 1) * TILE, leaf_rows)
                if t == tiles:
                    high = total
                if k in joins:
                    source, place = joins[k]
                    stop = leaf_rows - HALO
                    pieces = [
                        (outer["halo_l"], place * HALO, 0, HALO),
                        (outer[source], 0, HALO, stop),
                        (outer["halo_r"], place * HALO, stop, leaf_rows),
                    ]
                else:
                    pieces = [(outer[k], 0, 0, total)]
                for ref, offset, first, stop in pieces:
                    a, b = max(first, low), min(stop, high)
                    if a < b:
                        piece = ref.at[pl.ds(a - first + offset, b - a)]
                        copy(piece, inner.at[pl.ds(a, b - a)], sems.at[i, t]).start()
        body(r)
        for k in list(r.coming):
            if isinstance(r.coming[k], dict):
                r.arrive(k)
            else:
                r.wait(k)
        r.finish(*list(r.going))
        for one in r.pending:
            one.wait()

    vmem = pl.BlockSpec(memory_space=pltpu.VMEM)
    smem = pl.BlockSpec(memory_space=pltpu.SMEM)
    anywhere = pl.BlockSpec(memory_space=pl.ANY)

    def place(k):
        return smem if k in in_smem else anywhere if k in lazy or k in raw else vmem

    results = pl.pallas_call(
        kernel,
        out_shape=[jax.ShapeDtypeStruct(s, d) for s, d in outputs.values()],
        in_specs=[place(k) for k in inputs],
        out_specs=[place(k) for k in outputs],
        scratch_shapes=[pltpu.VMEM(s, d) for s, d in scratch.values()]
        + [pltpu.VMEM(s, d) for s, d in buffers.values()]
        + ([pltpu.SemaphoreType.DMA((len(buffers), tiles + 1))] if buffers else []),
        compiler_params=pltpu.CompilerParams(vmem_limit_bytes=VMEM),
        cost_estimate=pl.CostEstimate(
            flops=int(micros * 1e9), bytes_accessed=int(micros * 1e6), transcendentals=0
        ),
        name=name,
    )(*inputs.values())
    return Bag(zip(outputs, results, strict=True))


def saved_shapes(stars, leaf_rows):
    rows = leaf_rows + stars
    return dict(
        k=((leaf_rows, D), BF),
        v=((leaf_rows, D), BF),
        ub=((leaf_rows, D), BF),
        hb=((rows, D), BF),
        xh1=((rows, D), BF),
        xh2=((rows, D), BF),
        act=((rows, FF), BF),
        slope=((rows, FF), BF),
        inv=((rows, 128), F32),
        s=((HP, leaf_rows), F32),
        qs=((stars, D), F32),
        kc=((stars, D), F32),
        vc=((stars, D), F32),
        o=((stars, D), F32),
        self=((stars, HP), F32),
        logt=((stars, HP), F32),
    )


def pair_shapes(stars, *names):
    return {k: ((2 * stars, D), BF) for k in names}


def leaf_shapes(leaf_rows, *names):
    return {k: ((leaf_rows, D), BF) for k in names}


def star_shapes(stars, *names):
    return {k: ((stars, D), BF) for k in names}


def ffn_scratch(stars, leaf_rows):
    rows = leaf_rows + stars
    return {"dn": ((4, 8, D), F32), "dbr": ((rows, D), BF), "dpre": ((rows, FF), BF)}


def exchange(x, stage, value, sizes):
    axis, shift, bits = stage
    return lax.ppermute(x, axis, [(i, i ^ (value << shift)) for i in range(sizes[axis])])


def tree_stages(sizes, swap):
    bits = {axis: size.bit_length() - 1 for axis, size in sizes.items()}

    def cut(axis, start, stop):
        return [(axis, i, min(2, stop - i)) for i in range(start, stop, 2)]

    middle = [cut("leaf", 1, bits["leaf"]), cut("graph", 0, 1)]
    if swap:
        middle = middle[::-1]
    return [("leaf", 0, 1)] + middle[0] + middle[1] + cut("graph", 1, bits["graph"])


def tree_slot(relative, stages, leaf_bits):
    slot = jnp.zeros_like(relative)
    for axis, shift, bits in stages:
        shift = shift + (leaf_bits if axis == "graph" else 0)
        slot = (slot << bits) | ((relative >> shift) & ((1 << bits) - 1))
    return slot


def gather_step(held, stage, sizes):
    parts = [held] + [exchange(held, stage, v, sizes) for v in range(1, 1 << stage[2])]
    return jnp.concatenate(parts, axis=0)


def total(held, start, stop):
    return sum(x[at + start : at + stop].astype(F32) for x, at in held[0])


def reduce_step(held, stage, sizes):
    terms, rows = held
    count = rows >> stage[2]
    sent = [total(held, v * count, (v + 1) * count).astype(BF) for v in range(1, 1 << stage[2])]
    got = [(exchange(x, stage, v + 1, sizes), 0) for v, x in enumerate(sent)]
    return terms + got, count


def tie(helds, *others):
    newest, others = lax.optimization_barrier(([h[0][-1][0] for h in helds], others))
    return [
        (terms[:-1] + [(x, terms[-1][1])], rows)
        for (terms, rows), x in zip(helds, newest, strict=True)
    ], others


def to_rows(flat, rows):
    block = jnp.pad(flat.reshape(rows, D), ((0, 128 - rows), (0, 0)))
    tail = jnp.pad(block[:, 256:], ((0, 0), (0, 320 - D)))
    return jnp.concatenate(
        [block[:, :128], block[:, 128:256], jnp.concatenate([tail[:64], tail[64:]], axis=1)], axis=0
    )


def from_rows(packed, rows):
    tail = jnp.concatenate([packed[256:, : D - 256], packed[256:, 64 : D - 192]], axis=0)
    block = jnp.concatenate([packed[:128], packed[128:256], tail], axis=1)
    return block[:rows].reshape(-1)


def split_flat(vec):
    square = D * D
    mats = [vec[i * square : (i + 1) * square].reshape(D, D) for i in range(5)]
    at = 5 * square
    w1 = vec[at : at + D * FF].reshape(D, FF)
    at = at + D * FF
    w2 = vec[at : at + FF * D].reshape(FF, D)
    at = at + FF * D
    norm = jnp.pad(vec[at : at + 4 * D].reshape(4, D).astype(F32), ((0, 4), (0, 0)))
    return Bag(zip(WEIGHTS, mats + [w1, w2, norm], strict=True))


def halo(x):
    size = lax.axis_size("leaf")
    last, first = x
    left = lax.ppermute(last, "leaf", [(i, i + 1) for i in range(size - 1)])
    right = lax.ppermute(first, "leaf", [(i + 1, i) for i in range(size - 1)])
    return left, right


def local(
    weights,
    first_moment,
    second_moment,
    centers,
    leaves,
    edge_feats,
    center_cot,
    leaf_cot,
    edge_cot,
    graph_ids,
    star_sizes,
    leaf_mask,
    owner_list,
):
    sizes = {"graph": lax.axis_size("graph"), "leaf": lax.axis_size("leaf")}
    holders = sizes["graph"] * sizes["leaf"]
    block_len = weights.shape[1]
    block_rows = block_len // D
    in_rows = block_len % D == 0 and 64 < block_rows <= 128
    stars = centers.shape[1]
    own_rows = leaves.shape[1]
    leaf_rows = own_rows + 2 * HALO

    orders = [tree_stages(sizes, swap) for swap in (False, True)]
    me = lax.axis_index(("graph", "leaf"))
    leaf_bits = sizes["leaf"].bit_length() - 1
    slot = jnp.stack([tree_slot(owner_list ^ me, stages, leaf_bits) for stages in orders])
    nat_rows = ROWS_LAYER + 12
    nat = {"nat": ((3, nat_rows, 128), F32)}
    half = PACK // 2
    n_steps = len(orders[0])
    weights_low = weights.astype(BF)

    def gather_begin(rows):
        held = gather_step(jnp.concatenate(rows, axis=0)[None], orders[0][-1], sizes)
        size = rows[0].shape[0]
        return [held[:, :size], held[:, size:]]

    def gather_more(held, n):
        return [gather_step(h, o[n], sizes) for h, o in zip(held, orders, strict=True)]

    def unpack(i, near):
        if not in_rows:
            flat = gather_step(near, orders[i][0], sizes)
            return split_flat(jnp.take(flat, slot[i], axis=0).reshape(-1))
        far = exchange(near, orders[i][0], 1, sizes)
        return call(
            lambda r: unpack_blocks(r, holders, block_rows),
            dict(slot=slot[i : i + 1], near=near, far=far),
            dict(zip(WEIGHTS, WEIGHT_SHAPES, strict=True)),
            nat,
            4,
            in_smem=("slot",),
            name="unpack",
        )

    rows = [to_rows(x, block_rows) if in_rows else x for x in weights_low]
    rows, leaves, edge_feats, leaf_cot, edge_cot, graph_ids, leaf_mask = lax.optimization_barrier(
        (rows, leaves, edge_feats, leaf_cot, edge_cot, graph_ids, leaf_mask)
    )
    held = gather_begin(rows)
    raw = dict(leaves=leaves[0], edges=edge_feats[0], lcot=leaf_cot[0], ecot=edge_cot[0])
    marks = jnp.pad((graph_ids + 1).astype(BF), ((0, 15), (0, 0)))
    marks = jnp.concatenate([marks[:8], jnp.broadcast_to(leaf_mask.astype(BF), (8, own_rows))], axis=0)

    def edge(cut):
        note = jnp.pad(marks[:, cut], ((0, 0), (0, D - HALO)))
        return jnp.concatenate([x[cut] for x in raw.values()] + [note], axis=0)

    left, right = halo((edge(slice(own_rows - HALO, own_rows)), edge(slice(0, HALO))))
    at = len(raw)
    raw, held = lax.optimization_barrier((raw, held))
    raw = dict(raw, halo_l=left, halo_r=right)

    def with_marks(line, mine):
        sides = [x[at * HALO + line, :HALO].astype(jnp.int32)[None] for x in (left, right)]
        return jnp.concatenate([sides[0], mine, sides[1]], axis=1)

    ids = with_marks(0, graph_ids + 1) - 1
    live = with_marks(8, leaf_mask).astype(F32)
    edge_id = jnp.full((1, 1), -1, jnp.int32)
    last = (ids != jnp.concatenate([ids[:, 1:], edge_id], axis=1)).astype(F32)
    first = graph_ids[0] != ids[0, HALO - 1 : HALO - 1 + own_rows]
    star_index = jnp.arange(stars, dtype=jnp.int32)
    star_own = jnp.any((star_index[:, None] == graph_ids) & first[None, :], axis=1)[:, None]
    scale = (jnp.log(star_sizes[0].astype(F32)) / (math.log(32.0) * math.sqrt(HEAD)))[:, None]
    base = Bag(
        idc=ids.reshape(-1, 1),
        idr=ids,
        live=live,
        last=last,
        scale=scale,
        cown=star_own.astype(F32),
    )
    saved = saved_shapes(stars, leaf_rows)
    rows = leaf_rows + stars
    if in_rows:
        grads_out = {k: ((holders, half, 128), BF) for k in ("keep", "send")}
        grads_scratch = {k: ((holders, half, 128), BF) for k in ("all_a", "all_b")} | nat
    else:
        grads_out, grads_scratch = nat, {}
    lazy = ("w1", "w2", "wq", "wk", "wv", "wo", "we", "xl", "el", "gyl", "ge", "yl", "en", "inv") + (
        "k", "v", "ub", "hb", "xh1", "xh2", "act", "slope", "dz", "du", "dk", "dv", "gxl", "gel", "dbr", "dpre",
    )
    f_scratch = pair_shapes(stars, "qcat", "xcat")
    a_scratch = pair_shapes(stars, "qcat", "xcat", "docat") | leaf_shapes(leaf_rows, "dal", "mc", "m")
    handed = (
        {"dz": ((rows, D), F32)}
        | leaf_shapes(leaf_rows, "du", "dk", "dv")
        | star_shapes(stars, "dq", "dkc", "dvc")
    )
    squares = ("wq", "wk", "wv", "wo", "we")

    def halves_of(*names):
        return {k: raw[k] for k in (*names, "halo_l", "halo_r")}

    join = dict(xl=("leaves", 0), el=("edges", 1), gyl=("lcot", 2), ge=("ecot", 3))

    def joined(*names):
        return {k: join[k] for k in names}

    for n in range(n_steps - 2, 0, -1):
        held = gather_more(held, n)
    params = [unpack(i, near) for i, near in enumerate(held)]
    one = call(
        lambda r: forward(r, stars, leaf_rows),
        {**{k: params[0][k] for k in squares}, **halves_of("leaves", "edges"), **base}
        | {**{k: params[0][k] for k in ("w1", "w2", "norm")}, "xc": centers[0]},
        {"yc": ((stars, D), F32), "yl": ((leaf_rows, D), F32), "en": ((leaf_rows, D), BF), **saved},
        f_scratch,
        25,
        leaf_rows,
        lazy=lazy,
        joins=joined("xl", "el"),
        name="forward",
    )
    def end_grads(r):
        backward_attention(r, stars, leaf_rows)
        weight_grads(r, stars, leaf_rows, own_rows)
        if in_rows:
            pack_blocks(r, holders, block_rows)

    def both(r):
        forward(r, stars, leaf_rows)
        backward_ffn(r, stars, leaf_rows, own_rows)
        end_grads(r)

    two_in = dict(xc=one.yc, xl=one.yl, el=one.en, **halves_of("ecot"))
    own_out = {"yl": ((own_rows, D), BF), "en": ((own_rows, D), BF)}
    two = call(
        both,
        {**{k: params[1][k] for k in squares}, **two_in, **base, "slot": slot}
        | {k: params[1][k] for k in ("w1", "w2", "norm")}
        | {"gyc": center_cot[0], **halves_of("lcot")},
        {"yc": ((stars, D), F32), **own_out, **handed, **grads_out},
        {**a_scratch, **saved, **ffn_scratch(stars, leaf_rows), **grads_scratch},
        45,
        leaf_rows,
        in_smem=("slot",),
        lazy=lazy,
        joins=joined("gyl", "ge"),
        own=("yl", "en"),
        name="last",
    )

    def inputs_of(params, given, made, joins, out_rows, dtype, name):
        return call(
            lambda r: backward_inputs(r, stars, leaf_rows),
            {
                **{k: params[k] for k in ("wv", "wk", "we", "wq")},
                **{k: base[k] for k in ("idc", "idr")},
                **given,
                **{k: made[k] for k in handed},
            },
            {"gxc": ((stars, D), F32), "gxl": ((out_rows, D), F32), "gel": ((out_rows, D), dtype)},
            pair_shapes(stars, "xcat"),
            9,
            leaf_rows,
            lazy=lazy,
            joins=joins,
            own=("gxl", "gel") if out_rows == own_rows else (),
            name=name,
        )

    def begin(made):
        if not in_rows:
            flat = jnp.swapaxes(made.nat[:, :ROWS_LAYER], 0, 1).reshape(ROWS_LAYER, 384)
            flat = flat[:, :D].reshape(holders, block_len)
            placed = jnp.zeros_like(flat).at[slot[0]].set(flat).astype(BF)
            return [reduce_step(([(placed, 0)], holders), orders[0][0], sizes)]
        got = exchange(made.send, orders[0][0], 1, sizes)
        count = holders // 2
        return [([(made.keep, i), (got, i)], count) for i in (0, count)]

    def advance(held, n):
        return [reduce_step(h, o[n], sizes) for h, o in zip(held, orders, strict=False)]

    def finish(helds):
        flat = [h for held in helds for h in held]
        rows = flat[0][1]
        both = jnp.concatenate([total(h, 0, rows) for h in flat], axis=1)
        block = total(reduce_step(([(both, 0)], rows), orders[0][-1], sizes), 0, 1)[0]
        parts = jnp.split(block, LAYERS)
        return jnp.stack([from_rows(x, block_rows) if in_rows else x for x in parts])

    held_two = begin(two)
    two_grads = inputs_of(params[1], two_in, two, joined("ge"), leaf_rows, BF, "last_inputs")
    held_two, (gyc,) = tie(held_two, two_grads.gxc)
    held_two = advance(held_two, 1)
    made = {"dz": ((rows, D), F32), **ffn_scratch(stars, leaf_rows)}
    mid = call(
        lambda r: backward_ffn(r, stars, leaf_rows, own_rows),
        {
            "w2": params[0].w2,
            "gyl": two_grads.gxl,
            **{k: one[k] for k in ("xh2", "inv", "slope")},
            "w1": params[0].w1,
            "xh1": one.xh1,
            "norm": params[0].norm,
            "cown": base.cown,
            "gyc": gyc,
        },
        made,
        {},
        13,
        leaf_rows,
        lazy=lazy,
        name="first_ffn",
    )
    held_two, (dn,) = tie(held_two, mid.dn)
    if n_steps > 2:
        held_two = advance(held_two, 2)
    ffn_names = ("xh2", "inv", "slope", "xh1")
    three = call(
        end_grads,
        {
            **{k: params[0][k] for k in ("wo", "wv")},
            **mid,
            **{k: one[k] for k in saved if k not in ffn_names},
            **halves_of("leaves", "edges"),
            **base,
            "slot": slot,
            "xc": centers[0],
            "ge": two_grads.gel,
            "dn": dn,
        },
        {**{k: handed[k] for k in handed if k != "dz"}, **grads_out},
        {**a_scratch, **grads_scratch},
        18,
        leaf_rows,
        in_smem=("slot",),
        lazy=lazy,
        joins=joined("xl", "el"),
        name="first",
    )
    three["dz"] = mid.dz
    held_three = begin(three)
    yl, en, yc, _ = lax.optimization_barrier((two.yl, two.en, two.yc, three.dq))
    held_three, (dq,) = tie(held_three, three.dq)
    handed_three = {**{k: three[k] for k in handed}, "dq": dq}
    held_three = advance(held_three, 1)
    three_in = dict(xc=centers[0], ge=two_grads.gel, **halves_of("leaves", "edges"))
    three_grads = inputs_of(
        params[0], three_in, handed_three, joined("xl", "el"), own_rows, F32, "first_inputs"
    )
    held_three, (gxc, yc) = tie(held_three, three_grads.gxc, yc)
    center_rows = jnp.where(star_own, jnp.concatenate([yc, gxc], axis=1), 0.0)
    center_rows = center_rows + exchange(center_rows, ("leaf", 0, 1), 1, sizes)
    held_three = advance(held_three, 2) if n_steps > 3 else held_three
    for n in range(3, n_steps - 1):
        held_two = advance(held_two, n)
        held_three = advance(held_three, n)
    held_three, (gxl, gel, center_rows) = tie(
        held_three, three_grads.gxl, three_grads.gel, center_rows
    )
    for bit in range(1, leaf_bits):
        center_rows = center_rows + exchange(center_rows, ("leaf", bit, 1), 1, sizes)
    centers_out, grad_centers = center_rows[:, :D].astype(BF), center_rows[:, D:]
    grad_total = finish([held_three, held_two])
    first_new = BETA_ONE * first_moment + (1.0 - BETA_ONE) * grad_total
    second_new = BETA_TWO * second_moment + (1.0 - BETA_TWO) * grad_total * grad_total
    step_one = first_new / (1.0 - BETA_ONE**STEP)
    step_two = second_new / (1.0 - BETA_TWO**STEP)
    weights_new = weights - RATE * (step_one / (jnp.sqrt(step_two) + EPS_ADAM) + DECAY * weights)
    return (
        centers_out[None],
        yl[None],
        en[None],
        grad_centers[None],
        gxl[None],
        gel[None],
        first_new,
        second_new,
        weights_new,
        weights_new.astype(BF),
        grad_total,
    )


def solution(mesh):
    both = ("graph", "leaf")
    return jax.shard_map(
        local,
        mesh=mesh,
        in_specs=(
            P(None, both),
            P(None, both),
            P(None, both),
            P("graph", None, None),
            P("graph", "leaf", None),
            P("graph", "leaf", None),
            P("graph", None, None),
            P("graph", "leaf", None),
            P("graph", "leaf", None),
            P("graph", "leaf"),
            P("graph", None),
            P("graph", "leaf"),
            P(),
        ),
        out_specs=(
            P("graph", None, None),
            P("graph", "leaf", None),
            P("graph", "leaf", None),
            P("graph", None, None),
            P("graph", "leaf", None),
            P("graph", "leaf", None),
            P(None, both),
            P(None, both),
            P(None, both),
            P(None, both),
            P(None, both),
        ),
        check_vma=False,
    )
```

```python
import math

import jax
import jax.numpy as jnp
from jax import lax
from jax.experimental import pallas as pl
from jax.experimental.pallas import tpu as pltpu
from jax.sharding import PartitionSpec as P

D = 300
HEADS = 12
HEAD = 25
FF = 1200
LAYERS = 2
STEP = 5
ROWS_LAYER = 5 * D + 2 * FF + 4

NEG = -1e30
EPS_NORM = 1e-05
BETA_ONE = 0.9
BETA_TWO = 0.999
RATE = 0.05
DECAY = 0.01
EPS_ADAM = 1e-08
INV_ROOT_TWO = 0.7071067811865476
INV_ROOT_TWO_PI = 0.3989422804014327

HALO = 128
TILE = 320
WIDE = 2
FFN_WIDE = 1
HP = 16
PACK = 320
CHUNKS = tuple((i, min(i + 256, FF)) for i in range(0, FF, 256))
VMEM = 60 << 20
F32 = jnp.float32
BF = jnp.bfloat16

STEP_COLUMNS = 384
PAIR = STEP_COLUMNS + D

WEIGHTS = ("wq", "wkv", "wo", "we", "wvo", "w1", "w2", "norm")
WEIGHT_SHAPES = (
    ((D, D), BF),
    ((D, PAIR), BF),
    ((D, D), BF),
    ((D, D), BF),
    ((D, D), BF),
    ((D, FF), BF),
    ((FF, D), BF),
    ((8, D), F32),
)


def nn(a, b):
    return lax.dot_general(a, b, (((1,), (0,)), ((), ())), preferred_element_type=F32)


def nt(a, b):
    return lax.dot_general(a, b, (((1,), (1,)), ((), ())), preferred_element_type=F32)


def tn(a, b):
    return lax.dot_general(a, b, (((0,), (0,)), ((), ())), preferred_element_type=F32)


def halves(x):
    high = x.astype(BF)
    return high, (x - high.astype(F32)).astype(BF)


def thirds(x):
    high = x.astype(BF)
    rest = x - high.astype(F32)
    mid = rest.astype(BF)
    return high, mid, (rest - mid.astype(F32)).astype(BF)


def stacked(parts, axis=0):
    return jnp.concatenate([p.astype(F32) for p in parts], axis=axis).astype(BF)


def side_by_side(*parts):
    zeros = jnp.zeros((parts[0].shape[0], STEP_COLUMNS - D), F32)
    pieces = [parts[0]]
    for part in parts[1:]:
        pieces += [zeros, part]
    return jnp.concatenate(pieces, axis=1)


def column(values, i):
    return values[:, i * STEP_COLUMNS : i * STEP_COLUMNS + D]


def table(rows, repeat=1):
    head = lax.broadcasted_iota(jnp.int32, (repeat * rows, D), 0) % rows
    feature = lax.broadcasted_iota(jnp.int32, (repeat * rows, D), 1)
    low = head * HEAD
    return jnp.where((feature >= low) & (feature < low + HEAD), 1.0, 0.0).astype(BF)


def head_sum(values):
    high, low = halves(values)
    tab = table(HP)
    return nt(high, tab) + nt(low, tab)


def head_sum_t(values):
    high, low = halves(values)
    tab = table(HP)
    return nt(tab, high) + nt(tab, low)


def spread(values):
    high, low = halves(values)
    tab = table(HP)
    return nn(high, tab) + nn(low, tab)


def spread_t(values):
    return tn(stacked(halves(values)), table(HP, 2))


def onehot_col(ids, stars, repeat):
    lane = lax.broadcasted_iota(jnp.int32, (ids.shape[0], repeat * stars), 1)
    hit = lane == ids
    for i in range(1, repeat):
        hit = hit | (lane == ids + i * stars) & (ids >= 0)
    return jnp.where(hit, 1.0, 0.0).astype(BF)


def onehot_row(ids, stars, repeat):
    sub = lax.broadcasted_iota(jnp.int32, (repeat * stars, ids.shape[1]), 0)
    hit = sub == ids
    for i in range(1, repeat):
        hit = hit | (sub == ids + i * stars) & (ids >= 0)
    return jnp.where(hit, 1.0, 0.0).astype(BF)


def row_mean(x):
    return jnp.sum(x, axis=-1, keepdims=True) * (1.0 / D)


def normalized(x):
    dev = x - row_mean(x)
    inverse = lax.rsqrt(row_mean(dev * dev) + EPS_NORM)
    return dev * inverse, inverse


def norm_back(grad, scaled, inverse):
    return inverse * (grad - row_mean(grad) - scaled * row_mean(grad * scaled))


def put_normalized(ref, rows, scaled, inverse):
    ref[rows, 0:D] = scaled.astype(BF)
    high, low = halves(inverse)
    ref[rows, D : D + 1] = high
    ref[rows, D + 1 : D + 2] = low


def get_normalized(ref, rows):
    inverse = ref[rows, D : D + 1].astype(F32) + ref[rows, D + 1 : D + 2].astype(F32)
    return ref[rows, 0:D].astype(F32), inverse


def ffn_forward(r, z, rows):
    norm = r.norm
    g1, b1, g2, b2 = (norm[i : i + 1, :] for i in range(4))
    xh1, inv1 = normalized(z)
    h = xh1 * g1 + b1
    hb = h.astype(BF)
    r.hb[rows, :] = hb
    put_normalized(r.xh1, rows, xh1, inv1)
    total = h
    for lo, hi in CHUNKS:
        pre = nn(hb, r.w1[:, lo:hi])
        cdf = 0.5 * (1.0 + lax.erf(pre * INV_ROOT_TWO))
        act = (pre * cdf).astype(BF)
        r.act[rows, lo:hi] = act
        r.slope[rows, lo:hi] = (
            cdf + pre * jnp.exp(-0.5 * pre * pre) * INV_ROOT_TWO_PI
        ).astype(BF)
        total = total + nn(act, r.w2[lo:hi, :])
    xh2, inv2 = normalized(total)
    put_normalized(r.xh2, rows, xh2, inv2)
    return xh2 * g2 + b2


def fold(x):
    return jnp.sum(x.reshape(x.shape[0] // 8, 8, x.shape[1]), axis=0)


def ffn_backward(r, gy, rows, weight):
    norm = r.norm
    g1, g2 = norm[0:1, :], norm[2:3, :]
    xh2, inv2 = get_normalized(r.xh2, rows)
    gw = gy * weight
    r.dn[2] += fold(gw * xh2)
    r.dn[3] += fold(gw)
    mid = norm_back(gy * g2, xh2, inv2)
    branch = mid.astype(BF)
    r.dbr[rows, 0:D] = (mid * weight).astype(BF)
    total = mid
    for lo, hi in CHUNKS:
        dact = nt(branch, r.w2[lo:hi, :])
        dpre = dact * r.slope[rows, lo:hi].astype(F32)
        low = dpre.astype(BF)
        r.dpre[rows, lo:hi] = (dpre * weight).astype(BF)
        total = total + nt(low, r.w1[:, lo:hi])
    xh1, inv1 = get_normalized(r.xh1, rows)
    gw = total * weight
    r.dn[0] += fold(gw * xh1)
    r.dn[1] += fold(gw)
    return norm_back(total * g1, xh1, inv1)


def forward(r, stars, leaf_rows):
    xc = r.xc[...].astype(F32)
    low = xc.astype(BF)
    r.wait("wq", "wkv", "wo", "we", "wvo")
    r.settle("kv")
    qs = nn(low, r.wq[...]) * r.scale[...]
    kvc = nn(low, r.wkv[...])
    own_score = head_sum(qs * column(kvc, 0))
    r.qs[...] = qs
    r.kvc[...] = kvc
    r.self[...] = own_score
    r.cat[:, 0:PAIR] = stacked(halves(side_by_side(qs, xc)))

    def tile(start, size, rows, carry):
        el = r.el[rows, :]
        ew = el.astype(F32)
        xl = r.xl[rows, :].astype(F32)
        r.en[rows, :] = nn(el, r.we[...]).astype(BF)
        from_star = nn(onehot_col(r.idc[rows, :], stars, 2), r.cat[:, 0:PAIR])
        kv = nn((xl * ew).astype(BF), r.wkv[...])
        r.kv[rows, :] = kv.astype(BF)
        r.s[:, rows] = head_sum_t(column(from_star, 0) * column(kv, 0))
        mc = (column(from_star, 1) * ew).astype(BF)
        r.z[rows, :] = xl + nn(mc, r.wvo[...])
        return carry

    def ffn_tile(start, size, rows, carry):
        if start == 0:
            r.wait("w1", "w2")
            r.settle(*made)
        if start + size == leaf_rows:
            r.z[leaf_rows:, :] = xc + attend(r, stars, leaf_rows, own_score, column(kvc, 1))
        y = ffn_forward(r, r.z[rows, :], rows)
        r.yl[start : start + size, :] = y[:size].astype(r.yl.dtype)
        if start + size == leaf_rows:
            r.yc[...] = y[size:]
        return carry

    made = ("yl", "hb", "xh1", "xh2", "act", "slope")
    r.loop(("xl", "el"), ("en", "kv"), tile, 0)
    r.loop((), made, ffn_tile, 0, stars, FFN_WIDE)
    r.finish("en", "kv", *made)


def attend(r, stars, leaf_rows, own_score, vc):
    ids = r.idr[...]
    live = r.live[...] > 0.5
    score = r.s[...]
    top = jnp.where(live, score, NEG)
    lane = lax.broadcasted_iota(jnp.int32, (1, leaf_rows), 1)
    shift = 1
    while shift < 128:
        same = (pltpu.roll(ids, shift, 1) == ids) & (lane >= shift)
        top = jnp.maximum(top, jnp.where(same, pltpu.roll(top, shift, 1), NEG))
        shift *= 2
    hot_row = onehot_row(ids, stars, 1)
    last = hot_row.astype(F32) * r.last[...]
    present = jnp.sum(last, axis=1, keepdims=True) > 0.5
    last = last.astype(BF)
    star_top = sum(nt(last, part) for part in thirds(top))
    peak = jnp.where(present, jnp.maximum(star_top, own_score), own_score)
    peak_row = tn(stacked(thirds(peak)), onehot_row(ids, stars, 3))
    e = jnp.where(live, jnp.exp(jnp.where(live, score - peak_row, 0.0)), 0.0)
    self_weight = jnp.exp(own_score - peak)
    total = self_weight + sum(nt(hot_row, part) for part in halves(e))
    r.logt[...] = peak + jnp.log(total)
    weighted = (spread_t(e) * column(r.kv, 1).astype(F32)).astype(BF)
    o = (nn(hot_row, weighted) + spread(self_weight) * vc) / spread(total)
    r.o[...] = o
    return nn(o.astype(BF), r.wo[...])


def backward_ffn(r, stars, leaf_rows, own_rows):
    r.dn[...] = jnp.zeros_like(r.dn)
    r.wait("w2", "w1")

    def tile(start, size, rows, carry):
        row = lax.broadcasted_iota(jnp.int32, (size, 1), 0) + start
        mine = jnp.where((row >= HALO) & (row < HALO + own_rows), 1.0, 0.0)
        gy = r.gyl[start : start + size, :].astype(F32)
        if start + size == leaf_rows:
            gy = jnp.concatenate([gy, r.gyc[...].astype(F32)], axis=0)
            mine = jnp.concatenate([mine, r.cown[...]], axis=0)
        r.dz[rows, :] = ffn_backward(r, gy, rows, mine).astype(BF)
        return carry

    made = ("dz", "dbr", "dpre")
    r.loop(("gyl", "xh2", "slope", "xh1"), made, tile, 0, stars, FFN_WIDE)
    r.finish(*made)


def backward_attention(r, stars, leaf_rows):
    r.wait("wo")
    r.arrive_rest("dz")
    do = nt(r.dz[leaf_rows:, :], r.wo[...])
    kvc = r.kvc[...]
    kc, vc = column(kvc, 0), column(kvc, 1)
    qs = r.qs[...]
    xc = r.xc[...].astype(F32)
    r.cat[...] = stacked(halves(side_by_side(qs, xc, do)))
    delta = head_sum(do * r.o[...])
    self_p = jnp.exp(r.self[...] - r.logt[...])
    d_self = self_p * (head_sum(do * vc) - delta)
    coef_c = spread(d_self)
    r.dkvc[...] = side_by_side(coef_c * qs, spread(self_p) * do).astype(BF)
    logt_parts = stacked(thirds(r.logt[...]))
    delta_parts = stacked(thirds(delta))

    def tile(start, size, rows, total):
        el = r.el[rows, :].astype(F32)
        ids_row = r.idr[:, rows]
        hot3 = onehot_row(ids_row, stars, 3)
        from_star = nn(onehot_col(r.idc[rows, :], stars, 2), r.cat[...])
        r.mc[rows, :] = (column(from_star, 1) * el).astype(BF)
        live = r.live[:, rows] > 0.5
        score = r.s[:, rows] - tn(logt_parts, hot3)
        p = jnp.where(live, jnp.exp(jnp.where(live, score, 0.0)), 0.0)
        dor = column(from_star, 2)
        kv = r.kv[rows, :]
        ds = p * (head_sum_t(dor * column(kv, 1).astype(F32)) - tn(delta_parts, hot3))
        coef = spread_t(ds)
        r.dkv[rows, :] = side_by_side(coef * column(from_star, 0), spread_t(p) * dor).astype(BF)
        r.m[rows, :] = (r.xl[rows, :].astype(F32) * el).astype(BF)
        part = (coef * column(kv, 0).astype(F32)).astype(BF)
        return total + nn(onehot_row(ids_row, stars, 1), part)

    zero = jnp.zeros((stars, D), F32)
    total = r.loop(("el", "kv", "xl", "dz"), ("dkv",), tile, zero)
    r.dq[...] = ((total + coef_c * kc) * r.scale[...]).astype(BF)
    r.finish("dkv")


def weight_grads(r, stars, leaf_rows, own_rows):
    own = r.cown[...]
    own_leaf = slice(HALO, HALO + own_rows)
    r.wait("wkv")
    r.arrive("dz", "ge", "hb", "dpre", "act", "dbr")
    nat = r.nat
    xb = r.xc[...].astype(BF)
    dq, dkvc, dac = (
        (x.astype(F32) * own).astype(BF) for x in (r.dq[...], r.dkvc[...], r.dz[leaf_rows:, :])
    )
    nat_store(nat, pl.ds(0, D), tn(xb, dq))
    pair = tn(r.m[own_leaf, :], r.dkv[own_leaf, :]) + tn(xb, dkvc)
    both = tn(r.mc[own_leaf, :], r.dz[own_leaf, :]).astype(BF)
    nat_store(nat, pl.ds(D, D), column(pair, 0))
    nat_store(nat, pl.ds(2 * D, D), column(pair, 1) + nt(both, r.wo[...]))
    out = tn(column(r.wkv, 1), both) + tn(r.o[...].astype(BF), dac)
    nat_store(nat, pl.ds(3 * D, D), out)
    nat_store(nat, pl.ds(4 * D, D), tn(r.el[own_leaf, :], r.ge[own_leaf, :]))
    base = 5 * D
    for j in range(FF // D):
        columns = slice(j * D, (j + 1) * D)
        part = tn(r.hb[HALO:, :], r.dpre[HALO:, columns])
        nat_store(nat, pl.ds(base + j, D, stride=FF // D), part)
    base = base + FF
    for lo, hi in CHUNKS:
        part = tn(r.act[HALO:, lo:hi], r.dbr[HALO:, 0:D])
        nat_store(nat, pl.ds(base + lo, hi - lo), part)
    base = base + FF
    sums = [jnp.sum(r.dn[i], axis=0, keepdims=True) for i in range(4)]
    nat_store(nat, pl.ds(base, 4), jnp.concatenate(sums, axis=0))


def backward_inputs(r, stars, leaf_rows):
    r.wait("wq", "wkv", "wvo", "we")
    xc = r.xc[...].astype(F32)
    r.xcat[...] = stacked(halves(xc))

    def tile(start, size, rows, total):
        dz = r.dz[rows, :]
        dmc = nt(dz, r.wvo[...])
        el = r.el[rows, :].astype(F32)
        hot = onehot_col(r.idc[rows, :], stars, 2)
        dm = nt(r.dkv[rows, :], r.wkv[...])
        r.gxl[rows, :] = (dz.astype(F32) + dm * el).astype(r.gxl.dtype)
        de = dmc * nn(hot, r.xcat[...]) + dm * r.xl[rows, :].astype(F32)
        de = de + nt(r.ge[rows, :], r.we[...])
        r.gel[rows, :] = de.astype(r.gel.dtype)
        return total + nn(onehot_row(r.idr[:, rows], stars, 1), (dmc * el).astype(BF))

    zero = jnp.zeros((stars, D), F32)
    total = r.loop(("dz", "el", "dkv", "xl", "ge"), ("gxl", "gel"), tile, zero)
    r.arrive("dz")
    r.gxc[...] = (
        r.dz[leaf_rows:, :].astype(F32)
        + nt(r.dq[...], r.wq[...])
        + nt(r.dkvc[...], r.wkv[...])
        + total
    )
    r.finish("gxl", "gel")


def nat_load(nat, at):
    return jnp.concatenate([nat[c, at, :] for c in range(3)], axis=1)[:, :D]


def nat_store(nat, at, value):
    nat[0, at, :] = value[:, 0:128]
    nat[1, at, :] = value[:, 128:256]
    rest = jnp.zeros((value.shape[0], 384 - D), F32)
    nat[2, at, :] = jnp.concatenate([value[:, 256:D], rest], axis=1)


def pack_blocks(r, holders, rows):
    nat = r.nat
    lane = lax.broadcasted_iota(jnp.int32, (64, 128), 1)
    half = holders // 2
    for b in range(holders):
        top = b * rows
        at = r.slot[0, b]
        r.all_a[at, 0:128, :] = nat[0, top : top + 128, :].astype(BF)
        r.all_a[at, 128:160, :] = nat[1, top : top + 32, :].astype(BF)
        at = r.slot[1, b]
        r.all_b[at, 0:96, :] = nat[1, top + 32 : top + 128, :].astype(BF)
        high = pltpu.roll(nat[2, top + 64 : top + 128, :], 64, 1)
        tail = jnp.where(lane < 64, nat[2, top : top + 64, :], high)
        r.all_b[at, 96:160, :] = tail.astype(BF)
    for i, name in enumerate(("all_a", "all_b")):
        r.keep[i * half : (i + 1) * half] = r[name][:half]
        r.send[i * half : (i + 1) * half] = r[name][half:]


def unpack_copies(r, layer, holders):
    half = holders // 2
    return [
        pltpu.make_async_copy(r[f"{k}{layer}"], r.got.at[pl.ds(i * half, half)], r.sems.at[i])
        for i, k in enumerate(("near", "far"))
    ]


def unpack_blocks(r, layer, holders, rows):
    nat = r.nat
    for copy in unpack_copies(r, layer, holders):
        copy.wait()

    for b in range(holders):
        top = b * rows
        got = r.got[r.slot[layer, b]].astype(F32)
        nat[0, top : top + rows, :] = got[:rows]
        nat[1, top : top + rows, :] = got[128 : 128 + rows]
        tail = got[256:]
        nat[2, top : top + 64, :] = tail
        nat[2, top + 64 : top + rows, :] = pltpu.roll(tail, 64, 1)[: rows - 64]
    wq, wk, wv, wo, we = (nat_load(nat, pl.ds(i * D, D)).astype(BF) for i in range(5))
    put_squares(r, wq, wk, wv, wo, we)
    base = 5 * D
    for j in range(FF // D):
        part = nat_load(nat, pl.ds(base + j, D, stride=FF // D))
        r.w1[:, j * D : (j + 1) * D] = part.astype(BF)
    base = base + FF
    r.w2[...] = nat_load(nat, pl.ds(base, FF)).astype(BF)
    base = base + FF
    r.norm[...] = nat_load(nat, pl.ds(base, 8))
    r.finish(*WEIGHTS)


def put_squares(r, wq, wk, wv, wo, we):
    r.wq[...] = wq
    r.wkv[...] = side_by_side(wk.astype(F32), wv.astype(F32)).astype(BF)
    r.wo[...] = wo
    r.we[...] = we
    r.wvo[...] = nn(wv, wo).astype(BF)


class Bag(dict):
    def __getattr__(self, name):
        return self[name]


class Refs(Bag):
    def __init__(self, refs, leaf_rows):
        super().__init__(refs)
        state = dict(tiles=leaf_rows // TILE, alias={}, coming={}, going={}, pending=[])
        self.__dict__.update(state)

    def view(self, alias):
        other = Refs({**self, **{k: self[v] for k, v in alias.items()}}, self.tiles * TILE)
        state = dict(alias=alias, coming=self.coming, going=self.going, pending=self.pending)
        other.__dict__.update(state)
        return other

    def keys_of(self, names):
        return [self.alias.get(k, k) for k in names]

    def wait(self, *names):
        for name in self.keys_of(names):
            for copy in self.coming.pop(name, ()):
                copy.wait()

    def arrive(self, *names):
        for name in self.keys_of(names):
            if name in self.coming:
                for copy in self.coming.pop(name)["all"]():
                    copy.wait()

    def arrive_rest(self, name):
        (name,) = self.keys_of([name])
        if name in self.coming:
            for copy in self.coming[name]["rest"]():
                copy.wait()
            self.coming[name]["all"] = self.coming[name]["every"]
            self.coming[name]["rest"] = list

    def loop(self, names, made, body, carry, more=0, group=WIDE):
        coming = [self.coming[k] for k in self.keys_of(names) if "tile" in self.coming.get(k, ())]
        going = [self.going[k] for k in self.keys_of(made) if k in self.going]
        for first in range(0, self.tiles, group):
            stop = min(first + group, self.tiles)
            extra = more if stop == self.tiles else 0
            for k in coming:
                for t in range(first, stop):
                    k["tile"](t, t * TILE).wait()
            if extra:
                for name in names:
                    self.arrive_rest(name)
            start, size = first * TILE, (stop - first) * TILE
            carry = body(start, size, pl.ds(start, size + extra), carry)
            for t in range(first, stop):
                for k in going:
                    k["tile"](t, t * TILE)
        for k in coming:
            k["all"] = k["rest"]
            del k["tile"]
        return carry

    def finish(self, *names):
        for name in self.keys_of(names):
            if name in self.going:
                self.pending += [(name, copy) for copy in self.going.pop(name)["rest"]()]

    def settle(self, *names):
        for name, copy in self.pending:
            if name in names:
                copy.wait()
        self.pending[:] = [x for x in self.pending if x[0] not in names]


def call(body, inputs, outputs, scratch, micros, leaf_rows=TILE, lazy=(), joins=(), own=(), in_smem=(), name=None, loose=(), early=None):
    joins = dict(joins)
    tiles = leaf_rows // TILE
    raw = {k for k, _ in joins.values()} | ({"halo_l", "halo_r"} if joins else set())
    raw |= set(loose)
    lazy_in = [k for k in inputs if k in lazy and k not in raw] + list(joins)
    buffers = {}
    for k in lazy_in:
        source = inputs[joins[k][0]] if k in joins else inputs[k]
        rows = leaf_rows if k in joins else source.shape[0]
        buffers[k] = ((rows,) + source.shape[1:], source.dtype)
    lazy_out = [k for k in outputs if k in lazy]
    for k in lazy_out:
        shape, dtype = outputs[k]
        buffers[k] = ((leaf_rows,) + shape[1:] if k in own else shape, dtype)
    names = list(inputs) + list(outputs) + list(scratch)

    def kernel(*refs):
        outer = dict(zip(names, refs, strict=False))
        rest = refs[len(names) :]
        held = dict(zip(buffers, rest, strict=False))
        sems = rest[-1] if buffers else None
        r = Refs({**outer, **held}, leaf_rows)
        copy = pltpu.make_async_copy
        if early is not None:
            early(r)
        for i, k in enumerate(buffers):
            inner, total = held[k], buffers[k][0][0]
            if k in lazy_out:
                target = outer[k]
                if k in own or total < leaf_rows:
                    cut = pl.ds(HALO, leaf_rows - 2 * HALO) if k in own else pl.ds(0, total)

                    def last(inner=inner, target=target, cut=cut, i=i):
                        one = copy(inner.at[cut], target, sems.at[i, tiles])
                        one.start()
                        return [one]

                    def per_tile(t, start):
                        return None

                else:

                    def per_tile(t, start, inner=inner, target=target, i=i):
                        rows = pl.ds(start, TILE)
                        copy(inner.at[rows], target.at[rows], sems.at[i, t]).start()

                    def last(inner=inner, target=target, i=i, total=total):
                        done = [
                            copy(inner.at[pl.ds(t * TILE, TILE)], target.at[pl.ds(t * TILE, TILE)], sems.at[i, t])
                            for t in range(tiles)
                        ]
                        if total > leaf_rows:
                            rows = pl.ds(leaf_rows, total - leaf_rows)
                            done.append(copy(inner.at[rows], target.at[rows], sems.at[i, tiles]))
                            done[-1].start()
                        return done

                r.going[k] = {"tile": per_tile, "rest": last}
            elif total < leaf_rows or k in WEIGHTS or k[:-1] in WEIGHTS:
                one = copy(outer[k], inner, sems.at[i, 0])
                one.start()
                r.coming[k] = [one]
            else:

                def wait_for(t, start, inner=inner, i=i):
                    rows = inner.at[pl.ds(start, TILE)]
                    return copy(rows, rows, sems.at[i, t])

                def behind(inner=inner, i=i, total=total):
                    if total == leaf_rows:
                        return []
                    rows = inner.at[pl.ds(leaf_rows, total - leaf_rows)]
                    return [copy(rows, rows, sems.at[i, tiles])]

                def every(wait_for=wait_for):
                    return [wait_for(t, t * TILE) for t in range(tiles)]

                def whole(every=every, behind=behind):
                    return every() + behind()

                r.coming[k] = {"tile": wait_for, "rest": behind, "every": every, "all": whole}
        for t in [tiles] + list(range(tiles)):
            for i, k in enumerate(buffers):
                if k in lazy_out or not isinstance(r.coming.get(k), dict):
                    continue
                inner, total = held[k], buffers[k][0][0]
                low, high = t * TILE, min((t + 1) * TILE, leaf_rows)
                if t == tiles:
                    high = total
                if k in joins:
                    source, place = joins[k]
                    stop = leaf_rows - HALO
                    pieces = [
                        (outer["halo_l"], place * HALO, 0, HALO),
                        (outer[source], 0, HALO, stop),
                        (outer["halo_r"], place * HALO, stop, leaf_rows),
                    ]
                else:
                    pieces = [(outer[k], 0, 0, total)]
                for ref, offset, first, stop in pieces:
                    a, b = max(first, low), min(stop, high)
                    if a < b:
                        piece = ref.at[pl.ds(a - first + offset, b - a)]
                        copy(piece, inner.at[pl.ds(a, b - a)], sems.at[i, t]).start()
        body(r)
        for k in list(r.coming):
            if isinstance(r.coming[k], dict):
                r.arrive(k)
            else:
                r.wait(k)
        r.finish(*list(r.going))
        for _, one in r.pending:
            one.wait()

    vmem = pl.BlockSpec(memory_space=pltpu.VMEM)
    smem = pl.BlockSpec(memory_space=pltpu.SMEM)
    anywhere = pl.BlockSpec(memory_space=pl.ANY)

    def place(k):
        return smem if k in in_smem else anywhere if k in lazy or k in raw else vmem

    results = pl.pallas_call(
        kernel,
        out_shape=[jax.ShapeDtypeStruct(s, d) for s, d in outputs.values()],
        in_specs=[place(k) for k in inputs],
        out_specs=[place(k) for k in outputs],
        scratch_shapes=[
            pltpu.SemaphoreType.DMA(s) if d is None else pltpu.VMEM(s, d) for s, d in scratch.values()
        ]
        + [pltpu.VMEM(s, d) for s, d in buffers.values()]
        + ([pltpu.SemaphoreType.DMA((len(buffers), tiles + 1))] if buffers else []),
        compiler_params=pltpu.CompilerParams(vmem_limit_bytes=VMEM),
        cost_estimate=pl.CostEstimate(
            flops=int(micros * 1e9), bytes_accessed=int(micros * 1e6), transcendentals=0
        ),
        name=name,
    )(*inputs.values())
    return Bag(zip(outputs, results, strict=True))


def saved_shapes(stars, leaf_rows):
    rows = leaf_rows + stars
    return dict(
        kv=((leaf_rows, PAIR), BF),
        hb=((rows, D), BF),
        xh1=((rows, STEP_COLUMNS), BF),
        xh2=((rows, STEP_COLUMNS), BF),
        act=((rows, FF), BF),
        slope=((rows, FF), BF),
        s=((HP, leaf_rows), F32),
        qs=((stars, D), F32),
        kvc=((stars, PAIR), F32),
        o=((stars, D), F32),
        self=((stars, HP), F32),
        logt=((stars, HP), F32),
    )


def leaf_shapes(leaf_rows, *names):
    return {k: ((leaf_rows, D), BF) for k in names}


def ffn_scratch(stars, leaf_rows):
    rows = leaf_rows + stars
    return {"dn": ((4, 8, D), F32), "dbr": ((rows, STEP_COLUMNS), BF), "dpre": ((rows, FF), BF)}


def exchange(x, stage, value, sizes):
    axis, shift, bits = stage
    return lax.ppermute(x, axis, [(i, i ^ (value << shift)) for i in range(sizes[axis])])


def tree_stages(sizes, swap):
    bits = {axis: size.bit_length() - 1 for axis, size in sizes.items()}

    def cut(axis, start, stop):
        return [(axis, i, min(2, stop - i)) for i in range(start, stop, 2)]

    middle = [cut("leaf", 1, bits["leaf"]), cut("graph", 0, 1)]
    if swap:
        middle = middle[::-1]
    return [("leaf", 0, 1)] + middle[0] + middle[1] + cut("graph", 1, bits["graph"])


def tree_slot(relative, stages, leaf_bits):
    slot = jnp.zeros_like(relative)
    for axis, shift, bits in stages:
        shift = shift + (leaf_bits if axis == "graph" else 0)
        slot = (slot << bits) | ((relative >> shift) & ((1 << bits) - 1))
    return slot


def gather_step(held, stage, sizes):
    parts = [held] + [exchange(held, stage, v, sizes) for v in range(1, 1 << stage[2])]
    return jnp.concatenate(parts, axis=0)


def total(held, start, stop):
    return sum(x[at + start : at + stop].astype(F32) for x, at in held[0])


def reduce_step(held, stage, sizes):
    terms, rows = held
    count = rows >> stage[2]
    sent = [total(held, v * count, (v + 1) * count).astype(BF) for v in range(1, 1 << stage[2])]
    got = [(exchange(x, stage, v + 1, sizes), 0) for v, x in enumerate(sent)]
    return terms + got, count


def tie(helds, *others):
    newest, others = lax.optimization_barrier(([h[0][-1][0] for h in helds], others))
    return [
        (terms[:-1] + [(x, terms[-1][1])], rows)
        for (terms, rows), x in zip(helds, newest, strict=True)
    ], others


def to_rows(flat, rows):
    block = jnp.pad(flat.reshape(rows, D), ((0, 128 - rows), (0, 0)))
    tail = jnp.pad(block[:, 256:], ((0, 0), (0, 320 - D)))
    return jnp.concatenate(
        [block[:, :128], block[:, 128:256], jnp.concatenate([tail[:64], tail[64:]], axis=1)], axis=0
    )


def from_rows(packed, rows):
    tail = jnp.concatenate([packed[256:, : D - 256], packed[256:, 64 : D - 192]], axis=0)
    block = jnp.concatenate([packed[:128], packed[128:256], tail], axis=1)
    return block[:rows].reshape(-1)


def split_flat(vec):
    square = D * D
    wq, wk, wv, wo, we = (vec[i * square : (i + 1) * square].reshape(D, D) for i in range(5))
    at = 5 * square
    w1 = vec[at : at + D * FF].reshape(D, FF)
    at = at + D * FF
    w2 = vec[at : at + FF * D].reshape(FF, D)
    at = at + FF * D
    norm = jnp.pad(vec[at : at + 4 * D].reshape(4, D).astype(F32), ((0, 4), (0, 0)))
    wkv = jnp.concatenate([wk, jnp.zeros((D, STEP_COLUMNS - D), BF), wv], axis=1)
    return Bag(zip(WEIGHTS, (wq, wkv, wo, we, nn(wv, wo).astype(BF), w1, w2, norm), strict=True))


def halo(x):
    size = lax.axis_size("leaf")
    last, first = x
    left = lax.ppermute(last, "leaf", [(i, i + 1) for i in range(size - 1)])
    right = lax.ppermute(first, "leaf", [(i + 1, i) for i in range(size - 1)])
    return left, right


def local(
    weights,
    first_moment,
    second_moment,
    centers,
    leaves,
    edge_feats,
    center_cot,
    leaf_cot,
    edge_cot,
    graph_ids,
    star_sizes,
    leaf_mask,
    owner_list,
):
    sizes = {"graph": lax.axis_size("graph"), "leaf": lax.axis_size("leaf")}
    holders = sizes["graph"] * sizes["leaf"]
    block_len = weights.shape[1]
    block_rows = block_len // D
    in_rows = block_len % D == 0 and 64 < block_rows <= 128
    stars = centers.shape[1]
    own_rows = leaves.shape[1]
    leaf_rows = own_rows + 2 * HALO

    orders = [tree_stages(sizes, swap) for swap in (False, True)]
    me = lax.axis_index(("graph", "leaf"))
    leaf_bits = sizes["leaf"].bit_length() - 1
    slot = jnp.stack([tree_slot(owner_list ^ me, stages, leaf_bits) for stages in orders])
    nat_rows = ROWS_LAYER + 12
    nat = {"nat": ((3, nat_rows, 128), F32)}
    half = PACK // 2
    n_steps = len(orders[0])
    weights_low = weights.astype(BF)

    def gather_begin(rows):
        held = gather_step(jnp.concatenate(rows, axis=0)[None], orders[0][-1], sizes)
        size = rows[0].shape[0]
        return [held[:, :size], held[:, size:]]

    def gather_more(held, n):
        return [gather_step(h, o[n], sizes) for h, o in zip(held, orders, strict=True)]

    rows = [to_rows(x, block_rows) if in_rows else x for x in weights_low]
    rows, leaves, edge_feats, leaf_cot, edge_cot, graph_ids, leaf_mask = lax.optimization_barrier(
        (rows, leaves, edge_feats, leaf_cot, edge_cot, graph_ids, leaf_mask)
    )
    held = gather_begin(rows)
    raw = dict(leaves=leaves[0], edges=edge_feats[0], lcot=leaf_cot[0], ecot=edge_cot[0])
    marks = jnp.pad((graph_ids + 1).astype(BF), ((0, 15), (0, 0)))
    marks = jnp.concatenate([marks[:8], jnp.broadcast_to(leaf_mask.astype(BF), (8, own_rows))], axis=0)

    def edge(cut):
        note = jnp.pad(marks[:, cut], ((0, 0), (0, D - HALO)))
        return jnp.concatenate([x[cut] for x in raw.values()] + [note], axis=0)

    left, right = halo((edge(slice(own_rows - HALO, own_rows)), edge(slice(0, HALO))))
    at = len(raw)
    raw, held = lax.optimization_barrier((raw, held))
    raw = dict(raw, halo_l=left, halo_r=right)

    def with_marks(line, mine):
        sides = [x[at * HALO + line, :HALO].astype(jnp.int32)[None] for x in (left, right)]
        return jnp.concatenate([sides[0], mine, sides[1]], axis=1)

    ids = with_marks(0, graph_ids + 1) - 1
    live = with_marks(8, leaf_mask).astype(F32)
    edge_id = jnp.full((1, 1), -1, jnp.int32)
    last = (ids != jnp.concatenate([ids[:, 1:], edge_id], axis=1)).astype(F32)
    first = graph_ids[0] != ids[0, HALO - 1 : HALO - 1 + own_rows]
    star_index = jnp.arange(stars, dtype=jnp.int32)
    star_own = jnp.any((star_index[:, None] == graph_ids) & first[None, :], axis=1)[:, None]
    scale = (jnp.log(star_sizes[0].astype(F32)) / (math.log(32.0) * math.sqrt(HEAD)))[:, None]
    base = Bag(
        idc=ids.reshape(-1, 1),
        idr=ids,
        live=live,
        last=last,
        scale=scale,
        cown=star_own.astype(F32),
    )
    saved = saved_shapes(stars, leaf_rows)
    rows = leaf_rows + stars
    if in_rows:
        grads_out = {k: ((holders, half, 128), BF) for k in ("keep", "send")}
        grads_scratch = {k: ((holders, half, 128), BF) for k in ("all_a", "all_b")} | nat
    else:
        grads_out, grads_scratch = nat, {}
    lazy = WEIGHTS[:-1] + tuple(f"{k}{i}" for k in WEIGHTS for i in range(LAYERS)) + ("yl0", "en0", "xl", "el", "gyl", "ge", "yl", "en") + (
        "kv", "hb", "xh1", "xh2", "act", "slope", "dz", "dkv", "gxl", "gel", "dbr", "dpre",
    )
    f_scratch = dict(cat=((2 * stars, PAIR), BF), z=((rows, D), F32))
    a_scratch = {"cat": ((2 * stars, PAIR + STEP_COLUMNS), BF), **leaf_shapes(leaf_rows, "mc", "m")}
    handed = dict(
        dz=((rows, D), BF),
        dkv=((leaf_rows, PAIR), BF),
        dq=((stars, D), BF),
        dkvc=((stars, PAIR), BF),
    )
    def halves_of(*names):
        return {k: raw[k] for k in (*names, "halo_l", "halo_r")}

    join = dict(xl=("leaves", 0), el=("edges", 1), gyl=("lcot", 2), ge=("ecot", 3))

    def joined(*names):
        return {k: join[k] for k in names}

    for n in range(n_steps - 2, 0, -1):
        held = gather_more(held, n)

    def end_grads(r):
        backward_attention(r, stars, leaf_rows)
        weight_grads(r, stars, leaf_rows, own_rows)
        if in_rows:
            pack_blocks(r, holders, block_rows)

    small = [k for k in saved if k not in lazy]

    def start_first(r):
        for copy in unpack_copies(r, 0, holders):
            copy.start()

    def front(r):
        zero = r.view({**{k: k + "0" for k in WEIGHTS}, "yl": "yl0", "en": "en0", "yc": "yc0"})
        names = {**{k: k + "1" for k in (*WEIGHTS, *small)}, "xl": "yl0", "el": "en0", "xc": "yc0"}
        one = r.view(names)
        one.update(dpre=r.slope, dbr=r.xh2)
        if in_rows:
            unpack_blocks(zero, 0, holders, block_rows)
            for copy in unpack_copies(r, 1, holders):
                copy.start()
        forward(zero, stars, leaf_rows)
        if in_rows:
            unpack_blocks(one, 1, holders, block_rows)
            one.update(all_a=r.got.at[:, : PACK // 2], all_b=r.got.at[:, PACK // 2 :])
        forward(one, stars, leaf_rows)
        backward_ffn(one, stars, leaf_rows, own_rows)
        end_grads(one)

    weight_specs = dict(zip(WEIGHTS, WEIGHT_SHAPES, strict=True))
    params, unpacked, kept, loose = [], {}, {}, {}
    for i, near in enumerate(held):
        far = exchange(near, orders[i][0], 1, sizes)
        if in_rows:
            loose.update({f"near{i}": near, f"far{i}": far})
            used = WEIGHTS if i == 0 else ("wq", "wkv", "we", "wvo")
            unpacked.update({f"{k}{i}": weight_specs[k] for k in used})
            kept.update({f"{k}{i}": weight_specs[k] for k in WEIGHTS if k not in used})
        else:
            flat = jnp.concatenate([near, far], axis=0)
            params.append(split_flat(jnp.take(flat, slot[i], axis=0).reshape(-1)))
    if in_rows:
        kept.update(got=((holders, PACK, 128), BF), sems=((2,), None))
        kept.update(nat)
    scratch = {**f_scratch, **a_scratch, "dn": ((4, 8, D), F32), **kept, **{k + "1": saved[k] for k in small}}
    scratch["z"] = ((rows, D), F32)
    two = call(
        front,
        {
            "slot": slot,
            **loose,
            **{f"{k}{i}": x[k] for i, x in enumerate(params) for k in WEIGHTS},
            **halves_of("leaves", "edges", "lcot", "ecot"),
            **base,
            "xc": centers[0],
            "gyc": center_cot[0],
        },
        {
            "yc0": ((stars, D), F32),
            "yc": ((stars, D), F32),
            **leaf_shapes(leaf_rows, "yl0", "en0"),
            **leaf_shapes(own_rows, "yl", "en"),
            **unpacked,
            **saved,
            **handed,
            **grads_out,
        },
        scratch,
        60,
        leaf_rows,
        in_smem=("slot",),
        lazy=lazy,
        joins=joined("xl", "el", "gyl", "ge"),
        own=("yl", "en"),
        name="front",
        loose=loose,
        early=start_first if in_rows else None,
    )
    one = two
    if in_rows:
        params = [Bag({k[:-1]: two[k] for k in unpacked if k[-1] == str(i)}) for i in range(LAYERS)]
    two_in = dict(xc=two.yc0, xl=two.yl0, el=two.en0, **halves_of("ecot"))

    def inputs_of(params, given, made, joins, out_rows, dtype, name):
        return call(
            lambda r: backward_inputs(r, stars, leaf_rows),
            {
                **{k: params[k] for k in ("wvo", "wkv", "we", "wq")},
                **{k: base[k] for k in ("idc", "idr")},
                **given,
                **{k: made[k] for k in handed},
            },
            {"gxc": ((stars, D), F32), "gxl": ((out_rows, D), dtype), "gel": ((out_rows, D), dtype)},
            {"xcat": ((2 * stars, D), BF)},
            9,
            leaf_rows,
            lazy=lazy,
            joins=joins,
            own=("gxl", "gel") if out_rows == own_rows else (),
            name=name,
        )

    def begin(made):
        if not in_rows:
            flat = jnp.swapaxes(made.nat[:, :ROWS_LAYER], 0, 1).reshape(ROWS_LAYER, 384)
            flat = flat[:, :D].reshape(holders, block_len)
            placed = jnp.zeros_like(flat).at[slot[0]].set(flat).astype(BF)
            return [reduce_step(([(placed, 0)], holders), orders[0][0], sizes)]
        got = exchange(made.send, orders[0][0], 1, sizes)
        count = holders // 2
        return [([(made.keep, i), (got, i)], count) for i in (0, count)]

    def advance(held, n):
        return [reduce_step(h, o[n], sizes) for h, o in zip(held, orders, strict=False)]

    def finish(helds):
        flat = [h for held in helds for h in held]
        rows = flat[0][1]
        both = jnp.concatenate([total(h, 0, rows) for h in flat], axis=1)
        block = total(reduce_step(([(both, 0)], rows), orders[0][-1], sizes), 0, 1)[0]
        parts = jnp.split(block, LAYERS)
        return jnp.stack([from_rows(x, block_rows) if in_rows else x for x in parts])

    held_two = begin(two)
    two_grads = inputs_of(params[1], two_in, two, joined("ge"), leaf_rows, BF, "last_inputs")
    held_two, (gyc,) = tie(held_two, two_grads.gxc)
    held_two = advance(held_two, 1)
    made = {"dz": handed["dz"], **ffn_scratch(stars, leaf_rows)}
    mid = call(
        lambda r: backward_ffn(r, stars, leaf_rows, own_rows),
        {
            "w2": params[0].w2,
            "gyl": two_grads.gxl,
            **{k: one[k] for k in ("xh2", "slope")},
            "w1": params[0].w1,
            "xh1": one.xh1,
            "norm": params[0].norm,
            "cown": base.cown,
            "gyc": gyc,
        },
        made,
        {},
        13,
        leaf_rows,
        lazy=lazy,
        name="first_ffn",
    )
    held_two, (dn,) = tie(held_two, mid.dn)
    if n_steps > 2:
        held_two = advance(held_two, 2)
    ffn_names = ("xh2", "slope", "xh1")
    three = call(
        end_grads,
        {
            **{k: params[0][k] for k in ("wo", "wkv")},
            **mid,
            **{k: one[k] for k in saved if k not in ffn_names},
            **halves_of("leaves", "edges"),
            **base,
            "slot": slot,
            "xc": centers[0],
            "ge": two_grads.gel,
            "dn": dn,
        },
        {**{k: handed[k] for k in handed if k != "dz"}, **grads_out},
        {**a_scratch, **grads_scratch},
        18,
        leaf_rows,
        in_smem=("slot",),
        lazy=lazy,
        joins=joined("xl", "el"),
        name="first",
    )
    three["dz"] = mid.dz
    held_three = begin(three)
    yl, en, yc, _ = lax.optimization_barrier((two.yl, two.en, two.yc, three.dq))
    held_three, (dq,) = tie(held_three, three.dq)
    handed_three = {**{k: three[k] for k in handed}, "dq": dq}
    held_three = advance(held_three, 1)
    three_in = dict(xc=centers[0], ge=two_grads.gel, **halves_of("leaves", "edges"))
    three_grads = inputs_of(
        params[0], three_in, handed_three, joined("xl", "el"), own_rows, F32, "first_inputs"
    )
    held_three, (gxc, yc) = tie(held_three, three_grads.gxc, yc)
    center_rows = jnp.where(star_own, jnp.concatenate([yc, gxc], axis=1), 0.0)
    center_rows = center_rows + exchange(center_rows, ("leaf", 0, 1), 1, sizes)
    held_three = advance(held_three, 2) if n_steps > 3 else held_three
    for n in range(3, n_steps - 1):
        held_two = advance(held_two, n)
        held_three = advance(held_three, n)
    held_three, (gxl, gel, center_rows) = tie(
        held_three, three_grads.gxl, three_grads.gel, center_rows
    )
    for bit in range(1, leaf_bits):
        center_rows = center_rows + exchange(center_rows, ("leaf", bit, 1), 1, sizes)
    centers_out, grad_centers = center_rows[:, :D].astype(BF), center_rows[:, D:]
    grad_total = finish([held_three, held_two])
    first_new = BETA_ONE * first_moment + (1.0 - BETA_ONE) * grad_total
    second_new = BETA_TWO * second_moment + (1.0 - BETA_TWO) * grad_total * grad_total
    step_one = first_new / (1.0 - BETA_ONE**STEP)
    step_two = second_new / (1.0 - BETA_TWO**STEP)
    weights_new = weights - RATE * (step_one / (jnp.sqrt(step_two) + EPS_ADAM) + DECAY * weights)
    return (
        centers_out[None],
        yl[None],
        en[None],
        grad_centers[None],
        gxl[None],
        gel[None],
        first_new,
        second_new,
        weights_new,
        weights_new.astype(BF),
        grad_total,
    )


def solution(mesh):
    both = ("graph", "leaf")
    return jax.shard_map(
        local,
        mesh=mesh,
        in_specs=(
            P(None, both),
            P(None, both),
            P(None, both),
            P("graph", None, None),
            P("graph", "leaf", None),
            P("graph", "leaf", None),
            P("graph", None, None),
            P("graph", "leaf", None),
            P("graph", "leaf", None),
            P("graph", "leaf"),
            P("graph", None),
            P("graph", "leaf"),
            P(),
        ),
        out_specs=(
            P("graph", None, None),
            P("graph", "leaf", None),
            P("graph", "leaf", None),
            P("graph", None, None),
            P("graph", "leaf", None),
            P("graph", "leaf", None),
            P(None, both),
            P(None, both),
            P(None, both),
            P(None, both),
            P(None, both),
        ),
        check_vma=False,
    )
```

```python
import math

import jax
import jax.numpy as jnp
from jax import lax
from jax.experimental import pallas as pl
from jax.experimental.pallas import tpu as pltpu
from jax.sharding import PartitionSpec as P

D = 300
HEADS = 12
HEAD = 25
FF = 1200
LAYERS = 2
STEP = 5
ROWS_LAYER = 5 * D + 2 * FF + 4

NEG = -1e30
EPS_NORM = 1e-05
BETA_ONE = 0.9
BETA_TWO = 0.999
RATE = 0.05
DECAY = 0.01
EPS_ADAM = 1e-08
INV_ROOT_TWO = 0.7071067811865476
INV_ROOT_TWO_PI = 0.3989422804014327

HALO = 128
TILE = 320
WIDE = 2
FFN_WIDE = 1
HP = 16
PACK = 320
CHUNKS = tuple((i, min(i + 256, FF)) for i in range(0, FF, 256))
VMEM = 60 << 20
F32 = jnp.float32
BF = jnp.bfloat16

STEP_COLUMNS = 384
PAIR = STEP_COLUMNS + D

WEIGHTS = ("wq", "wkv", "wo", "we", "wvo", "w1", "w2", "norm")
WEIGHT_SHAPES = (
    ((D, D), BF),
    ((D, PAIR), BF),
    ((D, D), BF),
    ((D, D), BF),
    ((D, D), BF),
    ((D, FF), BF),
    ((FF, D), BF),
    ((8, D), F32),
)


def nn(a, b):
    return lax.dot_general(a, b, (((1,), (0,)), ((), ())), preferred_element_type=F32)


def nt(a, b):
    return lax.dot_general(a, b, (((1,), (1,)), ((), ())), preferred_element_type=F32)


def tn(a, b):
    return lax.dot_general(a, b, (((0,), (0,)), ((), ())), preferred_element_type=F32)


def halves(x):
    high = x.astype(BF)
    return high, (x - high.astype(F32)).astype(BF)


def thirds(x):
    high = x.astype(BF)
    rest = x - high.astype(F32)
    mid = rest.astype(BF)
    return high, mid, (rest - mid.astype(F32)).astype(BF)


def stacked(parts, axis=0):
    return jnp.concatenate([p.astype(F32) for p in parts], axis=axis).astype(BF)


def side_by_side(*parts):
    zeros = jnp.zeros((parts[0].shape[0], STEP_COLUMNS - D), F32)
    pieces = [parts[0]]
    for part in parts[1:]:
        pieces += [zeros, part]
    return jnp.concatenate(pieces, axis=1)


def column(values, i):
    return values[:, i * STEP_COLUMNS : i * STEP_COLUMNS + D]


def table(rows, repeat=1):
    head = lax.broadcasted_iota(jnp.int32, (repeat * rows, D), 0) % rows
    feature = lax.broadcasted_iota(jnp.int32, (repeat * rows, D), 1)
    low = head * HEAD
    return jnp.where((feature >= low) & (feature < low + HEAD), 1.0, 0.0).astype(BF)


def head_sum(values):
    high, low = halves(values)
    tab = table(HP)
    return nt(high, tab) + nt(low, tab)


def head_sum_t(values):
    high, low = halves(values)
    tab = table(HP)
    return nt(tab, high) + nt(tab, low)


def spread(values):
    high, low = halves(values)
    tab = table(HP)
    return nn(high, tab) + nn(low, tab)


def spread_t(values):
    return tn(stacked(halves(values)), table(HP, 2))


def onehot_col(ids, stars, repeat):
    lane = lax.broadcasted_iota(jnp.int32, (ids.shape[0], repeat * stars), 1)
    hit = lane == ids
    for i in range(1, repeat):
        hit = hit | (lane == ids + i * stars) & (ids >= 0)
    return jnp.where(hit, 1.0, 0.0).astype(BF)


def onehot_row(ids, stars, repeat):
    sub = lax.broadcasted_iota(jnp.int32, (repeat * stars, ids.shape[1]), 0)
    hit = sub == ids
    for i in range(1, repeat):
        hit = hit | (sub == ids + i * stars) & (ids >= 0)
    return jnp.where(hit, 1.0, 0.0).astype(BF)


def row_mean(x):
    return jnp.sum(x, axis=-1, keepdims=True) * (1.0 / D)


def normalized(x):
    dev = x - row_mean(x)
    inverse = lax.rsqrt(row_mean(dev * dev) + EPS_NORM)
    return dev * inverse, inverse


def norm_back(grad, scaled, inverse):
    return inverse * (grad - row_mean(grad) - scaled * row_mean(grad * scaled))


def put_normalized(ref, rows, scaled, inverse):
    ref[rows, 0:D] = scaled.astype(BF)
    high, low = halves(inverse)
    ref[rows, D : D + 1] = high
    ref[rows, D + 1 : D + 2] = low


def get_normalized(ref, rows):
    inverse = ref[rows, D : D + 1].astype(F32) + ref[rows, D + 1 : D + 2].astype(F32)
    return ref[rows, 0:D].astype(F32), inverse


def ffn_forward(r, z, rows):
    norm = r.norm
    g1, b1, g2, b2 = (norm[i : i + 1, :] for i in range(4))
    xh1, inv1 = normalized(z)
    h = xh1 * g1 + b1
    hb = h.astype(BF)
    r.hb[rows, :] = hb
    put_normalized(r.xh1, rows, xh1, inv1)
    total = h
    for lo, hi in CHUNKS:
        pre = nn(hb, r.w1[:, lo:hi])
        cdf = 0.5 * (1.0 + lax.erf(pre * INV_ROOT_TWO))
        act = (pre * cdf).astype(BF)
        r.act[rows, lo:hi] = act
        r.slope[rows, lo:hi] = (
            cdf + pre * jnp.exp(-0.5 * pre * pre) * INV_ROOT_TWO_PI
        ).astype(BF)
        total = total + nn(act, r.w2[lo:hi, :])
    xh2, inv2 = normalized(total)
    put_normalized(r.xh2, rows, xh2, inv2)
    return xh2 * g2 + b2


def fold(x):
    return jnp.sum(x.reshape(x.shape[0] // 8, 8, x.shape[1]), axis=0)


def ffn_backward(r, gy, rows, weight):
    norm = r.norm
    g1, g2 = norm[0:1, :], norm[2:3, :]
    xh2, inv2 = get_normalized(r.xh2, rows)
    gw = gy * weight
    r.dn[2] += fold(gw * xh2)
    r.dn[3] += fold(gw)
    mid = norm_back(gy * g2, xh2, inv2)
    branch = mid.astype(BF)
    r.dbr[rows, 0:D] = (mid * weight).astype(BF)
    total = mid
    for lo, hi in CHUNKS:
        dact = nt(branch, r.w2[lo:hi, :])
        dpre = dact * r.slope[rows, lo:hi].astype(F32)
        low = dpre.astype(BF)
        r.dpre[rows, lo:hi] = (dpre * weight).astype(BF)
        total = total + nt(low, r.w1[:, lo:hi])
    xh1, inv1 = get_normalized(r.xh1, rows)
    gw = total * weight
    r.dn[0] += fold(gw * xh1)
    r.dn[1] += fold(gw)
    return norm_back(total * g1, xh1, inv1)


def forward(r, stars, leaf_rows):
    xc = r.xc[...].astype(F32)
    low = xc.astype(BF)
    r.wait("wq", "wkv", "wo", "we", "wvo")
    r.settle("kv")
    qs = nn(low, r.wq[...]) * r.scale[...]
    kvc = nn(low, r.wkv[...])
    own_score = head_sum(qs * column(kvc, 0))
    r.qs[...] = qs
    r.kvc[...] = kvc
    r.self[...] = own_score
    r.cat[:, 0:PAIR] = stacked(halves(side_by_side(qs, xc)))

    def tile(start, size, rows, carry):
        el = r.el[rows, :]
        ew = el.astype(F32)
        xl = r.xl[rows, :].astype(F32)
        r.en[rows, :] = nn(el, r.we[...]).astype(BF)
        from_star = nn(onehot_col(r.idc[rows, :], stars, 2), r.cat[:, 0:PAIR])
        kv = nn((xl * ew).astype(BF), r.wkv[...])
        r.kv[rows, :] = kv.astype(BF)
        r.s[:, rows] = head_sum_t(column(from_star, 0) * column(kv, 0))
        mc = (column(from_star, 1) * ew).astype(BF)
        r.z[rows, :] = xl + nn(mc, r.wvo[...])
        return carry

    def ffn_tile(start, size, rows, carry):
        if start == 0:
            r.wait("w1", "w2")
            r.settle(*made)
        if start + size == leaf_rows:
            r.z[leaf_rows:, :] = xc + attend(r, stars, leaf_rows, own_score, column(kvc, 1))
        y = ffn_forward(r, r.z[rows, :], rows)
        r.yl[start : start + size, :] = y[:size].astype(r.yl.dtype)
        if start + size == leaf_rows:
            r.yc[...] = y[size:]
        return carry

    made = ("yl", "hb", "xh1", "xh2", "act", "slope")
    r.loop(("xl", "el"), ("en", "kv"), tile, 0)
    r.loop((), made, ffn_tile, 0, stars, FFN_WIDE)
    r.finish("en", "kv", *made)


def attend(r, stars, leaf_rows, own_score, vc):
    ids = r.idr[...]
    live = r.live[...] > 0.5
    score = r.s[...]
    top = jnp.where(live, score, NEG)
    lane = lax.broadcasted_iota(jnp.int32, (1, leaf_rows), 1)
    shift = 1
    while shift < 128:
        same = (pltpu.roll(ids, shift, 1) == ids) & (lane >= shift)
        top = jnp.maximum(top, jnp.where(same, pltpu.roll(top, shift, 1), NEG))
        shift *= 2
    hot_row = onehot_row(ids, stars, 1)
    last = hot_row.astype(F32) * r.last[...]
    present = jnp.sum(last, axis=1, keepdims=True) > 0.5
    last = last.astype(BF)
    star_top = sum(nt(last, part) for part in thirds(top))
    peak = jnp.where(present, jnp.maximum(star_top, own_score), own_score)
    peak_row = tn(stacked(thirds(peak)), onehot_row(ids, stars, 3))
    e = jnp.where(live, jnp.exp(jnp.where(live, score - peak_row, 0.0)), 0.0)
    self_weight = jnp.exp(own_score - peak)
    total = self_weight + sum(nt(hot_row, part) for part in halves(e))
    r.logt[...] = peak + jnp.log(total)
    weighted = (spread_t(e) * column(r.kv, 1).astype(F32)).astype(BF)
    o = (nn(hot_row, weighted) + spread(self_weight) * vc) / spread(total)
    r.o[...] = o
    return nn(o.astype(BF), r.wo[...])


def backward_ffn(r, stars, leaf_rows, own_rows):
    r.dn[...] = jnp.zeros_like(r.dn)
    r.wait("w2", "w1")

    def tile(start, size, rows, carry):
        row = lax.broadcasted_iota(jnp.int32, (size, 1), 0) + start
        mine = jnp.where((row >= HALO) & (row < HALO + own_rows), 1.0, 0.0)
        gy = r.gyl[start : start + size, :].astype(F32)
        if start + size == leaf_rows:
            gy = jnp.concatenate([gy, r.gyc[...].astype(F32)], axis=0)
            mine = jnp.concatenate([mine, r.cown[...]], axis=0)
        r.dz[rows, :] = ffn_backward(r, gy, rows, mine).astype(BF)
        return carry

    made = ("dz", "dbr", "dpre")
    r.loop(("gyl", "xh2", "slope", "xh1"), made, tile, 0, stars, FFN_WIDE)
    r.finish(*made)


def backward_attention(r, stars, leaf_rows):
    r.wait("wo")
    r.arrive_rest("dz")
    do = nt(r.dz[leaf_rows:, :], r.wo[...])
    kvc = r.kvc[...]
    kc, vc = column(kvc, 0), column(kvc, 1)
    qs = r.qs[...]
    xc = r.xc[...].astype(F32)
    r.cat[...] = stacked(halves(side_by_side(qs, xc, do)))
    delta = head_sum(do * r.o[...])
    self_p = jnp.exp(r.self[...] - r.logt[...])
    d_self = self_p * (head_sum(do * vc) - delta)
    coef_c = spread(d_self)
    r.dkvc[...] = side_by_side(coef_c * qs, spread(self_p) * do).astype(BF)
    logt_parts = stacked(thirds(r.logt[...]))
    delta_parts = stacked(thirds(delta))

    def tile(start, size, rows, total):
        el = r.el[rows, :].astype(F32)
        ids_row = r.idr[:, rows]
        hot3 = onehot_row(ids_row, stars, 3)
        from_star = nn(onehot_col(r.idc[rows, :], stars, 2), r.cat[...])
        r.mc[rows, :] = (column(from_star, 1) * el).astype(BF)
        live = r.live[:, rows] > 0.5
        score = r.s[:, rows] - tn(logt_parts, hot3)
        p = jnp.where(live, jnp.exp(jnp.where(live, score, 0.0)), 0.0)
        dor = column(from_star, 2)
        kv = r.kv[rows, :]
        ds = p * (head_sum_t(dor * column(kv, 1).astype(F32)) - tn(delta_parts, hot3))
        coef = spread_t(ds)
        r.dkv[rows, :] = side_by_side(coef * column(from_star, 0), spread_t(p) * dor).astype(BF)
        r.m[rows, :] = (r.xl[rows, :].astype(F32) * el).astype(BF)
        part = (coef * column(kv, 0).astype(F32)).astype(BF)
        return total + nn(onehot_row(ids_row, stars, 1), part)

    zero = jnp.zeros((stars, D), F32)
    total = r.loop(("el", "kv", "xl", "dz"), ("dkv",), tile, zero)
    r.dq[...] = ((total + coef_c * kc) * r.scale[...]).astype(BF)
    r.finish("dkv")


def weight_grads(r, stars, leaf_rows, own_rows):
    own = r.cown[...]
    own_leaf = slice(HALO, HALO + own_rows)
    r.wait("wkv")
    r.arrive("dz", "ge", "hb", "dpre", "act", "dbr")
    nat = r.nat
    xb = r.xc[...].astype(BF)
    dq, dkvc, dac = (
        (x.astype(F32) * own).astype(BF) for x in (r.dq[...], r.dkvc[...], r.dz[leaf_rows:, :])
    )
    nat_store(nat, pl.ds(0, D), tn(xb, dq))
    pair = tn(r.m[own_leaf, :], r.dkv[own_leaf, :]) + tn(xb, dkvc)
    both = tn(r.mc[own_leaf, :], r.dz[own_leaf, :]).astype(BF)
    nat_store(nat, pl.ds(D, D), column(pair, 0))
    nat_store(nat, pl.ds(2 * D, D), column(pair, 1) + nt(both, r.wo[...]))
    out = tn(column(r.wkv, 1), both) + tn(r.o[...].astype(BF), dac)
    nat_store(nat, pl.ds(3 * D, D), out)
    nat_store(nat, pl.ds(4 * D, D), tn(r.el[own_leaf, :], r.ge[own_leaf, :]))
    base = 5 * D
    whole = tn(r.hb[HALO:, :], r.dpre[HALO:, :])
    for j in range(FF // D):
        part = whole[:, j * D : (j + 1) * D]
        nat_store(nat, pl.ds(base + j, D, stride=FF // D), part)
    base = base + FF
    for lo, hi in CHUNKS:
        part = tn(r.dbr[HALO:, 0:D], r.act[HALO:, lo:hi]).T
        nat_store(nat, pl.ds(base + lo, hi - lo), part)
    base = base + FF
    sums = [jnp.sum(r.dn[i], axis=0, keepdims=True) for i in range(4)]
    nat_store(nat, pl.ds(base, 4), jnp.concatenate(sums, axis=0))


def backward_inputs(r, stars, leaf_rows):
    r.wait("wq", "wkv", "wvo", "we")
    xc = r.xc[...].astype(F32)
    r.xcat[...] = stacked(halves(xc))

    def tile(start, size, rows, total):
        dz = r.dz[rows, :]
        dmc = nt(dz, r.wvo[...])
        el = r.el[rows, :].astype(F32)
        hot = onehot_col(r.idc[rows, :], stars, 2)
        dm = nt(r.dkv[rows, :], r.wkv[...])
        r.gxl[rows, :] = (dz.astype(F32) + dm * el).astype(r.gxl.dtype)
        de = dmc * nn(hot, r.xcat[...]) + dm * r.xl[rows, :].astype(F32)
        de = de + nt(r.ge[rows, :], r.we[...])
        r.gel[rows, :] = de.astype(r.gel.dtype)
        return total + nn(onehot_row(r.idr[:, rows], stars, 1), (dmc * el).astype(BF))

    zero = jnp.zeros((stars, D), F32)
    total = r.loop(("dz", "el", "dkv", "xl", "ge"), ("gxl", "gel"), tile, zero)
    r.arrive("dz")
    r.gxc[...] = (
        r.dz[leaf_rows:, :].astype(F32)
        + nt(r.dq[...], r.wq[...])
        + nt(r.dkvc[...], r.wkv[...])
        + total
    )
    r.finish("gxl", "gel")


def nat_load(nat, at):
    return jnp.concatenate([nat[c, at, :] for c in range(3)], axis=1)[:, :D]


def nat_store(nat, at, value):
    nat[0, at, :] = value[:, 0:128]
    nat[1, at, :] = value[:, 128:256]
    rest = jnp.zeros((value.shape[0], 384 - D), F32)
    nat[2, at, :] = jnp.concatenate([value[:, 256:D], rest], axis=1)


def pack_blocks(r, holders, rows):
    nat = r.nat
    lane = lax.broadcasted_iota(jnp.int32, (64, 128), 1)
    half = holders // 2
    for b in range(holders):
        top = b * rows
        at = r.slot[0, b]
        r.all_a[at, 0:128, :] = nat[0, top : top + 128, :].astype(BF)
        r.all_a[at, 128:160, :] = nat[1, top : top + 32, :].astype(BF)
        at = r.slot[1, b]
        r.all_b[at, 0:96, :] = nat[1, top + 32 : top + 128, :].astype(BF)
        high = pltpu.roll(nat[2, top + 64 : top + 128, :], 64, 1)
        tail = jnp.where(lane < 64, nat[2, top : top + 64, :], high)
        r.all_b[at, 96:160, :] = tail.astype(BF)
    for i, name in enumerate(("all_a", "all_b")):
        r.keep[i * half : (i + 1) * half] = r[name][:half]
        r.send[i * half : (i + 1) * half] = r[name][half:]


def unpack_copies(r, layer, holders):
    half = holders // 2
    return [
        pltpu.make_async_copy(r[f"{k}{layer}"], r.got.at[pl.ds(i * half, half)], r.sems.at[i])
        for i, k in enumerate(("near", "far"))
    ]


def unpack_blocks(r, layer, holders, rows):
    nat = r.nat
    for copy in unpack_copies(r, layer, holders):
        copy.wait()

    for b in range(holders):
        top = b * rows
        got = r.got[r.slot[layer, b]].astype(F32)
        nat[0, top : top + rows, :] = got[:rows]
        nat[1, top : top + rows, :] = got[128 : 128 + rows]
        tail = got[256:]
        nat[2, top : top + 64, :] = tail
        nat[2, top + 64 : top + rows, :] = pltpu.roll(tail, 64, 1)[: rows - 64]
    wq, wk, wv, wo, we = (nat_load(nat, pl.ds(i * D, D)).astype(BF) for i in range(5))
    put_squares(r, wq, wk, wv, wo, we)
    base = 5 * D
    for j in range(FF // D):
        part = nat_load(nat, pl.ds(base + j, D, stride=FF // D))
        r.w1[:, j * D : (j + 1) * D] = part.astype(BF)
    base = base + FF
    r.w2[...] = nat_load(nat, pl.ds(base, FF)).astype(BF)
    base = base + FF
    r.norm[...] = nat_load(nat, pl.ds(base, 8))
    r.finish(*WEIGHTS)


def put_squares(r, wq, wk, wv, wo, we):
    r.wq[...] = wq
    r.wkv[...] = side_by_side(wk.astype(F32), wv.astype(F32)).astype(BF)
    r.wo[...] = wo
    r.we[...] = we
    r.wvo[...] = nn(wv, wo).astype(BF)


class Bag(dict):
    def __getattr__(self, name):
        return self[name]


class Refs(Bag):
    def __init__(self, refs, leaf_rows):
        super().__init__(refs)
        state = dict(tiles=leaf_rows // TILE, alias={}, coming={}, going={}, pending=[])
        self.__dict__.update(state)

    def view(self, alias):
        other = Refs({**self, **{k: self[v] for k, v in alias.items()}}, self.tiles * TILE)
        state = dict(alias=alias, coming=self.coming, going=self.going, pending=self.pending)
        other.__dict__.update(state)
        return other

    def keys_of(self, names):
        return [self.alias.get(k, k) for k in names]

    def wait(self, *names):
        for name in self.keys_of(names):
            for copy in self.coming.pop(name, ()):
                copy.wait()

    def arrive(self, *names):
        for name in self.keys_of(names):
            if name in self.coming:
                for copy in self.coming.pop(name)["all"]():
                    copy.wait()

    def arrive_rest(self, name):
        (name,) = self.keys_of([name])
        if name in self.coming:
            for copy in self.coming[name]["rest"]():
                copy.wait()
            self.coming[name]["all"] = self.coming[name]["every"]
            self.coming[name]["rest"] = list

    def loop(self, names, made, body, carry, more=0, group=WIDE):
        coming = [self.coming[k] for k in self.keys_of(names) if "tile" in self.coming.get(k, ())]
        going = [self.going[k] for k in self.keys_of(made) if k in self.going]
        for first in range(0, self.tiles, group):
            stop = min(first + group, self.tiles)
            extra = more if stop == self.tiles else 0
            for k in coming:
                for t in range(first, stop):
                    k["tile"](t, t * TILE).wait()
            if extra:
                for name in names:
                    self.arrive_rest(name)
            start, size = first * TILE, (stop - first) * TILE
            carry = body(start, size, pl.ds(start, size + extra), carry)
            for t in range(first, stop):
                for k in going:
                    k["tile"](t, t * TILE)
        for k in coming:
            k["all"] = k["rest"]
            del k["tile"]
        return carry

    def finish(self, *names):
        for name in self.keys_of(names):
            if name in self.going:
                self.pending += [(name, copy) for copy in self.going.pop(name)["rest"]()]

    def settle(self, *names):
        for name, copy in self.pending:
            if name in names:
                copy.wait()
        self.pending[:] = [x for x in self.pending if x[0] not in names]


def call(body, inputs, outputs, scratch, micros, leaf_rows=TILE, lazy=(), joins=(), own=(), in_smem=(), name=None, loose=(), early=None):
    joins = dict(joins)
    tiles = leaf_rows // TILE
    raw = {k for k, _ in joins.values()} | ({"halo_l", "halo_r"} if joins else set())
    raw |= set(loose)
    lazy_in = [k for k in inputs if k in lazy and k not in raw] + list(joins)
    buffers = {}
    for k in lazy_in:
        source = inputs[joins[k][0]] if k in joins else inputs[k]
        rows = leaf_rows if k in joins else source.shape[0]
        buffers[k] = ((rows,) + source.shape[1:], source.dtype)
    lazy_out = [k for k in outputs if k in lazy]
    for k in lazy_out:
        shape, dtype = outputs[k]
        buffers[k] = ((leaf_rows,) + shape[1:] if k in own else shape, dtype)
    names = list(inputs) + list(outputs) + list(scratch)

    def kernel(*refs):
        outer = dict(zip(names, refs, strict=False))
        rest = refs[len(names) :]
        held = dict(zip(buffers, rest, strict=False))
        sems = rest[-1] if buffers else None
        r = Refs({**outer, **held}, leaf_rows)
        copy = pltpu.make_async_copy
        if early is not None:
            early(r)
        for i, k in enumerate(buffers):
            inner, total = held[k], buffers[k][0][0]
            if k in lazy_out:
                target = outer[k]
                if k in own or total < leaf_rows:
                    cut = pl.ds(HALO, leaf_rows - 2 * HALO) if k in own else pl.ds(0, total)

                    def last(inner=inner, target=target, cut=cut, i=i):
                        one = copy(inner.at[cut], target, sems.at[i, tiles])
                        one.start()
                        return [one]

                    def per_tile(t, start):
                        return None

                else:

                    def per_tile(t, start, inner=inner, target=target, i=i):
                        rows = pl.ds(start, TILE)
                        copy(inner.at[rows], target.at[rows], sems.at[i, t]).start()

                    def last(inner=inner, target=target, i=i, total=total):
                        done = [
                            copy(inner.at[pl.ds(t * TILE, TILE)], target.at[pl.ds(t * TILE, TILE)], sems.at[i, t])
                            for t in range(tiles)
                        ]
                        if total > leaf_rows:
                            rows = pl.ds(leaf_rows, total - leaf_rows)
                            done.append(copy(inner.at[rows], target.at[rows], sems.at[i, tiles]))
                            done[-1].start()
                        return done

                r.going[k] = {"tile": per_tile, "rest": last}
            elif total < leaf_rows or k in WEIGHTS or k[:-1] in WEIGHTS:
                one = copy(outer[k], inner, sems.at[i, 0])
                one.start()
                r.coming[k] = [one]
            else:

                def wait_for(t, start, inner=inner, i=i):
                    rows = inner.at[pl.ds(start, TILE)]
                    return copy(rows, rows, sems.at[i, t])

                def behind(inner=inner, i=i, total=total):
                    if total == leaf_rows:
                        return []
                    rows = inner.at[pl.ds(leaf_rows, total - leaf_rows)]
                    return [copy(rows, rows, sems.at[i, tiles])]

                def every(wait_for=wait_for):
                    return [wait_for(t, t * TILE) for t in range(tiles)]

                def whole(every=every, behind=behind):
                    return every() + behind()

                r.coming[k] = {"tile": wait_for, "rest": behind, "every": every, "all": whole}
        for t in [tiles] + list(range(tiles)):
            for i, k in enumerate(buffers):
                if k in lazy_out or not isinstance(r.coming.get(k), dict):
                    continue
                inner, total = held[k], buffers[k][0][0]
                low, high = t * TILE, min((t + 1) * TILE, leaf_rows)
                if t == tiles:
                    high = total
                if k in joins:
                    source, place = joins[k]
                    stop = leaf_rows - HALO
                    pieces = [
                        (outer["halo_l"], place * HALO, 0, HALO),
                        (outer[source], 0, HALO, stop),
                        (outer["halo_r"], place * HALO, stop, leaf_rows),
                    ]
                else:
                    pieces = [(outer[k], 0, 0, total)]
                for ref, offset, first, stop in pieces:
                    a, b = max(first, low), min(stop, high)
                    if a < b:
                        piece = ref.at[pl.ds(a - first + offset, b - a)]
                        copy(piece, inner.at[pl.ds(a, b - a)], sems.at[i, t]).start()
        body(r)
        for k in list(r.coming):
            if isinstance(r.coming[k], dict):
                r.arrive(k)
            else:
                r.wait(k)
        r.finish(*list(r.going))
        for _, one in r.pending:
            one.wait()

    vmem = pl.BlockSpec(memory_space=pltpu.VMEM)
    smem = pl.BlockSpec(memory_space=pltpu.SMEM)
    anywhere = pl.BlockSpec(memory_space=pl.ANY)

    def place(k):
        return smem if k in in_smem else anywhere if k in lazy or k in raw else vmem

    results = pl.pallas_call(
        kernel,
        out_shape=[jax.ShapeDtypeStruct(s, d) for s, d in outputs.values()],
        in_specs=[place(k) for k in inputs],
        out_specs=[place(k) for k in outputs],
        scratch_shapes=[
            pltpu.SemaphoreType.DMA(s) if d is None else pltpu.VMEM(s, d) for s, d in scratch.values()
        ]
        + [pltpu.VMEM(s, d) for s, d in buffers.values()]
        + ([pltpu.SemaphoreType.DMA((len(buffers), tiles + 1))] if buffers else []),
        compiler_params=pltpu.CompilerParams(vmem_limit_bytes=VMEM),
        cost_estimate=pl.CostEstimate(
            flops=int(micros * 1e9), bytes_accessed=int(micros * 1e6), transcendentals=0
        ),
        name=name,
    )(*inputs.values())
    return Bag(zip(outputs, results, strict=True))


def saved_shapes(stars, leaf_rows):
    rows = leaf_rows + stars
    return dict(
        kv=((leaf_rows, PAIR), BF),
        hb=((rows, D), BF),
        xh1=((rows, STEP_COLUMNS), BF),
        xh2=((rows, STEP_COLUMNS), BF),
        act=((rows, FF), BF),
        slope=((rows, FF), BF),
        s=((HP, leaf_rows), F32),
        qs=((stars, D), F32),
        kvc=((stars, PAIR), F32),
        o=((stars, D), F32),
        self=((stars, HP), F32),
        logt=((stars, HP), F32),
    )


def leaf_shapes(leaf_rows, *names):
    return {k: ((leaf_rows, D), BF) for k in names}


def ffn_scratch(stars, leaf_rows):
    rows = leaf_rows + stars
    return {"dn": ((4, 8, D), F32), "dbr": ((rows, STEP_COLUMNS), BF), "dpre": ((rows, FF), BF)}


def exchange(x, stage, value, sizes):
    axis, shift, bits = stage
    return lax.ppermute(x, axis, [(i, i ^ (value << shift)) for i in range(sizes[axis])])


def tree_stages(sizes, swap):
    bits = {axis: size.bit_length() - 1 for axis, size in sizes.items()}

    def cut(axis, start, stop):
        return [(axis, i, min(2, stop - i)) for i in range(start, stop, 2)]

    middle = [cut("leaf", 1, bits["leaf"]), cut("graph", 0, 1)]
    if swap:
        middle = middle[::-1]
    return [("leaf", 0, 1)] + middle[0] + middle[1] + cut("graph", 1, bits["graph"])


def tree_slot(relative, stages, leaf_bits):
    slot = jnp.zeros_like(relative)
    for axis, shift, bits in stages:
        shift = shift + (leaf_bits if axis == "graph" else 0)
        slot = (slot << bits) | ((relative >> shift) & ((1 << bits) - 1))
    return slot


def gather_step(held, stage, sizes):
    parts = [held] + [exchange(held, stage, v, sizes) for v in range(1, 1 << stage[2])]
    return jnp.concatenate(parts, axis=0)


def total(held, start, stop):
    return sum(x[at + start : at + stop].astype(F32) for x, at in held[0])


def reduce_step(held, stage, sizes):
    terms, rows = held
    count = rows >> stage[2]
    sent = [total(held, v * count, (v + 1) * count).astype(BF) for v in range(1, 1 << stage[2])]
    got = [(exchange(x, stage, v + 1, sizes), 0) for v, x in enumerate(sent)]
    return terms + got, count


def tie(helds, *others):
    newest, others = lax.optimization_barrier(([h[0][-1][0] for h in helds], others))
    return [
        (terms[:-1] + [(x, terms[-1][1])], rows)
        for (terms, rows), x in zip(helds, newest, strict=True)
    ], others


def to_rows(flat, rows):
    block = jnp.pad(flat.reshape(rows, D), ((0, 128 - rows), (0, 0)))
    tail = jnp.pad(block[:, 256:], ((0, 0), (0, 320 - D)))
    return jnp.concatenate(
        [block[:, :128], block[:, 128:256], jnp.concatenate([tail[:64], tail[64:]], axis=1)], axis=0
    )


def from_rows(packed, rows):
    tail = jnp.concatenate([packed[256:, : D - 256], packed[256:, 64 : D - 192]], axis=0)
    block = jnp.concatenate([packed[:128], packed[128:256], tail], axis=1)
    return block[:rows].reshape(-1)


def split_flat(vec):
    square = D * D
    wq, wk, wv, wo, we = (vec[i * square : (i + 1) * square].reshape(D, D) for i in range(5))
    at = 5 * square
    w1 = vec[at : at + D * FF].reshape(D, FF)
    at = at + D * FF
    w2 = vec[at : at + FF * D].reshape(FF, D)
    at = at + FF * D
    norm = jnp.pad(vec[at : at + 4 * D].reshape(4, D).astype(F32), ((0, 4), (0, 0)))
    wkv = jnp.concatenate([wk, jnp.zeros((D, STEP_COLUMNS - D), BF), wv], axis=1)
    return Bag(zip(WEIGHTS, (wq, wkv, wo, we, nn(wv, wo).astype(BF), w1, w2, norm), strict=True))


def halo(x):
    size = lax.axis_size("leaf")
    last, first = x
    left = lax.ppermute(last, "leaf", [(i, i + 1) for i in range(size - 1)])
    right = lax.ppermute(first, "leaf", [(i + 1, i) for i in range(size - 1)])
    return left, right


def local(
    weights,
    first_moment,
    second_moment,
    centers,
    leaves,
    edge_feats,
    center_cot,
    leaf_cot,
    edge_cot,
    graph_ids,
    star_sizes,
    leaf_mask,
    owner_list,
):
    sizes = {"graph": lax.axis_size("graph"), "leaf": lax.axis_size("leaf")}
    holders = sizes["graph"] * sizes["leaf"]
    block_len = weights.shape[1]
    block_rows = block_len // D
    in_rows = block_len % D == 0 and 64 < block_rows <= 128
    stars = centers.shape[1]
    own_rows = leaves.shape[1]
    leaf_rows = own_rows + 2 * HALO

    orders = [tree_stages(sizes, swap) for swap in (False, True)]
    me = lax.axis_index(("graph", "leaf"))
    leaf_bits = sizes["leaf"].bit_length() - 1
    slot = jnp.stack([tree_slot(owner_list ^ me, stages, leaf_bits) for stages in orders])
    nat_rows = ROWS_LAYER + 12
    nat = {"nat": ((3, nat_rows, 128), F32)}
    half = PACK // 2
    n_steps = len(orders[0])
    weights_low = weights.astype(BF)

    def gather_begin(rows):
        held = gather_step(jnp.concatenate(rows, axis=0)[None], orders[0][-1], sizes)
        size = rows[0].shape[0]
        return [held[:, :size], held[:, size:]]

    def gather_more(held, n):
        return [gather_step(h, o[n], sizes) for h, o in zip(held, orders, strict=True)]

    rows = [to_rows(x, block_rows) if in_rows else x for x in weights_low]
    rows, leaves, edge_feats, leaf_cot, edge_cot, graph_ids, leaf_mask = lax.optimization_barrier(
        (rows, leaves, edge_feats, leaf_cot, edge_cot, graph_ids, leaf_mask)
    )
    held = gather_begin(rows)
    raw = dict(leaves=leaves[0], edges=edge_feats[0], lcot=leaf_cot[0], ecot=edge_cot[0])
    marks = jnp.pad((graph_ids + 1).astype(BF), ((0, 15), (0, 0)))
    marks = jnp.concatenate([marks[:8], jnp.broadcast_to(leaf_mask.astype(BF), (8, own_rows))], axis=0)

    def edge(cut):
        note = jnp.pad(marks[:, cut], ((0, 0), (0, D - HALO)))
        return jnp.concatenate([x[cut] for x in raw.values()] + [note], axis=0)

    left, right = halo((edge(slice(own_rows - HALO, own_rows)), edge(slice(0, HALO))))
    at = len(raw)
    raw, held = lax.optimization_barrier((raw, held))
    raw = dict(raw, halo_l=left, halo_r=right)

    def with_marks(line, mine):
        sides = [x[at * HALO + line, :HALO].astype(jnp.int32)[None] for x in (left, right)]
        return jnp.concatenate([sides[0], mine, sides[1]], axis=1)

    ids = with_marks(0, graph_ids + 1) - 1
    live = with_marks(8, leaf_mask).astype(F32)
    edge_id = jnp.full((1, 1), -1, jnp.int32)
    last = (ids != jnp.concatenate([ids[:, 1:], edge_id], axis=1)).astype(F32)
    first = graph_ids[0] != ids[0, HALO - 1 : HALO - 1 + own_rows]
    star_index = jnp.arange(stars, dtype=jnp.int32)
    star_own = jnp.any((star_index[:, None] == graph_ids) & first[None, :], axis=1)[:, None]
    scale = (jnp.log(star_sizes[0].astype(F32)) / (math.log(32.0) * math.sqrt(HEAD)))[:, None]
    base = Bag(
        idc=ids.reshape(-1, 1),
        idr=ids,
        live=live,
        last=last,
        scale=scale,
        cown=star_own.astype(F32),
    )
    saved = saved_shapes(stars, leaf_rows)
    rows = leaf_rows + stars
    if in_rows:
        grads_out = {k: ((holders, half, 128), BF) for k in ("keep", "send")}
        grads_scratch = {k: ((holders, half, 128), BF) for k in ("all_a", "all_b")} | nat
    else:
        grads_out, grads_scratch = nat, {}
    lazy = WEIGHTS[:-1] + tuple(f"{k}{i}" for k in WEIGHTS for i in range(LAYERS)) + ("yl0", "en0", "xl", "el", "gyl", "ge", "yl", "en") + (
        "kv", "hb", "xh1", "xh2", "act", "slope", "dz", "dkv", "gxl", "gel", "dbr", "dpre",
    )
    f_scratch = dict(cat=((2 * stars, PAIR), BF), z=((rows, D), F32))
    a_scratch = {"cat": ((2 * stars, PAIR + STEP_COLUMNS), BF), **leaf_shapes(leaf_rows, "mc", "m")}
    handed = dict(
        dz=((rows, D), BF),
        dkv=((leaf_rows, PAIR), BF),
        dq=((stars, D), BF),
        dkvc=((stars, PAIR), BF),
    )
    def halves_of(*names):
        return {k: raw[k] for k in (*names, "halo_l", "halo_r")}

    join = dict(xl=("leaves", 0), el=("edges", 1), gyl=("lcot", 2), ge=("ecot", 3))

    def joined(*names):
        return {k: join[k] for k in names}

    for n in range(n_steps - 2, 0, -1):
        held = gather_more(held, n)

    def end_grads(r):
        backward_attention(r, stars, leaf_rows)
        weight_grads(r, stars, leaf_rows, own_rows)
        if in_rows:
            pack_blocks(r, holders, block_rows)

    small = [k for k in saved if k not in lazy]

    def start_first(r):
        for copy in unpack_copies(r, 0, holders):
            copy.start()

    def front(r):
        zero = r.view({**{k: k + "0" for k in WEIGHTS}, "yl": "yl0", "en": "en0", "yc": "yc0"})
        names = {**{k: k + "1" for k in (*WEIGHTS, *small)}, "xl": "yl0", "el": "en0", "xc": "yc0"}
        one = r.view(names)
        one.update(dpre=r.slope, dbr=r.xh2)
        if in_rows:
            unpack_blocks(zero, 0, holders, block_rows)
            for copy in unpack_copies(r, 1, holders):
                copy.start()
        forward(zero, stars, leaf_rows)
        if in_rows:
            unpack_blocks(one, 1, holders, block_rows)
            one.update(all_a=r.got.at[:, : PACK // 2], all_b=r.got.at[:, PACK // 2 :])
        forward(one, stars, leaf_rows)
        backward_ffn(one, stars, leaf_rows, own_rows)
        end_grads(one)

    weight_specs = dict(zip(WEIGHTS, WEIGHT_SHAPES, strict=True))
    params, unpacked, kept, loose = [], {}, {}, {}
    for i, near in enumerate(held):
        far = exchange(near, orders[i][0], 1, sizes)
        if in_rows:
            loose.update({f"near{i}": near, f"far{i}": far})
            used = WEIGHTS if i == 0 else ("wq", "wkv", "we", "wvo")
            unpacked.update({f"{k}{i}": weight_specs[k] for k in used})
            kept.update({f"{k}{i}": weight_specs[k] for k in WEIGHTS if k not in used})
        else:
            flat = jnp.concatenate([near, far], axis=0)
            params.append(split_flat(jnp.take(flat, slot[i], axis=0).reshape(-1)))
    if in_rows:
        kept.update(got=((holders, PACK, 128), BF), sems=((2,), None))
        kept.update(nat)
    scratch = {**f_scratch, **a_scratch, "dn": ((4, 8, D), F32), **kept, **{k + "1": saved[k] for k in small}}
    scratch["z"] = ((rows, D), F32)
    two = call(
        front,
        {
            "slot": slot,
            **loose,
            **{f"{k}{i}": x[k] for i, x in enumerate(params) for k in WEIGHTS},
            **halves_of("leaves", "edges", "lcot", "ecot"),
            **base,
            "xc": centers[0],
            "gyc": center_cot[0],
        },
        {
            "yc0": ((stars, D), F32),
            "yc": ((stars, D), F32),
            **leaf_shapes(leaf_rows, "yl0", "en0"),
            **leaf_shapes(own_rows, "yl", "en"),
            **unpacked,
            **saved,
            **handed,
            **grads_out,
        },
        scratch,
        60,
        leaf_rows,
        in_smem=("slot",),
        lazy=lazy,
        joins=joined("xl", "el", "gyl", "ge"),
        own=("yl", "en"),
        name="front",
        loose=loose,
        early=start_first if in_rows else None,
    )
    one = two
    if in_rows:
        params = [Bag({k[:-1]: two[k] for k in unpacked if k[-1] == str(i)}) for i in range(LAYERS)]
    two_in = dict(xc=two.yc0, xl=two.yl0, el=two.en0, **halves_of("ecot"))

    def inputs_of(params, given, made, joins, out_rows, dtype, name):
        return call(
            lambda r: backward_inputs(r, stars, leaf_rows),
            {
                **{k: params[k] for k in ("wvo", "wkv", "we", "wq")},
                **{k: base[k] for k in ("idc", "idr")},
                **given,
                **{k: made[k] for k in handed},
            },
            {"gxc": ((stars, D), F32), "gxl": ((out_rows, D), dtype), "gel": ((out_rows, D), dtype)},
            {"xcat": ((2 * stars, D), BF)},
            9,
            leaf_rows,
            lazy=lazy,
            joins=joins,
            own=("gxl", "gel") if out_rows == own_rows else (),
            name=name,
        )

    def begin(made):
        if not in_rows:
            flat = jnp.swapaxes(made.nat[:, :ROWS_LAYER], 0, 1).reshape(ROWS_LAYER, 384)
            flat = flat[:, :D].reshape(holders, block_len)
            placed = jnp.zeros_like(flat).at[slot[0]].set(flat).astype(BF)
            return [reduce_step(([(placed, 0)], holders), orders[0][0], sizes)]
        got = exchange(made.send, orders[0][0], 1, sizes)
        count = holders // 2
        return [([(made.keep, i), (got, i)], count) for i in (0, count)]

    def advance(held, n):
        return [reduce_step(h, o[n], sizes) for h, o in zip(held, orders, strict=False)]

    def joined_total(held):
        rows = held[0][1]
        both = jnp.concatenate([total(h, 0, rows) for h in held], axis=1)
        return [([(both.astype(BF), 0)], rows)]

    def last_step(held):
        return reduce_step(held[0], orders[0][-1], sizes)

    def end(held):
        block = total(held, 0, 1)[0]
        return from_rows(block, block_rows) if in_rows else block

    held_two = begin(two)
    two_grads = inputs_of(params[1], two_in, two, joined("ge"), leaf_rows, BF, "last_inputs")
    held_two, (gyc,) = tie(held_two, two_grads.gxc)
    held_two = advance(held_two, 1)
    made = {"dz": handed["dz"], **ffn_scratch(stars, leaf_rows)}
    mid = call(
        lambda r: backward_ffn(r, stars, leaf_rows, own_rows),
        {
            "w2": params[0].w2,
            "gyl": two_grads.gxl,
            **{k: one[k] for k in ("xh2", "slope")},
            "w1": params[0].w1,
            "xh1": one.xh1,
            "norm": params[0].norm,
            "cown": base.cown,
            "gyc": gyc,
        },
        made,
        {},
        13,
        leaf_rows,
        lazy=lazy,
        name="first_ffn",
    )
    held_two, (dn,) = tie(held_two, mid.dn)
    if n_steps > 2:
        held_two = advance(held_two, 2)
    ffn_names = ("xh2", "slope", "xh1")
    three = call(
        end_grads,
        {
            **{k: params[0][k] for k in ("wo", "wkv")},
            **mid,
            **{k: one[k] for k in saved if k not in ffn_names},
            **halves_of("leaves", "edges"),
            **base,
            "slot": slot,
            "xc": centers[0],
            "ge": two_grads.gel,
            "dn": dn,
        },
        {**{k: handed[k] for k in handed if k != "dz"}, **grads_out},
        {**a_scratch, **grads_scratch},
        18,
        leaf_rows,
        in_smem=("slot",),
        lazy=lazy,
        joins=joined("xl", "el"),
        name="first",
    )
    three["dz"] = mid.dz
    for n in range(3, n_steps - 1):
        held_two = advance(held_two, n)
    key = "send" if in_rows else "nat"
    held_two, (three[key],) = tie(held_two, three[key])
    held_three = begin(three)
    held_two = joined_total(held_two)
    count = len(held_two)
    both, (dq,) = tie(held_two + held_three, three.dq)
    held_three = both[count:]
    last_two = last_step(both[:count])
    handed_three = {**{k: three[k] for k in handed}, "dq": dq}
    held_three = advance(held_three, 1)
    three_in = dict(xc=centers[0], ge=two_grads.gel, **halves_of("leaves", "edges"))
    three_grads = inputs_of(
        params[0], three_in, handed_three, joined("xl", "el"), own_rows, F32, "first_inputs"
    )
    late = [x for x, _ in last_two[0][1:]]
    held_three, (gxc, yc, *late) = tie(held_three, three_grads.gxc, two.yc, *late)
    last_two = (last_two[0][:1] + [(x, 0) for x in late], last_two[1])
    center_rows = jnp.where(star_own, jnp.concatenate([yc, gxc], axis=1), 0.0)
    center_rows = center_rows + exchange(center_rows, ("leaf", 0, 1), 1, sizes)
    held_three = advance(held_three, 2) if n_steps > 3 else held_three
    for n in range(3, n_steps - 1):
        held_three = advance(held_three, n)
    held_three, (gxl, gel, yl, en, center_rows) = tie(
        held_three, three_grads.gxl, three_grads.gel, two.yl, two.en, center_rows
    )
    for bit in range(1, leaf_bits):
        center_rows = center_rows + exchange(center_rows, ("leaf", bit, 1), 1, sizes)
    centers_out, grad_centers = center_rows[:, :D].astype(BF), center_rows[:, D:]
    lasts, _ = tie([last_step(joined_total(held_three)), last_two])
    grad_total = jnp.stack([end(x) for x in lasts])
    first_new = BETA_ONE * first_moment + (1.0 - BETA_ONE) * grad_total
    second_new = BETA_TWO * second_moment + (1.0 - BETA_TWO) * grad_total * grad_total
    step_one = first_new / (1.0 - BETA_ONE**STEP)
    step_two = second_new / (1.0 - BETA_TWO**STEP)
    weights_new = weights - RATE * (step_one / (jnp.sqrt(step_two) + EPS_ADAM) + DECAY * weights)
    return (
        centers_out[None],
        yl[None],
        en[None],
        grad_centers[None],
        gxl[None],
        gel[None],
        first_new,
        second_new,
        weights_new,
        weights_new.astype(BF),
        grad_total,
    )


def solution(mesh):
    both = ("graph", "leaf")
    return jax.shard_map(
        local,
        mesh=mesh,
        in_specs=(
            P(None, both),
            P(None, both),
            P(None, both),
            P("graph", None, None),
            P("graph", "leaf", None),
            P("graph", "leaf", None),
            P("graph", None, None),
            P("graph", "leaf", None),
            P("graph", "leaf", None),
            P("graph", "leaf"),
            P("graph", None),
            P("graph", "leaf"),
            P(),
        ),
        out_specs=(
            P("graph", None, None),
            P("graph", "leaf", None),
            P("graph", "leaf", None),
            P("graph", None, None),
            P("graph", "leaf", None),
            P("graph", "leaf", None),
            P(None, both),
            P(None, both),
            P(None, both),
            P(None, both),
            P(None, both),
        ),
        check_vma=False,
    )
```

```python
import math

import jax
import jax.numpy as jnp
from jax import lax
from jax.experimental import pallas as pl
from jax.experimental.pallas import tpu as pltpu
from jax.sharding import PartitionSpec as P

D = 300
HEADS = 12
HEAD = 25
FF = 1200
LAYERS = 2
STEP = 5
ROWS_LAYER = 5 * D + 2 * FF + 4

NEG = -1e30
EPS_NORM = 1e-05
BETA_ONE = 0.9
BETA_TWO = 0.999
RATE = 0.05
DECAY = 0.01
EPS_ADAM = 1e-08
INV_ROOT_TWO = 0.7071067811865476
INV_ROOT_TWO_PI = 0.3989422804014327

HALO = 128
TILE = 320
WIDE = 2
FFN_WIDE = 1
HP = 16
PACK = 320
CHUNKS = tuple((i, min(i + 256, FF)) for i in range(0, FF, 256))
VMEM = 60 << 20
F32 = jnp.float32
BF = jnp.bfloat16

STEP_COLUMNS = 384
PAIR = STEP_COLUMNS + D

WEIGHTS = ("wq", "wkv", "wo", "we", "wvo", "w1", "w2", "norm")
WEIGHT_SHAPES = (
    ((D, D), BF),
    ((D, PAIR), BF),
    ((D, D), BF),
    ((D, D), BF),
    ((D, D), BF),
    ((D, FF), BF),
    ((FF, D), BF),
    ((8, D), F32),
)


def nn(a, b):
    return lax.dot_general(a, b, (((1,), (0,)), ((), ())), preferred_element_type=F32)


def nt(a, b):
    return lax.dot_general(a, b, (((1,), (1,)), ((), ())), preferred_element_type=F32)


def tn(a, b):
    return lax.dot_general(a, b, (((0,), (0,)), ((), ())), preferred_element_type=F32)


def halves(x):
    high = x.astype(BF)
    return high, (x - high.astype(F32)).astype(BF)


def thirds(x):
    high = x.astype(BF)
    rest = x - high.astype(F32)
    mid = rest.astype(BF)
    return high, mid, (rest - mid.astype(F32)).astype(BF)


def stacked(parts, axis=0):
    return jnp.concatenate([p.astype(F32) for p in parts], axis=axis).astype(BF)


def side_by_side(*parts):
    zeros = jnp.zeros((parts[0].shape[0], STEP_COLUMNS - D), F32)
    pieces = [parts[0]]
    for part in parts[1:]:
        pieces += [zeros, part]
    return jnp.concatenate(pieces, axis=1)


def column(values, i):
    return values[:, i * STEP_COLUMNS : i * STEP_COLUMNS + D]


def table(rows, repeat=1):
    head = lax.broadcasted_iota(jnp.int32, (repeat * rows, D), 0) % rows
    feature = lax.broadcasted_iota(jnp.int32, (repeat * rows, D), 1)
    low = head * HEAD
    return jnp.where((feature >= low) & (feature < low + HEAD), 1.0, 0.0).astype(BF)


def head_sum(values):
    high, low = halves(values)
    tab = table(HP)
    return nt(high, tab) + nt(low, tab)


def head_sum_t(values):
    high, low = halves(values)
    tab = table(HP)
    return nt(tab, high) + nt(tab, low)


def spread(values):
    high, low = halves(values)
    tab = table(HP)
    return nn(high, tab) + nn(low, tab)


def spread_t(values):
    return tn(stacked(halves(values)), table(HP, 2))


def onehot_col(ids, stars, repeat):
    lane = lax.broadcasted_iota(jnp.int32, (ids.shape[0], repeat * stars), 1)
    hit = lane == ids
    for i in range(1, repeat):
        hit = hit | (lane == ids + i * stars) & (ids >= 0)
    return jnp.where(hit, 1.0, 0.0).astype(BF)


def onehot_row(ids, stars, repeat):
    sub = lax.broadcasted_iota(jnp.int32, (repeat * stars, ids.shape[1]), 0)
    hit = sub == ids
    for i in range(1, repeat):
        hit = hit | (sub == ids + i * stars) & (ids >= 0)
    return jnp.where(hit, 1.0, 0.0).astype(BF)


def row_mean(x):
    return jnp.sum(x, axis=-1, keepdims=True) * (1.0 / D)


def normalized(x):
    dev = x - row_mean(x)
    inverse = lax.rsqrt(row_mean(dev * dev) + EPS_NORM)
    return dev * inverse, inverse


def norm_back(grad, scaled, inverse):
    return inverse * (grad - row_mean(grad) - scaled * row_mean(grad * scaled))


def put_normalized(ref, rows, scaled, inverse):
    ref[rows, 0:D] = scaled.astype(BF)
    high, low = halves(inverse)
    ref[rows, D : D + 1] = high
    ref[rows, D + 1 : D + 2] = low


def get_normalized(ref, rows):
    inverse = ref[rows, D : D + 1].astype(F32) + ref[rows, D + 1 : D + 2].astype(F32)
    return ref[rows, 0:D].astype(F32), inverse


def ffn_forward(r, z, rows):
    norm = r.norm
    g1, b1, g2, b2 = (norm[i : i + 1, :] for i in range(4))
    xh1, inv1 = normalized(z)
    h = xh1 * g1 + b1
    hb = h.astype(BF)
    r.hb[rows, :] = hb
    put_normalized(r.xh1, rows, xh1, inv1)
    total = h
    for lo, hi in CHUNKS:
        pre = nn(hb, r.w1[:, lo:hi])
        cdf = 0.5 * (1.0 + lax.erf(pre * INV_ROOT_TWO))
        act = (pre * cdf).astype(BF)
        r.act[rows, lo:hi] = act
        r.slope[rows, lo:hi] = (
            cdf + pre * jnp.exp(-0.5 * pre * pre) * INV_ROOT_TWO_PI
        ).astype(BF)
        total = total + nn(act, r.w2[lo:hi, :])
    xh2, inv2 = normalized(total)
    put_normalized(r.xh2, rows, xh2, inv2)
    return xh2 * g2 + b2


def fold(x):
    return jnp.sum(x.reshape(x.shape[0] // 8, 8, x.shape[1]), axis=0)


def ffn_backward(r, gy, rows, weight):
    norm = r.norm
    g1, g2 = norm[0:1, :], norm[2:3, :]
    xh2, inv2 = get_normalized(r.xh2, rows)
    gw = gy * weight
    r.dn[2] += fold(gw * xh2)
    r.dn[3] += fold(gw)
    mid = norm_back(gy * g2, xh2, inv2)
    branch = mid.astype(BF)
    r.dbr[rows, 0:D] = (mid * weight).astype(BF)
    total = mid
    for lo, hi in CHUNKS:
        dact = nt(branch, r.w2[lo:hi, :])
        dpre = dact * r.slope[rows, lo:hi].astype(F32)
        low = dpre.astype(BF)
        r.dpre[rows, lo:hi] = (dpre * weight).astype(BF)
        total = total + nt(low, r.w1[:, lo:hi])
    xh1, inv1 = get_normalized(r.xh1, rows)
    gw = total * weight
    r.dn[0] += fold(gw * xh1)
    r.dn[1] += fold(gw)
    return norm_back(total * g1, xh1, inv1)


def forward(r, stars, leaf_rows):
    xc = r.xc[...].astype(F32)
    low = xc.astype(BF)
    r.wait("wq", "wkv", "wo", "we", "wvo")
    r.settle("kv")
    qs = nn(low, r.wq[...]) * r.scale[...]
    kvc = nn(low, r.wkv[...])
    own_score = head_sum(qs * column(kvc, 0))
    r.qs[...] = qs
    r.kvc[...] = kvc
    r.self[...] = own_score
    r.cat[:, 0:PAIR] = stacked(halves(side_by_side(qs, xc)))

    def tile(start, size, rows, carry):
        el = r.el[rows, :]
        ew = el.astype(F32)
        xl = r.xl[rows, :].astype(F32)
        r.en[rows, :] = nn(el, r.we[...]).astype(BF)
        from_star = nn(onehot_col(r.idc[rows, :], stars, 2), r.cat[:, 0:PAIR])
        kv = nn((xl * ew).astype(BF), r.wkv[...])
        r.kv[rows, :] = kv.astype(BF)
        r.s[:, rows] = head_sum_t(column(from_star, 0) * column(kv, 0))
        mc = (column(from_star, 1) * ew).astype(BF)
        r.z[rows, :] = xl + nn(mc, r.wvo[...])
        return carry

    def ffn_tile(start, size, rows, carry):
        if start == 0:
            r.wait("w1", "w2")
            r.settle(*made)
        if start + size == leaf_rows:
            r.z[leaf_rows:, :] = xc + attend(r, stars, leaf_rows, own_score, column(kvc, 1))
        y = ffn_forward(r, r.z[rows, :], rows)
        r.yl[start : start + size, :] = y[:size].astype(r.yl.dtype)
        if start + size == leaf_rows:
            r.yc[...] = y[size:]
        return carry

    made = ("yl", "hb", "xh1", "xh2", "act", "slope")
    r.loop(("xl", "el"), ("en", "kv"), tile, 0)
    r.loop((), made, ffn_tile, 0, stars, FFN_WIDE)
    r.finish("en", "kv", *made)


def attend(r, stars, leaf_rows, own_score, vc):
    ids = r.idr[...]
    live = r.live[...] > 0.5
    score = r.s[...]
    top = jnp.where(live, score, NEG)
    lane = lax.broadcasted_iota(jnp.int32, (1, leaf_rows), 1)
    shift = 1
    while shift < 128:
        same = (pltpu.roll(ids, shift, 1) == ids) & (lane >= shift)
        top = jnp.maximum(top, jnp.where(same, pltpu.roll(top, shift, 1), NEG))
        shift *= 2
    hot_row = onehot_row(ids, stars, 1)
    last = hot_row.astype(F32) * r.last[...]
    present = jnp.sum(last, axis=1, keepdims=True) > 0.5
    last = last.astype(BF)
    star_top = sum(nt(last, part) for part in thirds(top))
    peak = jnp.where(present, jnp.maximum(star_top, own_score), own_score)
    peak_row = tn(stacked(thirds(peak)), onehot_row(ids, stars, 3))
    e = jnp.where(live, jnp.exp(jnp.where(live, score - peak_row, 0.0)), 0.0)
    self_weight = jnp.exp(own_score - peak)
    total = self_weight + sum(nt(hot_row, part) for part in halves(e))
    r.logt[...] = peak + jnp.log(total)
    weighted = (spread_t(e) * column(r.kv, 1).astype(F32)).astype(BF)
    o = (nn(hot_row, weighted) + spread(self_weight) * vc) / spread(total)
    r.o[...] = o
    return nn(o.astype(BF), r.wo[...])


def backward_ffn(r, stars, leaf_rows, own_rows):
    r.dn[...] = jnp.zeros_like(r.dn)
    r.wait("w2", "w1")

    def tile(start, size, rows, carry):
        row = lax.broadcasted_iota(jnp.int32, (size, 1), 0) + start
        mine = jnp.where((row >= HALO) & (row < HALO + own_rows), 1.0, 0.0)
        gy = r.gyl[start : start + size, :].astype(F32)
        if start + size == leaf_rows:
            gy = jnp.concatenate([gy, r.gyc[...].astype(F32)], axis=0)
            mine = jnp.concatenate([mine, r.cown[...]], axis=0)
        r.dz[rows, :] = ffn_backward(r, gy, rows, mine).astype(BF)
        return carry

    made = ("dz", "dbr", "dpre")
    r.loop(("gyl", "xh2", "slope", "xh1"), made, tile, 0, stars, FFN_WIDE)
    r.finish(*made)


def backward_attention(r, stars, leaf_rows):
    r.wait("wo")
    r.arrive_rest("dz")
    do = nt(r.dz[leaf_rows:, :], r.wo[...])
    kvc = r.kvc[...]
    kc, vc = column(kvc, 0), column(kvc, 1)
    qs = r.qs[...]
    xc = r.xc[...].astype(F32)
    r.cat[...] = stacked(halves(side_by_side(qs, xc, do)))
    delta = head_sum(do * r.o[...])
    self_p = jnp.exp(r.self[...] - r.logt[...])
    d_self = self_p * (head_sum(do * vc) - delta)
    coef_c = spread(d_self)
    r.dkvc[...] = side_by_side(coef_c * qs, spread(self_p) * do).astype(BF)
    logt_parts = stacked(thirds(r.logt[...]))
    delta_parts = stacked(thirds(delta))

    def tile(start, size, rows, total):
        el = r.el[rows, :].astype(F32)
        ids_row = r.idr[:, rows]
        hot3 = onehot_row(ids_row, stars, 3)
        from_star = nn(onehot_col(r.idc[rows, :], stars, 2), r.cat[...])
        r.mc[rows, :] = (column(from_star, 1) * el).astype(BF)
        live = r.live[:, rows] > 0.5
        score = r.s[:, rows] - tn(logt_parts, hot3)
        p = jnp.where(live, jnp.exp(jnp.where(live, score, 0.0)), 0.0)
        dor = column(from_star, 2)
        kv = r.kv[rows, :]
        ds = p * (head_sum_t(dor * column(kv, 1).astype(F32)) - tn(delta_parts, hot3))
        coef = spread_t(ds)
        r.dkv[rows, :] = side_by_side(coef * column(from_star, 0), spread_t(p) * dor).astype(BF)
        r.m[rows, :] = (r.xl[rows, :].astype(F32) * el).astype(BF)
        part = (coef * column(kv, 0).astype(F32)).astype(BF)
        return total + nn(onehot_row(ids_row, stars, 1), part)

    zero = jnp.zeros((stars, D), F32)
    total = r.loop(("el", "kv", "xl", "dz"), ("dkv",), tile, zero)
    r.dq[...] = ((total + coef_c * kc) * r.scale[...]).astype(BF)
    r.finish("dkv")


def weight_grads(r, stars, leaf_rows, own_rows):
    own = r.cown[...]
    own_leaf = slice(HALO, HALO + own_rows)
    r.wait("wkv")
    r.arrive("dz", "ge", "hb", "dpre", "act", "dbr")
    nat = r.nat
    xb = r.xc[...].astype(BF)
    dq, dkvc, dac = (
        (x.astype(F32) * own).astype(BF) for x in (r.dq[...], r.dkvc[...], r.dz[leaf_rows:, :])
    )
    nat_store(nat, pl.ds(0, D), tn(xb, dq))
    pair = tn(r.m[own_leaf, :], r.dkv[own_leaf, :]) + tn(xb, dkvc)
    both = tn(r.mc[own_leaf, :], r.dz[own_leaf, :]).astype(BF)
    nat_store(nat, pl.ds(D, D), column(pair, 0))
    nat_store(nat, pl.ds(2 * D, D), column(pair, 1) + nt(both, r.wo[...]))
    out = tn(column(r.wkv, 1), both) + tn(r.o[...].astype(BF), dac)
    nat_store(nat, pl.ds(3 * D, D), out)
    nat_store(nat, pl.ds(4 * D, D), tn(r.el[own_leaf, :], r.ge[own_leaf, :]))
    base = 5 * D
    whole = tn(r.hb[HALO:, :], r.dpre[HALO:, :])
    for j in range(FF // D):
        part = whole[:, j * D : (j + 1) * D]
        nat_store(nat, pl.ds(base + j, D, stride=FF // D), part)
    base = base + FF
    for lo, hi in CHUNKS:
        part = tn(r.dbr[HALO:, 0:D], r.act[HALO:, lo:hi]).T
        nat_store(nat, pl.ds(base + lo, hi - lo), part)
    base = base + FF
    sums = [jnp.sum(r.dn[i], axis=0, keepdims=True) for i in range(4)]
    nat_store(nat, pl.ds(base, 4), jnp.concatenate(sums, axis=0))


def backward_inputs(r, stars, leaf_rows):
    r.wait("wq", "wkv", "wvo", "we")
    xc = r.xc[...].astype(F32)
    r.xcat[...] = stacked(halves(xc))

    def tile(start, size, rows, total):
        dz = r.dz[rows, :]
        dmc = nt(dz, r.wvo[...])
        el = r.el[rows, :].astype(F32)
        hot = onehot_col(r.idc[rows, :], stars, 2)
        dm = nt(r.dkv[rows, :], r.wkv[...])
        r.gxl[rows, :] = (dz.astype(F32) + dm * el).astype(r.gxl.dtype)
        de = dmc * nn(hot, r.xcat[...]) + dm * r.xl[rows, :].astype(F32)
        de = de + nt(r.ge[rows, :], r.we[...])
        r.gel[rows, :] = de.astype(r.gel.dtype)
        return total + nn(onehot_row(r.idr[:, rows], stars, 1), (dmc * el).astype(BF))

    zero = jnp.zeros((stars, D), F32)
    total = r.loop(("dz", "el", "dkv", "xl", "ge"), ("gxl", "gel"), tile, zero)
    r.arrive("dz")
    r.gxc[...] = (
        r.dz[leaf_rows:, :].astype(F32)
        + nt(r.dq[...], r.wq[...])
        + nt(r.dkvc[...], r.wkv[...])
        + total
    )
    r.finish("gxl", "gel")


def nat_load(nat, at):
    return jnp.concatenate([nat[c, at, :] for c in range(3)], axis=1)[:, :D]


def nat_store(nat, at, value):
    nat[0, at, :] = value[:, 0:128]
    nat[1, at, :] = value[:, 128:256]
    rest = jnp.zeros((value.shape[0], 384 - D), F32)
    nat[2, at, :] = jnp.concatenate([value[:, 256:D], rest], axis=1)


def pack_blocks(r, holders, rows):
    nat = r.nat
    lane = lax.broadcasted_iota(jnp.int32, (64, 128), 1)
    half = holders // 2
    for b in range(holders):
        top = b * rows
        at = r.slot[0, b]
        r.all_a[at, 0:128, :] = nat[0, top : top + 128, :].astype(BF)
        r.all_a[at, 128:160, :] = nat[1, top : top + 32, :].astype(BF)
        at = r.slot[1, b]
        r.all_b[at, 0:96, :] = nat[1, top + 32 : top + 128, :].astype(BF)
        high = pltpu.roll(nat[2, top + 64 : top + 128, :], 64, 1)
        tail = jnp.where(lane < 64, nat[2, top : top + 64, :], high)
        r.all_b[at, 96:160, :] = tail.astype(BF)
    for i, name in enumerate(("all_a", "all_b")):
        r.keep[i * half : (i + 1) * half] = r[name][:half]
        r.send[i * half : (i + 1) * half] = r[name][half:]


def unpack_copies(r, layer, holders):
    half = holders // 2
    return [
        pltpu.make_async_copy(r[f"{k}{layer}"], r.got.at[pl.ds(i * half, half)], r.sems.at[i])
        for i, k in enumerate(("near", "far"))
    ]


def unpack_blocks(r, layer, holders, rows):
    nat = r.nat
    for copy in unpack_copies(r, layer, holders):
        copy.wait()

    for b in range(holders):
        top = b * rows
        got = r.got[r.slot[layer, b]].astype(F32)
        nat[0, top : top + rows, :] = got[:rows]
        nat[1, top : top + rows, :] = got[128 : 128 + rows]
        tail = got[256:]
        nat[2, top : top + 64, :] = tail
        nat[2, top + 64 : top + rows, :] = pltpu.roll(tail, 64, 1)[: rows - 64]
    wq, wk, wv, wo, we = (nat_load(nat, pl.ds(i * D, D)).astype(BF) for i in range(5))
    put_squares(r, wq, wk, wv, wo, we)
    base = 5 * D
    for j in range(FF // D):
        part = nat_load(nat, pl.ds(base + j, D, stride=FF // D))
        r.w1[:, j * D : (j + 1) * D] = part.astype(BF)
    base = base + FF
    r.w2[...] = nat_load(nat, pl.ds(base, FF)).astype(BF)
    base = base + FF
    r.norm[...] = nat_load(nat, pl.ds(base, 8))
    r.finish(*WEIGHTS)


def put_squares(r, wq, wk, wv, wo, we):
    r.wq[...] = wq
    r.wkv[...] = side_by_side(wk.astype(F32), wv.astype(F32)).astype(BF)
    r.wo[...] = wo
    r.we[...] = we
    r.wvo[...] = nn(wv, wo).astype(BF)


class Bag(dict):
    def __getattr__(self, name):
        return self[name]


class Refs(Bag):
    def __init__(self, refs, leaf_rows):
        super().__init__(refs)
        state = dict(tiles=leaf_rows // TILE, alias={}, coming={}, going={}, pending=[])
        self.__dict__.update(state)

    def view(self, alias):
        other = Refs({**self, **{k: self[v] for k, v in alias.items()}}, self.tiles * TILE)
        state = dict(alias=alias, coming=self.coming, going=self.going, pending=self.pending)
        other.__dict__.update(state)
        return other

    def keys_of(self, names):
        return [self.alias.get(k, k) for k in names]

    def wait(self, *names):
        for name in self.keys_of(names):
            for copy in self.coming.pop(name, ()):
                copy.wait()

    def arrive(self, *names):
        for name in self.keys_of(names):
            if name in self.coming:
                for copy in self.coming.pop(name)["all"]():
                    copy.wait()

    def arrive_rest(self, name):
        (name,) = self.keys_of([name])
        if name in self.coming:
            for copy in self.coming[name]["rest"]():
                copy.wait()
            self.coming[name]["all"] = self.coming[name]["every"]
            self.coming[name]["rest"] = list

    def loop(self, names, made, body, carry, more=0, group=WIDE):
        coming = [self.coming[k] for k in self.keys_of(names) if "tile" in self.coming.get(k, ())]
        going = [self.going[k] for k in self.keys_of(made) if k in self.going]
        for first in range(0, self.tiles, group):
            stop = min(first + group, self.tiles)
            extra = more if stop == self.tiles else 0
            for k in coming:
                for t in range(first, stop):
                    k["tile"](t, t * TILE).wait()
            if extra:
                for name in names:
                    self.arrive_rest(name)
            start, size = first * TILE, (stop - first) * TILE
            carry = body(start, size, pl.ds(start, size + extra), carry)
            for t in range(first, stop):
                for k in going:
                    k["tile"](t, t * TILE)
        for k in coming:
            k["all"] = k["rest"]
            del k["tile"]
        return carry

    def finish(self, *names):
        for name in self.keys_of(names):
            if name in self.going:
                self.pending += [(name, copy) for copy in self.going.pop(name)["rest"]()]

    def settle(self, *names):
        for name, copy in self.pending:
            if name in names:
                copy.wait()
        self.pending[:] = [x for x in self.pending if x[0] not in names]


LATER = ("gyl", "ge", "hb", "dpre", "act", "dbr")


def call(body, inputs, outputs, scratch, micros, leaf_rows=TILE, lazy=(), joins=(), own=(), in_smem=(), name=None, loose=(), early=None, soon=None):
    joins = dict(joins)
    tiles = leaf_rows // TILE
    raw = {k for k, _ in joins.values()} | ({"halo_l", "halo_r"} if joins else set())
    raw |= set(loose)
    lazy_in = [k for k in inputs if k in lazy and k not in raw] + list(joins)
    buffers = {}
    for k in lazy_in:
        source = inputs[joins[k][0]] if k in joins else inputs[k]
        rows = leaf_rows if k in joins else source.shape[0]
        buffers[k] = ((rows,) + source.shape[1:], source.dtype)
    lazy_out = [k for k in outputs if k in lazy]
    for k in lazy_out:
        shape, dtype = outputs[k]
        buffers[k] = ((leaf_rows,) + shape[1:] if k in own else shape, dtype)
    names = list(inputs) + list(outputs) + list(scratch)

    def kernel(*refs):
        outer = dict(zip(names, refs, strict=False))
        rest = refs[len(names) :]
        held = dict(zip(buffers, rest, strict=False))
        sems = rest[-1] if buffers else None
        r = Refs({**outer, **held}, leaf_rows)
        copy = pltpu.make_async_copy
        if early is not None:
            early(r)
        for i, k in enumerate(buffers):
            inner, total = held[k], buffers[k][0][0]
            if k in lazy_out:
                target = outer[k]
                if k in own or total < leaf_rows:
                    cut = pl.ds(HALO, leaf_rows - 2 * HALO) if k in own else pl.ds(0, total)

                    def last(inner=inner, target=target, cut=cut, i=i):
                        one = copy(inner.at[cut], target, sems.at[i, tiles])
                        one.start()
                        return [one]

                    def per_tile(t, start):
                        return None

                else:

                    def per_tile(t, start, inner=inner, target=target, i=i):
                        rows = pl.ds(start, TILE)
                        copy(inner.at[rows], target.at[rows], sems.at[i, t]).start()

                    def last(inner=inner, target=target, i=i, total=total):
                        done = [
                            copy(inner.at[pl.ds(t * TILE, TILE)], target.at[pl.ds(t * TILE, TILE)], sems.at[i, t])
                            for t in range(tiles)
                        ]
                        if total > leaf_rows:
                            rows = pl.ds(leaf_rows, total - leaf_rows)
                            done.append(copy(inner.at[rows], target.at[rows], sems.at[i, tiles]))
                            done[-1].start()
                        return done

                r.going[k] = {"tile": per_tile, "rest": last}
            elif total < leaf_rows or k in WEIGHTS or k[:-1] in WEIGHTS:
                one = copy(outer[k], inner, sems.at[i, 0])
                one.start()
                r.coming[k] = [one]
            else:

                def wait_for(t, start, inner=inner, i=i):
                    rows = inner.at[pl.ds(start, TILE)]
                    return copy(rows, rows, sems.at[i, t])

                def behind(inner=inner, i=i, total=total):
                    if total == leaf_rows:
                        return []
                    rows = inner.at[pl.ds(leaf_rows, total - leaf_rows)]
                    return [copy(rows, rows, sems.at[i, tiles])]

                def every(wait_for=wait_for):
                    return [wait_for(t, t * TILE) for t in range(tiles)]

                def whole(every=every, behind=behind):
                    return every() + behind()

                r.coming[k] = {"tile": wait_for, "rest": behind, "every": every, "all": whole}
        order = [
            (t, i, k)
            for later in (False, True)
            for t in [tiles] + list(range(tiles))
            for i, k in enumerate(buffers)
            if (k in LATER and k != soon) == later
        ]
        for t, i, k in order:
            if k not in lazy_out and isinstance(r.coming.get(k), dict):
                inner, total = held[k], buffers[k][0][0]
                low, high = t * TILE, min((t + 1) * TILE, leaf_rows)
                if t == tiles:
                    high = total
                if k in joins:
                    source, place = joins[k]
                    stop = leaf_rows - HALO
                    pieces = [
                        (outer["halo_l"], place * HALO, 0, HALO),
                        (outer[source], 0, HALO, stop),
                        (outer["halo_r"], place * HALO, stop, leaf_rows),
                    ]
                else:
                    pieces = [(outer[k], 0, 0, total)]
                for ref, offset, first, stop in pieces:
                    a, b = max(first, low), min(stop, high)
                    if a < b:
                        piece = ref.at[pl.ds(a - first + offset, b - a)]
                        copy(piece, inner.at[pl.ds(a, b - a)], sems.at[i, t]).start()
        body(r)
        for k in list(r.coming):
            if isinstance(r.coming[k], dict):
                r.arrive(k)
            else:
                r.wait(k)
        r.finish(*list(r.going))
        for _, one in r.pending:
            one.wait()

    vmem = pl.BlockSpec(memory_space=pltpu.VMEM)
    smem = pl.BlockSpec(memory_space=pltpu.SMEM)
    anywhere = pl.BlockSpec(memory_space=pl.ANY)

    def place(k):
        return smem if k in in_smem else anywhere if k in lazy or k in raw else vmem

    results = pl.pallas_call(
        kernel,
        out_shape=[jax.ShapeDtypeStruct(s, d) for s, d in outputs.values()],
        in_specs=[place(k) for k in inputs],
        out_specs=[place(k) for k in outputs],
        scratch_shapes=[
            pltpu.SemaphoreType.DMA(s) if d is None else pltpu.VMEM(s, d) for s, d in scratch.values()
        ]
        + [pltpu.VMEM(s, d) for s, d in buffers.values()]
        + ([pltpu.SemaphoreType.DMA((len(buffers), tiles + 1))] if buffers else []),
        compiler_params=pltpu.CompilerParams(vmem_limit_bytes=VMEM),
        cost_estimate=pl.CostEstimate(
            flops=int(micros * 1e9), bytes_accessed=int(micros * 1e6), transcendentals=0
        ),
        name=name,
    )(*inputs.values())
    return Bag(zip(outputs, results, strict=True))


def saved_shapes(stars, leaf_rows):
    rows = leaf_rows + stars
    return dict(
        kv=((leaf_rows, PAIR), BF),
        hb=((rows, D), BF),
        xh1=((rows, STEP_COLUMNS), BF),
        xh2=((rows, STEP_COLUMNS), BF),
        act=((rows, FF), BF),
        slope=((rows, FF), BF),
        s=((HP, leaf_rows), F32),
        qs=((stars, D), F32),
        kvc=((stars, PAIR), F32),
        o=((stars, D), F32),
        self=((stars, HP), F32),
        logt=((stars, HP), F32),
    )


def leaf_shapes(leaf_rows, *names):
    return {k: ((leaf_rows, D), BF) for k in names}


def ffn_scratch(stars, leaf_rows):
    rows = leaf_rows + stars
    return {"dn": ((4, 8, D), F32), "dbr": ((rows, STEP_COLUMNS), BF), "dpre": ((rows, FF), BF)}


def exchange(x, stage, value, sizes):
    axis, shift, bits = stage
    return lax.ppermute(x, axis, [(i, i ^ (value << shift)) for i in range(sizes[axis])])


def tree_stages(sizes, swap):
    bits = {axis: size.bit_length() - 1 for axis, size in sizes.items()}

    def cut(axis, start, stop):
        return [(axis, i, min(2, stop - i)) for i in range(start, stop, 2)]

    middle = [cut("leaf", 1, bits["leaf"]), cut("graph", 0, 1)]
    if swap:
        middle = middle[::-1]
    return [("leaf", 0, 1)] + middle[0] + middle[1] + cut("graph", 1, bits["graph"])


def tree_slot(relative, stages, leaf_bits):
    slot = jnp.zeros_like(relative)
    for axis, shift, bits in stages:
        shift = shift + (leaf_bits if axis == "graph" else 0)
        slot = (slot << bits) | ((relative >> shift) & ((1 << bits) - 1))
    return slot


def gather_step(held, stage, sizes):
    parts = [held] + [exchange(held, stage, v, sizes) for v in range(1, 1 << stage[2])]
    return jnp.concatenate(parts, axis=0)


def total(held, start, stop):
    return sum(x[at + start : at + stop].astype(F32) for x, at in held[0])


def reduce_step(held, stage, sizes):
    terms, rows = held
    count = rows >> stage[2]
    sent = [total(held, v * count, (v + 1) * count).astype(BF) for v in range(1, 1 << stage[2])]
    got = [(exchange(x, stage, v + 1, sizes), 0) for v, x in enumerate(sent)]
    return terms + got, count


def tie(helds, *others):
    newest, others = lax.optimization_barrier(([h[0][-1][0] for h in helds], others))
    return [
        (terms[:-1] + [(x, terms[-1][1])], rows)
        for (terms, rows), x in zip(helds, newest, strict=True)
    ], others


def to_rows(flat, rows):
    block = jnp.pad(flat.reshape(rows, D), ((0, 128 - rows), (0, 0)))
    tail = jnp.pad(block[:, 256:], ((0, 0), (0, 320 - D)))
    return jnp.concatenate(
        [block[:, :128], block[:, 128:256], jnp.concatenate([tail[:64], tail[64:]], axis=1)], axis=0
    )


def from_rows(packed, rows):
    tail = jnp.concatenate([packed[256:, : D - 256], packed[256:, 64 : D - 192]], axis=0)
    block = jnp.concatenate([packed[:128], packed[128:256], tail], axis=1)
    return block[:rows].reshape(-1)


def split_flat(vec):
    square = D * D
    wq, wk, wv, wo, we = (vec[i * square : (i + 1) * square].reshape(D, D) for i in range(5))
    at = 5 * square
    w1 = vec[at : at + D * FF].reshape(D, FF)
    at = at + D * FF
    w2 = vec[at : at + FF * D].reshape(FF, D)
    at = at + FF * D
    norm = jnp.pad(vec[at : at + 4 * D].reshape(4, D).astype(F32), ((0, 4), (0, 0)))
    wkv = jnp.concatenate([wk, jnp.zeros((D, STEP_COLUMNS - D), BF), wv], axis=1)
    return Bag(zip(WEIGHTS, (wq, wkv, wo, we, nn(wv, wo).astype(BF), w1, w2, norm), strict=True))


def halo(x):
    size = lax.axis_size("leaf")
    last, first = x
    left = lax.ppermute(last, "leaf", [(i, i + 1) for i in range(size - 1)])
    right = lax.ppermute(first, "leaf", [(i + 1, i) for i in range(size - 1)])
    return left, right


def local(
    weights,
    first_moment,
    second_moment,
    centers,
    leaves,
    edge_feats,
    center_cot,
    leaf_cot,
    edge_cot,
    graph_ids,
    star_sizes,
    leaf_mask,
    owner_list,
):
    sizes = {"graph": lax.axis_size("graph"), "leaf": lax.axis_size("leaf")}
    holders = sizes["graph"] * sizes["leaf"]
    block_len = weights.shape[1]
    block_rows = block_len // D
    in_rows = block_len % D == 0 and 64 < block_rows <= 128
    stars = centers.shape[1]
    own_rows = leaves.shape[1]
    leaf_rows = own_rows + 2 * HALO

    orders = [tree_stages(sizes, swap) for swap in (False, True)]
    me = lax.axis_index(("graph", "leaf"))
    leaf_bits = sizes["leaf"].bit_length() - 1
    slot = jnp.stack([tree_slot(owner_list ^ me, stages, leaf_bits) for stages in orders])
    nat_rows = ROWS_LAYER + 12
    nat = {"nat": ((3, nat_rows, 128), F32)}
    half = PACK // 2
    n_steps = len(orders[0])
    weights_low = weights.astype(BF)

    def gather_begin(rows):
        held = gather_step(jnp.concatenate(rows, axis=0)[None], orders[0][-1], sizes)
        size = rows[0].shape[0]
        return [held[:, :size], held[:, size:]]

    def gather_more(held, n):
        return [gather_step(h, o[n], sizes) for h, o in zip(held, orders, strict=True)]

    rows = [to_rows(x, block_rows) if in_rows else x for x in weights_low]
    held = gather_begin(rows)
    raw = dict(leaves=leaves[0], edges=edge_feats[0], lcot=leaf_cot[0], ecot=edge_cot[0])
    marks = jnp.pad((graph_ids + 1).astype(BF), ((0, 15), (0, 0)))
    marks = jnp.concatenate([marks[:8], jnp.broadcast_to(leaf_mask.astype(BF), (8, own_rows))], axis=0)

    def edge(cut):
        note = jnp.pad(marks[:, cut], ((0, 0), (0, D - HALO)))
        return jnp.concatenate([x[cut] for x in raw.values()] + [note], axis=0)

    left, right = halo((edge(slice(own_rows - HALO, own_rows)), edge(slice(0, HALO))))
    at = len(raw)
    raw, held = lax.optimization_barrier((raw, held))
    raw = dict(raw, halo_l=left, halo_r=right)

    def with_marks(line, mine):
        sides = [x[at * HALO + line, :HALO].astype(jnp.int32)[None] for x in (left, right)]
        return jnp.concatenate([sides[0], mine, sides[1]], axis=1)

    ids = with_marks(0, graph_ids + 1) - 1
    live = with_marks(8, leaf_mask).astype(F32)
    edge_id = jnp.full((1, 1), -1, jnp.int32)
    last = (ids != jnp.concatenate([ids[:, 1:], edge_id], axis=1)).astype(F32)
    first = graph_ids[0] != ids[0, HALO - 1 : HALO - 1 + own_rows]
    star_index = jnp.arange(stars, dtype=jnp.int32)
    star_own = jnp.any((star_index[:, None] == graph_ids) & first[None, :], axis=1)[:, None]
    scale = (jnp.log(star_sizes[0].astype(F32)) / (math.log(32.0) * math.sqrt(HEAD)))[:, None]
    base = Bag(
        idc=ids.reshape(-1, 1),
        idr=ids,
        live=live,
        last=last,
        scale=scale,
        cown=star_own.astype(F32),
    )
    saved = saved_shapes(stars, leaf_rows)
    rows = leaf_rows + stars
    if in_rows:
        grads_out = {k: ((holders, half, 128), BF) for k in ("keep", "send")}
        grads_scratch = {k: ((holders, half, 128), BF) for k in ("all_a", "all_b")} | nat
    else:
        grads_out, grads_scratch = nat, {}
    lazy = WEIGHTS[:-1] + tuple(f"{k}{i}" for k in WEIGHTS for i in range(LAYERS)) + ("yl0", "en0", "xl", "el", "gyl", "ge", "yl", "en") + (
        "kv", "hb", "xh1", "xh2", "act", "slope", "dz", "dkv", "gxl", "gel", "dbr", "dpre",
    )
    f_scratch = dict(cat=((2 * stars, PAIR), BF), z=((rows, D), F32))
    a_scratch = {"cat": ((2 * stars, PAIR + STEP_COLUMNS), BF), **leaf_shapes(leaf_rows, "mc", "m")}
    handed = dict(
        dz=((rows, D), BF),
        dkv=((leaf_rows, PAIR), BF),
        dq=((stars, D), BF),
        dkvc=((stars, PAIR), BF),
    )
    def halves_of(*names):
        return {k: raw[k] for k in (*names, "halo_l", "halo_r")}

    join = dict(xl=("leaves", 0), el=("edges", 1), gyl=("lcot", 2), ge=("ecot", 3))

    def joined(*names):
        return {k: join[k] for k in names}

    for n in range(n_steps - 2, 0, -1):
        held = gather_more(held, n)

    def end_grads(r):
        backward_attention(r, stars, leaf_rows)
        weight_grads(r, stars, leaf_rows, own_rows)
        if in_rows:
            pack_blocks(r, holders, block_rows)

    small = [k for k in saved if k not in lazy]

    def start_first(r):
        for copy in unpack_copies(r, 0, holders):
            copy.start()

    def front(r):
        zero = r.view({**{k: k + "0" for k in WEIGHTS}, "yl": "yl0", "en": "en0", "yc": "yc0"})
        names = {**{k: k + "1" for k in (*WEIGHTS, *small)}, "xl": "yl0", "el": "en0", "xc": "yc0"}
        one = r.view(names)
        one.update(dpre=r.slope, dbr=r.xh2)
        if in_rows:
            unpack_blocks(zero, 0, holders, block_rows)
            for copy in unpack_copies(r, 1, holders):
                copy.start()
        forward(zero, stars, leaf_rows)
        if in_rows:
            unpack_blocks(one, 1, holders, block_rows)
            one.update(all_a=r.got.at[:, : PACK // 2], all_b=r.got.at[:, PACK // 2 :])
        forward(one, stars, leaf_rows)
        backward_ffn(one, stars, leaf_rows, own_rows)
        end_grads(one)

    weight_specs = dict(zip(WEIGHTS, WEIGHT_SHAPES, strict=True))
    params, unpacked, kept, loose = [], {}, {}, {}
    for i, near in enumerate(held):
        far = exchange(near, orders[i][0], 1, sizes)
        if in_rows:
            loose.update({f"near{i}": near, f"far{i}": far})
            used = WEIGHTS if i == 0 else ("wq", "wkv", "we", "wvo")
            unpacked.update({f"{k}{i}": weight_specs[k] for k in used})
            kept.update({f"{k}{i}": weight_specs[k] for k in WEIGHTS if k not in used})
        else:
            flat = jnp.concatenate([near, far], axis=0)
            params.append(split_flat(jnp.take(flat, slot[i], axis=0).reshape(-1)))
    if in_rows:
        kept.update(got=((holders, PACK, 128), BF), sems=((2,), None))
        kept.update(nat)
    scratch = {**f_scratch, **a_scratch, "dn": ((4, 8, D), F32), **kept, **{k + "1": saved[k] for k in small}}
    scratch["z"] = ((rows, D), F32)
    two = call(
        front,
        {
            "slot": slot,
            **loose,
            **{f"{k}{i}": x[k] for i, x in enumerate(params) for k in WEIGHTS},
            **halves_of("leaves", "edges", "lcot", "ecot"),
            **base,
            "xc": centers[0],
            "gyc": center_cot[0],
        },
        {
            "yc0": ((stars, D), F32),
            "yc": ((stars, D), F32),
            **leaf_shapes(leaf_rows, "yl0", "en0"),
            **leaf_shapes(own_rows, "yl", "en"),
            **unpacked,
            **saved,
            **handed,
            **grads_out,
        },
        scratch,
        60,
        leaf_rows,
        in_smem=("slot",),
        lazy=lazy,
        joins=joined("xl", "el", "gyl", "ge"),
        own=("yl", "en"),
        name="front",
        loose=loose,
        early=start_first if in_rows else None,
    )
    one = two
    if in_rows:
        params = [Bag({k[:-1]: two[k] for k in unpacked if k[-1] == str(i)}) for i in range(LAYERS)]
    two_in = dict(xc=two.yc0, xl=two.yl0, el=two.en0, **halves_of("ecot"))

    def inputs_of(params, given, made, joins, out_rows, dtype, name):
        return call(
            lambda r: backward_inputs(r, stars, leaf_rows),
            {
                **{k: params[k] for k in ("wvo", "wkv", "we", "wq")},
                **{k: base[k] for k in ("idc", "idr")},
                **given,
                **{k: made[k] for k in handed},
            },
            {"gxc": ((stars, D), F32), "gxl": ((out_rows, D), dtype), "gel": ((out_rows, D), dtype)},
            {"xcat": ((2 * stars, D), BF)},
            9,
            leaf_rows,
            lazy=lazy,
            joins=joins,
            own=("gxl", "gel") if out_rows == own_rows else (),
            name=name,
            soon="ge",
        )

    def begin(made):
        if not in_rows:
            flat = jnp.swapaxes(made.nat[:, :ROWS_LAYER], 0, 1).reshape(ROWS_LAYER, 384)
            flat = flat[:, :D].reshape(holders, block_len)
            placed = jnp.zeros_like(flat).at[slot[0]].set(flat).astype(BF)
            return [reduce_step(([(placed, 0)], holders), orders[0][0], sizes)]
        got = exchange(made.send, orders[0][0], 1, sizes)
        count = holders // 2
        return [([(made.keep, i), (got, i)], count) for i in (0, count)]

    def advance(held, n):
        return [reduce_step(h, o[n], sizes) for h, o in zip(held, orders, strict=False)]

    def joined_total(held):
        rows = held[0][1]
        both = jnp.concatenate([total(h, 0, rows) for h in held], axis=1)
        return [([(both.astype(BF), 0)], rows)]

    def last_step(held):
        return reduce_step(held[0], orders[0][-1], sizes)

    def end(held):
        block = total(held, 0, 1)[0]
        return from_rows(block, block_rows) if in_rows else block

    held_two = begin(two)
    two_grads = inputs_of(params[1], two_in, two, joined("ge"), leaf_rows, BF, "last_inputs")
    held_two, (gyc,) = tie(held_two, two_grads.gxc)
    held_two = advance(held_two, 1)
    made = {"dz": handed["dz"], **ffn_scratch(stars, leaf_rows)}
    mid = call(
        lambda r: backward_ffn(r, stars, leaf_rows, own_rows),
        {
            "w2": params[0].w2,
            "gyl": two_grads.gxl,
            **{k: one[k] for k in ("xh2", "slope")},
            "w1": params[0].w1,
            "xh1": one.xh1,
            "norm": params[0].norm,
            "cown": base.cown,
            "gyc": gyc,
        },
        made,
        {},
        13,
        leaf_rows,
        lazy=lazy,
        name="first_ffn",
        soon="gyl",
    )
    held_two, (dn,) = tie(held_two, mid.dn)
    if n_steps > 2:
        held_two = advance(held_two, 2)
    ffn_names = ("xh2", "slope", "xh1")
    three = call(
        end_grads,
        {
            **{k: params[0][k] for k in ("wo", "wkv")},
            **mid,
            **{k: one[k] for k in saved if k not in ffn_names},
            **halves_of("leaves", "edges"),
            **base,
            "slot": slot,
            "xc": centers[0],
            "ge": two_grads.gel,
            "dn": dn,
        },
        {**{k: handed[k] for k in handed if k != "dz"}, **grads_out},
        {**a_scratch, **grads_scratch},
        18,
        leaf_rows,
        in_smem=("slot",),
        lazy=lazy,
        joins=joined("xl", "el"),
        name="first",
    )
    three["dz"] = mid.dz
    for n in range(3, n_steps - 1):
        held_two = advance(held_two, n)
    key = "send" if in_rows else "nat"
    held_two, (three[key],) = tie(held_two, three[key])
    held_three = begin(three)
    held_two = joined_total(held_two)
    count = len(held_two)
    both, (dq,) = tie(held_two + held_three, three.dq)
    held_three = both[count:]
    last_two = last_step(both[:count])
    handed_three = {**{k: three[k] for k in handed}, "dq": dq}
    held_three = advance(held_three, 1)
    three_in = dict(xc=centers[0], ge=two_grads.gel, **halves_of("leaves", "edges"))
    three_grads = inputs_of(
        params[0], three_in, handed_three, joined("xl", "el"), own_rows, F32, "first_inputs"
    )
    late = [x for x, _ in last_two[0][1:]]
    held_three, (gxc, yc, *late) = tie(held_three, three_grads.gxc, two.yc, *late)
    last_two = (last_two[0][:1] + [(x, 0) for x in late], last_two[1])
    center_rows = jnp.where(star_own, jnp.concatenate([yc, gxc], axis=1), 0.0)
    center_rows = center_rows + exchange(center_rows, ("leaf", 0, 1), 1, sizes)
    held_three = advance(held_three, 2) if n_steps > 3 else held_three
    for n in range(3, n_steps - 1):
        held_three = advance(held_three, n)
    held_three, (gxl, gel, yl, en, center_rows) = tie(
        held_three, three_grads.gxl, three_grads.gel, two.yl, two.en, center_rows
    )
    for bit in range(1, leaf_bits):
        center_rows = center_rows + exchange(center_rows, ("leaf", bit, 1), 1, sizes)
    centers_out, grad_centers = center_rows[:, :D].astype(BF), center_rows[:, D:]
    lasts, _ = tie([last_step(joined_total(held_three)), last_two])
    grad_total = jnp.stack([end(x) for x in lasts])
    first_new = BETA_ONE * first_moment + (1.0 - BETA_ONE) * grad_total
    second_new = BETA_TWO * second_moment + (1.0 - BETA_TWO) * grad_total * grad_total
    step_one = first_new / (1.0 - BETA_ONE**STEP)
    step_two = second_new / (1.0 - BETA_TWO**STEP)
    weights_new = weights - RATE * (step_one / (jnp.sqrt(step_two) + EPS_ADAM) + DECAY * weights)
    return (
        centers_out[None],
        yl[None],
        en[None],
        grad_centers[None],
        gxl[None],
        gel[None],
        first_new,
        second_new,
        weights_new,
        weights_new.astype(BF),
        grad_total,
    )


def solution(mesh):
    both = ("graph", "leaf")
    return jax.shard_map(
        local,
        mesh=mesh,
        in_specs=(
            P(None, both),
            P(None, both),
            P(None, both),
            P("graph", None, None),
            P("graph", "leaf", None),
            P("graph", "leaf", None),
            P("graph", None, None),
            P("graph", "leaf", None),
            P("graph", "leaf", None),
            P("graph", "leaf"),
            P("graph", None),
            P("graph", "leaf"),
            P(),
        ),
        out_specs=(
            P("graph", None, None),
            P("graph", "leaf", None),
            P("graph", "leaf", None),
            P("graph", None, None),
            P("graph", "leaf", None),
            P("graph", "leaf", None),
            P(None, both),
            P(None, both),
            P(None, both),
            P(None, both),
            P(None, both),
        ),
        check_vma=False,
    )
```

```python
import math

import jax
import jax.numpy as jnp
from jax import lax
from jax.experimental import pallas as pl
from jax.experimental.pallas import tpu as pltpu
from jax.sharding import PartitionSpec as P

D = 300
HEADS = 12
HEAD = 25
FF = 1200
LAYERS = 2
STEP = 5
ROWS_LAYER = 5 * D + 2 * FF + 4

NEG = -1e30
EPS_NORM = 1e-05
BETA_ONE = 0.9
BETA_TWO = 0.999
RATE = 0.05
DECAY = 0.01
EPS_ADAM = 1e-08
INV_ROOT_TWO = 0.7071067811865476
INV_ROOT_TWO_PI = 0.3989422804014327

HALO = 128
TILE = 320
WIDE = 2
FFN_WIDE = 1
HP = 16
PACK = 320
CHUNKS = tuple((i, min(i + 256, FF)) for i in range(0, FF, 256))
VMEM = 60 << 20
F32 = jnp.float32
BF = jnp.bfloat16

STEP_COLUMNS = 384
PAIR = STEP_COLUMNS + D

WEIGHTS = ("wq", "wkv", "wo", "we", "wvo", "w1", "w2", "norm")
WEIGHT_SHAPES = (
    ((D, D), BF),
    ((D, PAIR), BF),
    ((D, D), BF),
    ((D, D), BF),
    ((D, D), BF),
    ((D, FF), BF),
    ((FF, D), BF),
    ((8, D), F32),
)


def nn(a, b):
    return lax.dot_general(a, b, (((1,), (0,)), ((), ())), preferred_element_type=F32)


def nt(a, b):
    return lax.dot_general(a, b, (((1,), (1,)), ((), ())), preferred_element_type=F32)


def tn(a, b):
    return lax.dot_general(a, b, (((0,), (0,)), ((), ())), preferred_element_type=F32)


def halves(x):
    high = x.astype(BF)
    return high, (x - high.astype(F32)).astype(BF)


def thirds(x):
    high = x.astype(BF)
    rest = x - high.astype(F32)
    mid = rest.astype(BF)
    return high, mid, (rest - mid.astype(F32)).astype(BF)


def stacked(parts, axis=0):
    return jnp.concatenate([p.astype(F32) for p in parts], axis=axis).astype(BF)


def side_by_side(*parts):
    zeros = jnp.zeros((parts[0].shape[0], STEP_COLUMNS - D), F32)
    pieces = [parts[0]]
    for part in parts[1:]:
        pieces += [zeros, part]
    return jnp.concatenate(pieces, axis=1)


def column(values, i):
    return values[:, i * STEP_COLUMNS : i * STEP_COLUMNS + D]


def table(rows, repeat=1):
    head = lax.broadcasted_iota(jnp.int32, (repeat * rows, D), 0) % rows
    feature = lax.broadcasted_iota(jnp.int32, (repeat * rows, D), 1)
    low = head * HEAD
    return jnp.where((feature >= low) & (feature < low + HEAD), 1.0, 0.0).astype(BF)


def head_sum(values):
    high, low = halves(values)
    tab = table(HP)
    return nt(high, tab) + nt(low, tab)


def head_sum_t(values):
    high, low = halves(values)
    tab = table(HP)
    return nt(tab, high) + nt(tab, low)


def spread(values):
    high, low = halves(values)
    tab = table(HP)
    return nn(high, tab) + nn(low, tab)


def spread_t(values):
    return tn(stacked(halves(values)), table(HP, 2))


def onehot_col(ids, stars, repeat):
    lane = lax.broadcasted_iota(jnp.int32, (ids.shape[0], repeat * stars), 1)
    hit = lane == ids
    for i in range(1, repeat):
        hit = hit | (lane == ids + i * stars) & (ids >= 0)
    return jnp.where(hit, 1.0, 0.0).astype(BF)


def onehot_row(ids, stars, repeat):
    sub = lax.broadcasted_iota(jnp.int32, (repeat * stars, ids.shape[1]), 0)
    hit = sub == ids
    for i in range(1, repeat):
        hit = hit | (sub == ids + i * stars) & (ids >= 0)
    return jnp.where(hit, 1.0, 0.0).astype(BF)


def row_mean(x):
    return jnp.sum(x, axis=-1, keepdims=True) * (1.0 / D)


def normalized(x):
    dev = x - row_mean(x)
    inverse = lax.rsqrt(row_mean(dev * dev) + EPS_NORM)
    return dev * inverse, inverse


def norm_back(grad, scaled, inverse):
    return inverse * (grad - row_mean(grad) - scaled * row_mean(grad * scaled))


def put_normalized(ref, rows, scaled, inverse):
    ref[rows, 0:D] = scaled.astype(BF)
    high, low = halves(inverse)
    ref[rows, D : D + 1] = high
    ref[rows, D + 1 : D + 2] = low


def get_normalized(ref, rows):
    inverse = ref[rows, D : D + 1].astype(F32) + ref[rows, D + 1 : D + 2].astype(F32)
    return ref[rows, 0:D].astype(F32), inverse


def ffn_forward(r, z, rows):
    norm = r.norm
    g1, b1, g2, b2 = (norm[i : i + 1, :] for i in range(4))
    xh1, inv1 = normalized(z)
    h = xh1 * g1 + b1
    hb = h.astype(BF)
    r.hb[rows, :] = hb
    put_normalized(r.xh1, rows, xh1, inv1)
    total = h
    for lo, hi in CHUNKS:
        pre = nn(hb, r.w1[:, lo:hi])
        cdf = 0.5 * (1.0 + lax.erf(pre * INV_ROOT_TWO))
        act = (pre * cdf).astype(BF)
        r.act[rows, lo:hi] = act
        r.slope[rows, lo:hi] = (
            cdf + pre * jnp.exp(-0.5 * pre * pre) * INV_ROOT_TWO_PI
        ).astype(BF)
        total = total + nn(act, r.w2[lo:hi, :])
    xh2, inv2 = normalized(total)
    put_normalized(r.xh2, rows, xh2, inv2)
    return xh2 * g2 + b2


def fold(x):
    return jnp.sum(x.reshape(x.shape[0] // 8, 8, x.shape[1]), axis=0)


def ffn_backward(r, gy, rows, weight):
    norm = r.norm
    g1, g2 = norm[0:1, :], norm[2:3, :]
    xh2, inv2 = get_normalized(r.xh2, rows)
    gw = gy * weight
    r.dn[2] += fold(gw * xh2)
    r.dn[3] += fold(gw)
    mid = norm_back(gy * g2, xh2, inv2)
    branch = mid.astype(BF)
    r.dbr[rows, 0:D] = (mid * weight).astype(BF)
    total = mid
    for lo, hi in CHUNKS:
        dact = nt(branch, r.w2[lo:hi, :])
        dpre = dact * r.slope[rows, lo:hi].astype(F32)
        low = dpre.astype(BF)
        r.dpre[rows, lo:hi] = (dpre * weight).astype(BF)
        total = total + nt(low, r.w1[:, lo:hi])
    xh1, inv1 = get_normalized(r.xh1, rows)
    gw = total * weight
    r.dn[0] += fold(gw * xh1)
    r.dn[1] += fold(gw)
    return norm_back(total * g1, xh1, inv1)


def forward(r, stars, leaf_rows):
    xc = r.xc[...].astype(F32)
    low = xc.astype(BF)
    r.wait("wq", "wkv", "wo", "we", "wvo")
    r.settle("kv")
    qs = nn(low, r.wq[...]) * r.scale[...]
    kvc = nn(low, r.wkv[...])
    own_score = head_sum(qs * column(kvc, 0))
    r.qs[...] = qs
    r.kvc[...] = kvc
    r.self[...] = own_score
    r.cat[:, 0:PAIR] = stacked(halves(side_by_side(qs, xc)))

    def tile(start, size, rows, carry):
        el = r.el[rows, :]
        ew = el.astype(F32)
        xl = r.xl[rows, :].astype(F32)
        r.en[rows, :] = nn(el, r.we[...]).astype(BF)
        from_star = nn(onehot_col(r.idc[rows, :], stars, 2), r.cat[:, 0:PAIR])
        kv = nn((xl * ew).astype(BF), r.wkv[...])
        r.kv[rows, :] = kv.astype(BF)
        r.s[:, rows] = head_sum_t(column(from_star, 0) * column(kv, 0))
        mc = (column(from_star, 1) * ew).astype(BF)
        r.z[rows, :] = xl + nn(mc, r.wvo[...])
        return carry

    def ffn_tile(start, size, rows, carry):
        if start == 0:
            r.wait("w1", "w2")
            r.settle(*made)
        if start + size == leaf_rows:
            r.z[leaf_rows:, :] = xc + attend(r, stars, leaf_rows, own_score, column(kvc, 1))
        y = ffn_forward(r, r.z[rows, :], rows)
        r.yl[start : start + size, :] = y[:size].astype(r.yl.dtype)
        if start + size == leaf_rows:
            r.yc[...] = y[size:]
        return carry

    made = ("yl", "hb", "xh1", "xh2", "act", "slope")
    r.loop(("xl", "el"), ("en", "kv"), tile, 0)
    r.loop((), made, ffn_tile, 0, stars, FFN_WIDE)
    r.finish("en", "kv", *made)


def attend(r, stars, leaf_rows, own_score, vc):
    ids = r.idr[...]
    live = r.live[...] > 0.5
    score = r.s[...]
    top = jnp.where(live, score, NEG)
    lane = lax.broadcasted_iota(jnp.int32, (1, leaf_rows), 1)
    shift = 1
    while shift < 128:
        same = (pltpu.roll(ids, shift, 1) == ids) & (lane >= shift)
        top = jnp.maximum(top, jnp.where(same, pltpu.roll(top, shift, 1), NEG))
        shift *= 2
    hot_row = onehot_row(ids, stars, 1)
    last = hot_row.astype(F32) * r.last[...]
    present = jnp.sum(last, axis=1, keepdims=True) > 0.5
    last = last.astype(BF)
    star_top = sum(nt(last, part) for part in thirds(top))
    peak = jnp.where(present, jnp.maximum(star_top, own_score), own_score)
    peak_row = tn(stacked(thirds(peak)), onehot_row(ids, stars, 3))
    e = jnp.where(live, jnp.exp(jnp.where(live, score - peak_row, 0.0)), 0.0)
    self_weight = jnp.exp(own_score - peak)
    total = self_weight + sum(nt(hot_row, part) for part in halves(e))
    r.logt[...] = peak + jnp.log(total)
    weighted = (spread_t(e) * column(r.kv, 1).astype(F32)).astype(BF)
    o = (nn(hot_row, weighted) + spread(self_weight) * vc) / spread(total)
    r.o[...] = o
    return nn(o.astype(BF), r.wo[...])


def backward_ffn(r, stars, leaf_rows, own_rows):
    r.dn[...] = jnp.zeros_like(r.dn)
    r.wait("w2", "w1")

    def tile(start, size, rows, carry):
        row = lax.broadcasted_iota(jnp.int32, (size, 1), 0) + start
        mine = jnp.where((row >= HALO) & (row < HALO + own_rows), 1.0, 0.0)
        gy = r.gyl[start : start + size, :].astype(F32)
        if start + size == leaf_rows:
            gy = jnp.concatenate([gy, r.gyc[...].astype(F32)], axis=0)
            mine = jnp.concatenate([mine, r.cown[...]], axis=0)
        r.dz[rows, :] = ffn_backward(r, gy, rows, mine).astype(BF)
        return carry

    made = ("dz", "dbr", "dpre")
    r.loop(("gyl", "xh2", "slope", "xh1"), made, tile, 0, stars, FFN_WIDE)
    r.finish(*made)


def backward_attention(r, stars, leaf_rows):
    r.wait("wo")
    r.arrive_rest("dz")
    do = nt(r.dz[leaf_rows:, :], r.wo[...])
    kvc = r.kvc[...]
    kc, vc = column(kvc, 0), column(kvc, 1)
    qs = r.qs[...]
    xc = r.xc[...].astype(F32)
    r.cat[...] = stacked(halves(side_by_side(qs, xc, do)))
    delta = head_sum(do * r.o[...])
    self_p = jnp.exp(r.self[...] - r.logt[...])
    d_self = self_p * (head_sum(do * vc) - delta)
    coef_c = spread(d_self)
    r.dkvc[...] = side_by_side(coef_c * qs, spread(self_p) * do).astype(BF)
    logt_parts = stacked(thirds(r.logt[...]))
    delta_parts = stacked(thirds(delta))

    def tile(start, size, rows, total):
        el = r.el[rows, :].astype(F32)
        ids_row = r.idr[:, rows]
        hot3 = onehot_row(ids_row, stars, 3)
        from_star = nn(onehot_col(r.idc[rows, :], stars, 2), r.cat[...])
        r.mc[rows, :] = (column(from_star, 1) * el).astype(BF)
        live = r.live[:, rows] > 0.5
        score = r.s[:, rows] - tn(logt_parts, hot3)
        p = jnp.where(live, jnp.exp(jnp.where(live, score, 0.0)), 0.0)
        dor = column(from_star, 2)
        kv = r.kv[rows, :]
        ds = p * (head_sum_t(dor * column(kv, 1).astype(F32)) - tn(delta_parts, hot3))
        coef = spread_t(ds)
        r.dkv[rows, :] = side_by_side(coef * column(from_star, 0), spread_t(p) * dor).astype(BF)
        r.m[rows, :] = (r.xl[rows, :].astype(F32) * el).astype(BF)
        part = (coef * column(kv, 0).astype(F32)).astype(BF)
        return total + nn(onehot_row(ids_row, stars, 1), part)

    zero = jnp.zeros((stars, D), F32)
    total = r.loop(("el", "kv", "xl", "dz"), ("dkv",), tile, zero)
    r.dq[...] = ((total + coef_c * kc) * r.scale[...]).astype(BF)
    r.finish("dkv")


def weight_grads(r, stars, leaf_rows, own_rows):
    own = r.cown[...]
    own_leaf = slice(HALO, HALO + own_rows)
    r.wait("wkv")
    r.arrive("dz", "ge", "hb", "dpre", "act", "dbr")
    nat = r.nat
    xb = r.xc[...].astype(BF)
    dq, dkvc, dac = (
        (x.astype(F32) * own).astype(BF) for x in (r.dq[...], r.dkvc[...], r.dz[leaf_rows:, :])
    )
    nat_store(nat, pl.ds(0, D), tn(xb, dq))
    pair = tn(r.m[own_leaf, :], r.dkv[own_leaf, :]) + tn(xb, dkvc)
    both = tn(r.mc[own_leaf, :], r.dz[own_leaf, :]).astype(BF)
    nat_store(nat, pl.ds(D, D), column(pair, 0))
    nat_store(nat, pl.ds(2 * D, D), column(pair, 1) + nt(both, r.wo[...]))
    out = tn(column(r.wkv, 1), both) + tn(r.o[...].astype(BF), dac)
    nat_store(nat, pl.ds(3 * D, D), out)
    nat_store(nat, pl.ds(4 * D, D), tn(r.el[own_leaf, :], r.ge[own_leaf, :]))
    base = 5 * D
    whole = tn(r.hb[HALO:, :], r.dpre[HALO:, :])
    for j in range(FF // D):
        part = whole[:, j * D : (j + 1) * D]
        nat_store(nat, pl.ds(base + j, D, stride=FF // D), part)
    base = base + FF
    for lo, hi in CHUNKS:
        part = tn(r.dbr[HALO:, 0:D], r.act[HALO:, lo:hi]).T
        nat_store(nat, pl.ds(base + lo, hi - lo), part)
    base = base + FF
    sums = [jnp.sum(r.dn[i], axis=0, keepdims=True) for i in range(4)]
    nat_store(nat, pl.ds(base, 4), jnp.concatenate(sums, axis=0))


def backward_inputs(r, stars, leaf_rows):
    r.wait("wq", "wkv", "wvo", "we")
    xc = r.xc[...].astype(F32)
    r.xcat[...] = stacked(halves(xc))

    def tile(start, size, rows, total):
        dz = r.dz[rows, :]
        dmc = nt(dz, r.wvo[...])
        el = r.el[rows, :].astype(F32)
        hot = onehot_col(r.idc[rows, :], stars, 2)
        dm = nt(r.dkv[rows, :], r.wkv[...])
        r.gxl[rows, :] = (dz.astype(F32) + dm * el).astype(r.gxl.dtype)
        de = dmc * nn(hot, r.xcat[...]) + dm * r.xl[rows, :].astype(F32)
        de = de + nt(r.ge[rows, :], r.we[...])
        r.gel[rows, :] = de.astype(r.gel.dtype)
        return total + nn(onehot_row(r.idr[:, rows], stars, 1), (dmc * el).astype(BF))

    zero = jnp.zeros((stars, D), F32)
    total = r.loop(("dz", "el", "dkv", "xl", "ge"), ("gxl", "gel"), tile, zero)
    r.arrive("dz")
    r.gxc[...] = (
        r.dz[leaf_rows:, :].astype(F32)
        + nt(r.dq[...], r.wq[...])
        + nt(r.dkvc[...], r.wkv[...])
        + total
    )
    r.finish("gxl", "gel")


def nat_load(nat, at):
    return jnp.concatenate([nat[c, at, :] for c in range(3)], axis=1)[:, :D]


def nat_store(nat, at, value):
    nat[0, at, :] = value[:, 0:128]
    nat[1, at, :] = value[:, 128:256]
    rest = jnp.zeros((value.shape[0], 384 - D), F32)
    nat[2, at, :] = jnp.concatenate([value[:, 256:D], rest], axis=1)


def pack_blocks(r, holders, rows):
    nat = r.nat
    lane = lax.broadcasted_iota(jnp.int32, (64, 128), 1)
    half = holders // 2
    for b in range(holders):
        top = b * rows
        at = r.slot[0, b]
        r.all_a[at, 0:128, :] = nat[0, top : top + 128, :].astype(BF)
        r.all_a[at, 128:160, :] = nat[1, top : top + 32, :].astype(BF)
        at = r.slot[1, b]
        r.all_b[at, 0:96, :] = nat[1, top + 32 : top + 128, :].astype(BF)
        high = pltpu.roll(nat[2, top + 64 : top + 128, :], 64, 1)
        tail = jnp.where(lane < 64, nat[2, top : top + 64, :], high)
        r.all_b[at, 96:160, :] = tail.astype(BF)
    for i, name in enumerate(("all_a", "all_b")):
        r.keep[i * half : (i + 1) * half] = r[name][:half]
        r.send[i * half : (i + 1) * half] = r[name][half:]


def unpack_copies(r, layer, holders):
    half = holders // 2
    return [
        pltpu.make_async_copy(r[f"{k}{layer}"], r.got.at[pl.ds(i * half, half)], r.sems.at[i])
        for i, k in enumerate(("near", "far"))
    ]


def unpack_blocks(r, layer, holders, rows):
    nat = r.nat
    for copy in unpack_copies(r, layer, holders):
        copy.wait()

    for b in range(holders):
        top = b * rows
        got = r.got[r.slot[layer, b]].astype(F32)
        nat[0, top : top + rows, :] = got[:rows]
        nat[1, top : top + rows, :] = got[128 : 128 + rows]
        tail = got[256:]
        nat[2, top : top + 64, :] = tail
        nat[2, top + 64 : top + rows, :] = pltpu.roll(tail, 64, 1)[: rows - 64]
    wq, wk, wv, wo, we = (nat_load(nat, pl.ds(i * D, D)).astype(BF) for i in range(5))
    put_squares(r, wq, wk, wv, wo, we)
    base = 5 * D
    for j in range(FF // D):
        part = nat_load(nat, pl.ds(base + j, D, stride=FF // D))
        r.w1[:, j * D : (j + 1) * D] = part.astype(BF)
    base = base + FF
    r.w2[...] = nat_load(nat, pl.ds(base, FF)).astype(BF)
    base = base + FF
    r.norm[...] = nat_load(nat, pl.ds(base, 8))
    r.finish(*WEIGHTS)


def put_squares(r, wq, wk, wv, wo, we):
    r.wq[...] = wq
    r.wkv[...] = side_by_side(wk.astype(F32), wv.astype(F32)).astype(BF)
    r.wo[...] = wo
    r.we[...] = we
    r.wvo[...] = nn(wv, wo).astype(BF)


class Bag(dict):
    def __getattr__(self, name):
        return self[name]


class Refs(Bag):
    def __init__(self, refs, leaf_rows):
        super().__init__(refs)
        state = dict(tiles=leaf_rows // TILE, alias={}, coming={}, going={}, pending=[])
        self.__dict__.update(state)

    def view(self, alias):
        other = Refs({**self, **{k: self[v] for k, v in alias.items()}}, self.tiles * TILE)
        state = dict(alias=alias, coming=self.coming, going=self.going, pending=self.pending)
        other.__dict__.update(state)
        return other

    def keys_of(self, names):
        return [self.alias.get(k, k) for k in names]

    def wait(self, *names):
        for name in self.keys_of(names):
            for copy in self.coming.pop(name, ()):
                copy.wait()

    def arrive(self, *names):
        for name in self.keys_of(names):
            if name in self.coming:
                for copy in self.coming.pop(name)["all"]():
                    copy.wait()

    def arrive_rest(self, name):
        (name,) = self.keys_of([name])
        if name in self.coming:
            for copy in self.coming[name]["rest"]():
                copy.wait()
            self.coming[name]["all"] = self.coming[name]["every"]
            self.coming[name]["rest"] = list

    def loop(self, names, made, body, carry, more=0, group=WIDE):
        coming = [self.coming[k] for k in self.keys_of(names) if "tile" in self.coming.get(k, ())]
        going = [self.going[k] for k in self.keys_of(made) if k in self.going]
        for first in range(0, self.tiles, group):
            stop = min(first + group, self.tiles)
            extra = more if stop == self.tiles else 0
            for k in coming:
                for t in range(first, stop):
                    k["tile"](t, t * TILE).wait()
            if extra:
                for name in names:
                    self.arrive_rest(name)
            start, size = first * TILE, (stop - first) * TILE
            carry = body(start, size, pl.ds(start, size + extra), carry)
            for t in range(first, stop):
                for k in going:
                    k["tile"](t, t * TILE)
        for k in coming:
            k["all"] = k["rest"]
            del k["tile"]
        return carry

    def finish(self, *names):
        for name in self.keys_of(names):
            if name in self.going:
                self.pending += [(name, copy) for copy in self.going.pop(name)["rest"]()]

    def settle(self, *names):
        for name, copy in self.pending:
            if name in names:
                copy.wait()
        self.pending[:] = [x for x in self.pending if x[0] not in names]


LATER = ("gyl", "ge", "hb", "dpre", "act", "dbr")


def call(body, inputs, outputs, scratch, micros, leaf_rows=TILE, lazy=(), joins=(), own=(), in_smem=(), name=None, loose=(), early=None, soon=None):
    joins = dict(joins)
    tiles = leaf_rows // TILE
    raw = {k for k, _ in joins.values()} | ({"halo_l", "halo_r"} if joins else set())
    raw |= set(loose)
    lazy_in = [k for k in inputs if k in lazy and k not in raw] + list(joins)
    buffers = {}
    for k in lazy_in:
        source = inputs[joins[k][0]] if k in joins else inputs[k]
        rows = leaf_rows if k in joins else source.shape[0]
        buffers[k] = ((rows,) + source.shape[1:], source.dtype)
    lazy_out = [k for k in outputs if k in lazy]
    for k in lazy_out:
        shape, dtype = outputs[k]
        buffers[k] = ((leaf_rows,) + shape[1:] if k in own else shape, dtype)
    names = list(inputs) + list(outputs) + list(scratch)

    def kernel(*refs):
        outer = dict(zip(names, refs, strict=False))
        rest = refs[len(names) :]
        held = dict(zip(buffers, rest, strict=False))
        sems = rest[-1] if buffers else None
        r = Refs({**outer, **held}, leaf_rows)
        copy = pltpu.make_async_copy
        if early is not None:
            early(r)
        for i, k in enumerate(buffers):
            inner, total = held[k], buffers[k][0][0]
            if k in lazy_out:
                target = outer[k]
                if k in own or total < leaf_rows:
                    cut = pl.ds(HALO, leaf_rows - 2 * HALO) if k in own else pl.ds(0, total)

                    def last(inner=inner, target=target, cut=cut, i=i):
                        one = copy(inner.at[cut], target, sems.at[i, tiles])
                        one.start()
                        return [one]

                    def per_tile(t, start):
                        return None

                else:

                    def per_tile(t, start, inner=inner, target=target, i=i):
                        rows = pl.ds(start, TILE)
                        copy(inner.at[rows], target.at[rows], sems.at[i, t]).start()

                    def last(inner=inner, target=target, i=i, total=total):
                        done = [
                            copy(inner.at[pl.ds(t * TILE, TILE)], target.at[pl.ds(t * TILE, TILE)], sems.at[i, t])
                            for t in range(tiles)
                        ]
                        if total > leaf_rows:
                            rows = pl.ds(leaf_rows, total - leaf_rows)
                            done.append(copy(inner.at[rows], target.at[rows], sems.at[i, tiles]))
                            done[-1].start()
                        return done

                r.going[k] = {"tile": per_tile, "rest": last}
            elif total < leaf_rows or k in WEIGHTS or k[:-1] in WEIGHTS:
                one = copy(outer[k], inner, sems.at[i, 0])
                one.start()
                r.coming[k] = [one]
            else:

                def wait_for(t, start, inner=inner, i=i):
                    rows = inner.at[pl.ds(start, TILE)]
                    return copy(rows, rows, sems.at[i, t])

                def behind(inner=inner, i=i, total=total):
                    if total == leaf_rows:
                        return []
                    rows = inner.at[pl.ds(leaf_rows, total - leaf_rows)]
                    return [copy(rows, rows, sems.at[i, tiles])]

                def every(wait_for=wait_for):
                    return [wait_for(t, t * TILE) for t in range(tiles)]

                def whole(every=every, behind=behind):
                    return every() + behind()

                r.coming[k] = {"tile": wait_for, "rest": behind, "every": every, "all": whole}
        order = [
            (t, i, k)
            for later in (False, True)
            for t in ([tiles, *range(tiles)] if "dz" in inputs else range(tiles + 1))
            for i, k in enumerate(buffers)
            if (k in LATER and k != soon) == later
        ]
        for t, i, k in order:
            if k not in lazy_out and isinstance(r.coming.get(k), dict):
                inner, total = held[k], buffers[k][0][0]
                low, high = t * TILE, min((t + 1) * TILE, leaf_rows)
                if t == tiles:
                    high = total
                if k in joins:
                    source, place = joins[k]
                    stop = leaf_rows - HALO
                    pieces = [
                        (outer["halo_l"], place * HALO, 0, HALO),
                        (outer[source], 0, HALO, stop),
                        (outer["halo_r"], place * HALO, stop, leaf_rows),
                    ]
                else:
                    pieces = [(outer[k], 0, 0, total)]
                for ref, offset, first, stop in pieces:
                    a, b = max(first, low), min(stop, high)
                    if a < b:
                        piece = ref.at[pl.ds(a - first + offset, b - a)]
                        copy(piece, inner.at[pl.ds(a, b - a)], sems.at[i, t]).start()
        body(r)
        for k in list(r.coming):
            if isinstance(r.coming[k], dict):
                r.arrive(k)
            else:
                r.wait(k)
        r.finish(*list(r.going))
        for _, one in r.pending:
            one.wait()

    vmem = pl.BlockSpec(memory_space=pltpu.VMEM)
    smem = pl.BlockSpec(memory_space=pltpu.SMEM)
    anywhere = pl.BlockSpec(memory_space=pl.ANY)

    def place(k):
        return smem if k in in_smem else anywhere if k in lazy or k in raw else vmem

    results = pl.pallas_call(
        kernel,
        out_shape=[jax.ShapeDtypeStruct(s, d) for s, d in outputs.values()],
        in_specs=[place(k) for k in inputs],
        out_specs=[place(k) for k in outputs],
        scratch_shapes=[
            pltpu.SemaphoreType.DMA(s) if d is None else pltpu.VMEM(s, d) for s, d in scratch.values()
        ]
        + [pltpu.VMEM(s, d) for s, d in buffers.values()]
        + ([pltpu.SemaphoreType.DMA((len(buffers), tiles + 1))] if buffers else []),
        compiler_params=pltpu.CompilerParams(vmem_limit_bytes=VMEM),
        cost_estimate=pl.CostEstimate(
            flops=int(micros * 1e9), bytes_accessed=int(micros * 1e6), transcendentals=0
        ),
        name=name,
    )(*inputs.values())
    return Bag(zip(outputs, results, strict=True))


def saved_shapes(stars, leaf_rows):
    rows = leaf_rows + stars
    return dict(
        kv=((leaf_rows, PAIR), BF),
        hb=((rows, D), BF),
        xh1=((rows, STEP_COLUMNS), BF),
        xh2=((rows, STEP_COLUMNS), BF),
        act=((rows, FF), BF),
        slope=((rows, FF), BF),
        s=((HP, leaf_rows), F32),
        qs=((stars, D), F32),
        kvc=((stars, PAIR), F32),
        o=((stars, D), F32),
        self=((stars, HP), F32),
        logt=((stars, HP), F32),
    )


def leaf_shapes(leaf_rows, *names):
    return {k: ((leaf_rows, D), BF) for k in names}


def ffn_scratch(stars, leaf_rows):
    rows = leaf_rows + stars
    return {"dn": ((4, 8, D), F32), "dbr": ((rows, STEP_COLUMNS), BF), "dpre": ((rows, FF), BF)}


def exchange(x, stage, value, sizes):
    axis, shift, bits = stage
    return lax.ppermute(x, axis, [(i, i ^ (value << shift)) for i in range(sizes[axis])])


def tree_stages(sizes, swap):
    bits = {axis: size.bit_length() - 1 for axis, size in sizes.items()}

    def cut(axis, start, stop):
        return [(axis, i, min(2, stop - i)) for i in range(start, stop, 2)]

    middle = [cut("leaf", 1, bits["leaf"]), cut("graph", 0, 1)]
    if swap:
        middle = middle[::-1]
    return [("leaf", 0, 1)] + middle[0] + middle[1] + cut("graph", 1, bits["graph"])


def tree_slot(relative, stages, leaf_bits):
    slot = jnp.zeros_like(relative)
    for axis, shift, bits in stages:
        shift = shift + (leaf_bits if axis == "graph" else 0)
        slot = (slot << bits) | ((relative >> shift) & ((1 << bits) - 1))
    return slot


def gather_step(held, stage, sizes):
    parts = [held] + [exchange(held, stage, v, sizes) for v in range(1, 1 << stage[2])]
    return jnp.concatenate(parts, axis=0)


def total(held, start, stop):
    return sum(x[at + start : at + stop].astype(F32) for x, at in held[0])


def reduce_step(held, stage, sizes):
    terms, rows = held
    count = rows >> stage[2]
    sent = [total(held, v * count, (v + 1) * count).astype(BF) for v in range(1, 1 << stage[2])]
    got = [(exchange(x, stage, v + 1, sizes), 0) for v, x in enumerate(sent)]
    return terms + got, count


def tie(helds, *others):
    newest, others = lax.optimization_barrier(([h[0][-1][0] for h in helds], others))
    return [
        (terms[:-1] + [(x, terms[-1][1])], rows)
        for (terms, rows), x in zip(helds, newest, strict=True)
    ], others


def to_rows(flat, rows):
    block = jnp.pad(flat.reshape(rows, D), ((0, 128 - rows), (0, 0)))
    tail = jnp.pad(block[:, 256:], ((0, 0), (0, 320 - D)))
    return jnp.concatenate(
        [block[:, :128], block[:, 128:256], jnp.concatenate([tail[:64], tail[64:]], axis=1)], axis=0
    )


def from_rows(packed, rows):
    tail = jnp.concatenate([packed[256:, : D - 256], packed[256:, 64 : D - 192]], axis=0)
    block = jnp.concatenate([packed[:128], packed[128:256], tail], axis=1)
    return block[:rows].reshape(-1)


def split_flat(vec):
    square = D * D
    wq, wk, wv, wo, we = (vec[i * square : (i + 1) * square].reshape(D, D) for i in range(5))
    at = 5 * square
    w1 = vec[at : at + D * FF].reshape(D, FF)
    at = at + D * FF
    w2 = vec[at : at + FF * D].reshape(FF, D)
    at = at + FF * D
    norm = jnp.pad(vec[at : at + 4 * D].reshape(4, D).astype(F32), ((0, 4), (0, 0)))
    wkv = jnp.concatenate([wk, jnp.zeros((D, STEP_COLUMNS - D), BF), wv], axis=1)
    return Bag(zip(WEIGHTS, (wq, wkv, wo, we, nn(wv, wo).astype(BF), w1, w2, norm), strict=True))


def halo(x):
    size = lax.axis_size("leaf")
    last, first = x
    left = lax.ppermute(last, "leaf", [(i, i + 1) for i in range(size - 1)])
    right = lax.ppermute(first, "leaf", [(i + 1, i) for i in range(size - 1)])
    return left, right


def local(
    weights,
    first_moment,
    second_moment,
    centers,
    leaves,
    edge_feats,
    center_cot,
    leaf_cot,
    edge_cot,
    graph_ids,
    star_sizes,
    leaf_mask,
    owner_list,
):
    sizes = {"graph": lax.axis_size("graph"), "leaf": lax.axis_size("leaf")}
    holders = sizes["graph"] * sizes["leaf"]
    block_len = weights.shape[1]
    block_rows = block_len // D
    in_rows = block_len % D == 0 and 64 < block_rows <= 128
    stars = centers.shape[1]
    own_rows = leaves.shape[1]
    leaf_rows = own_rows + 2 * HALO

    orders = [tree_stages(sizes, swap) for swap in (False, True)]
    me = lax.axis_index(("graph", "leaf"))
    leaf_bits = sizes["leaf"].bit_length() - 1
    slot = jnp.stack([tree_slot(owner_list ^ me, stages, leaf_bits) for stages in orders])
    nat_rows = ROWS_LAYER + 12
    nat = {"nat": ((3, nat_rows, 128), F32)}
    half = PACK // 2
    n_steps = len(orders[0])
    weights_low = weights.astype(BF)

    def gather_begin(rows):
        held = gather_step(jnp.concatenate(rows, axis=0)[None], orders[0][-1], sizes)
        size = rows[0].shape[0]
        return [held[:, :size], held[:, size:]]

    def gather_more(held, n):
        return [gather_step(h, o[n], sizes) for h, o in zip(held, orders, strict=True)]

    rows = [to_rows(x, block_rows) if in_rows else x for x in weights_low]
    held = gather_begin(rows)
    raw = dict(leaves=leaves[0], edges=edge_feats[0], lcot=leaf_cot[0], ecot=edge_cot[0])
    marks = jnp.pad((graph_ids + 1).astype(BF), ((0, 15), (0, 0)))
    marks = jnp.concatenate([marks[:8], jnp.broadcast_to(leaf_mask.astype(BF), (8, own_rows))], axis=0)

    def edge(cut):
        note = jnp.pad(marks[:, cut], ((0, 0), (0, D - HALO)))
        return jnp.concatenate([x[cut] for x in raw.values()] + [note], axis=0)

    left, right = halo((edge(slice(own_rows - HALO, own_rows)), edge(slice(0, HALO))))
    at = len(raw)
    raw, held = lax.optimization_barrier((raw, held))
    raw = dict(raw, halo_l=left, halo_r=right)

    def with_marks(line, mine):
        sides = [x[at * HALO + line, :HALO].astype(jnp.int32)[None] for x in (left, right)]
        return jnp.concatenate([sides[0], mine, sides[1]], axis=1)

    ids = with_marks(0, graph_ids + 1) - 1
    live = with_marks(8, leaf_mask).astype(F32)
    edge_id = jnp.full((1, 1), -1, jnp.int32)
    last = (ids != jnp.concatenate([ids[:, 1:], edge_id], axis=1)).astype(F32)
    first = graph_ids[0] != ids[0, HALO - 1 : HALO - 1 + own_rows]
    star_index = jnp.arange(stars, dtype=jnp.int32)
    star_own = jnp.any((star_index[:, None] == graph_ids) & first[None, :], axis=1)[:, None]
    scale = (jnp.log(star_sizes[0].astype(F32)) / (math.log(32.0) * math.sqrt(HEAD)))[:, None]
    base = Bag(
        idc=ids.reshape(-1, 1),
        idr=ids,
        live=live,
        last=last,
        scale=scale,
        cown=star_own.astype(F32),
    )
    saved = saved_shapes(stars, leaf_rows)
    rows = leaf_rows + stars
    if in_rows:
        grads_out = {k: ((holders, half, 128), BF) for k in ("keep", "send")}
        grads_scratch = {k: ((holders, half, 128), BF) for k in ("all_a", "all_b")} | nat
    else:
        grads_out, grads_scratch = nat, {}
    lazy = WEIGHTS[:-1] + tuple(f"{k}{i}" for k in WEIGHTS for i in range(LAYERS)) + ("yl0", "en0", "xl", "el", "gyl", "ge", "yl", "en") + (
        "kv", "hb", "xh1", "xh2", "act", "slope", "dz", "dkv", "gxl", "gel", "dbr", "dpre",
    )
    f_scratch = dict(cat=((2 * stars, PAIR), BF), z=((rows, D), F32))
    a_scratch = {"cat": ((2 * stars, PAIR + STEP_COLUMNS), BF), **leaf_shapes(leaf_rows, "mc", "m")}
    handed = dict(
        dz=((rows, D), BF),
        dkv=((leaf_rows, PAIR), BF),
        dq=((stars, D), BF),
        dkvc=((stars, PAIR), BF),
    )
    def halves_of(*names):
        return {k: raw[k] for k in (*names, "halo_l", "halo_r")}

    join = dict(xl=("leaves", 0), el=("edges", 1), gyl=("lcot", 2), ge=("ecot", 3))

    def joined(*names):
        return {k: join[k] for k in names}

    for n in range(n_steps - 2, 0, -1):
        held = gather_more(held, n)

    def end_grads(r):
        backward_attention(r, stars, leaf_rows)
        weight_grads(r, stars, leaf_rows, own_rows)
        if in_rows:
            pack_blocks(r, holders, block_rows)

    small = [k for k in saved if k not in lazy]

    def start_first(r):
        for copy in unpack_copies(r, 0, holders):
            copy.start()

    def front(r):
        zero = r.view({**{k: k + "0" for k in WEIGHTS}, "yl": "yl0", "en": "en0", "yc": "yc0"})
        names = {**{k: k + "1" for k in (*WEIGHTS, *small)}, "xl": "yl0", "el": "en0", "xc": "yc0"}
        one = r.view(names)
        one.update(dpre=r.slope, dbr=r.xh2)
        if in_rows:
            unpack_blocks(zero, 0, holders, block_rows)
            for copy in unpack_copies(r, 1, holders):
                copy.start()
        forward(zero, stars, leaf_rows)
        if in_rows:
            unpack_blocks(one, 1, holders, block_rows)
            one.update(all_a=r.got.at[:, : PACK // 2], all_b=r.got.at[:, PACK // 2 :])
        forward(one, stars, leaf_rows)
        backward_ffn(one, stars, leaf_rows, own_rows)
        end_grads(one)

    weight_specs = dict(zip(WEIGHTS, WEIGHT_SHAPES, strict=True))
    params, unpacked, kept, loose = [], {}, {}, {}
    for i, near in enumerate(held):
        far = exchange(near, orders[i][0], 1, sizes)
        if in_rows:
            loose.update({f"near{i}": near, f"far{i}": far})
            used = WEIGHTS if i == 0 else ("wq", "wkv", "we", "wvo")
            unpacked.update({f"{k}{i}": weight_specs[k] for k in used})
            kept.update({f"{k}{i}": weight_specs[k] for k in WEIGHTS if k not in used})
        else:
            flat = jnp.concatenate([near, far], axis=0)
            params.append(split_flat(jnp.take(flat, slot[i], axis=0).reshape(-1)))
    if in_rows:
        kept.update(got=((holders, PACK, 128), BF), sems=((2,), None))
        kept.update(nat)
    scratch = {**f_scratch, **a_scratch, "dn": ((4, 8, D), F32), **kept, **{k + "1": saved[k] for k in small}}
    scratch["z"] = ((rows, D), F32)
    two = call(
        front,
        {
            "slot": slot,
            **loose,
            **{f"{k}{i}": x[k] for i, x in enumerate(params) for k in WEIGHTS},
            **halves_of("leaves", "edges", "lcot", "ecot"),
            **base,
            "xc": centers[0],
            "gyc": center_cot[0],
        },
        {
            "yc0": ((stars, D), F32),
            "yc": ((stars, D), F32),
            **leaf_shapes(leaf_rows, "yl0", "en0"),
            **leaf_shapes(own_rows, "yl", "en"),
            **unpacked,
            **saved,
            **handed,
            **grads_out,
        },
        scratch,
        60,
        leaf_rows,
        in_smem=("slot",),
        lazy=lazy,
        joins=joined("xl", "el", "gyl", "ge"),
        own=("yl", "en"),
        name="front",
        loose=loose,
        early=start_first if in_rows else None,
    )
    one = two
    if in_rows:
        params = [Bag({k[:-1]: two[k] for k in unpacked if k[-1] == str(i)}) for i in range(LAYERS)]
    two_in = dict(xc=two.yc0, xl=two.yl0, el=two.en0, **halves_of("ecot"))

    def inputs_of(params, given, made, joins, out_rows, dtype, name):
        return call(
            lambda r: backward_inputs(r, stars, leaf_rows),
            {
                **{k: params[k] for k in ("wvo", "wkv", "we", "wq")},
                **{k: base[k] for k in ("idc", "idr")},
                **given,
                **{k: made[k] for k in handed},
            },
            {"gxc": ((stars, D), F32), "gxl": ((out_rows, D), dtype), "gel": ((out_rows, D), dtype)},
            {"xcat": ((2 * stars, D), BF)},
            9,
            leaf_rows,
            lazy=lazy,
            joins=joins,
            own=("gxl", "gel") if out_rows == own_rows else (),
            name=name,
            soon="ge",
        )

    def begin(made):
        if not in_rows:
            flat = jnp.swapaxes(made.nat[:, :ROWS_LAYER], 0, 1).reshape(ROWS_LAYER, 384)
            flat = flat[:, :D].reshape(holders, block_len)
            placed = jnp.zeros_like(flat).at[slot[0]].set(flat).astype(BF)
            return [reduce_step(([(placed, 0)], holders), orders[0][0], sizes)]
        got = exchange(made.send, orders[0][0], 1, sizes)
        count = holders // 2
        return [([(made.keep, i), (got, i)], count) for i in (0, count)]

    def advance(held, n):
        return [reduce_step(h, o[n], sizes) for h, o in zip(held, orders, strict=False)]

    def joined_total(held):
        rows = held[0][1]
        both = jnp.concatenate([total(h, 0, rows) for h in held], axis=1)
        return [([(both.astype(BF), 0)], rows)]

    def last_step(held):
        return reduce_step(held[0], orders[0][-1], sizes)

    def end(held):
        block = total(held, 0, 1)[0]
        return from_rows(block, block_rows) if in_rows else block

    held_two = begin(two)
    two_grads = inputs_of(params[1], two_in, two, joined("ge"), leaf_rows, BF, "last_inputs")
    held_two, (gyc,) = tie(held_two, two_grads.gxc)
    held_two = advance(held_two, 1)
    made = {"dz": handed["dz"], **ffn_scratch(stars, leaf_rows)}
    mid = call(
        lambda r: backward_ffn(r, stars, leaf_rows, own_rows),
        {
            "w2": params[0].w2,
            "gyl": two_grads.gxl,
            **{k: one[k] for k in ("xh2", "slope")},
            "w1": params[0].w1,
            "xh1": one.xh1,
            "norm": params[0].norm,
            "cown": base.cown,
            "gyc": gyc,
        },
        made,
        {},
        13,
        leaf_rows,
        lazy=lazy,
        name="first_ffn",
        soon="gyl",
    )
    held_two, (dn,) = tie(held_two, mid.dn)
    if n_steps > 2:
        held_two = advance(held_two, 2)
    ffn_names = ("xh2", "slope", "xh1")
    three = call(
        end_grads,
        {
            **{k: params[0][k] for k in ("wo", "wkv")},
            **mid,
            **{k: one[k] for k in saved if k not in ffn_names},
            **halves_of("leaves", "edges"),
            **base,
            "slot": slot,
            "xc": centers[0],
            "ge": two_grads.gel,
            "dn": dn,
        },
        {**{k: handed[k] for k in handed if k != "dz"}, **grads_out},
        {**a_scratch, **grads_scratch},
        18,
        leaf_rows,
        in_smem=("slot",),
        lazy=lazy,
        joins=joined("xl", "el"),
        name="first",
    )
    three["dz"] = mid.dz
    for n in range(3, n_steps - 1):
        held_two = advance(held_two, n)
    key = "send" if in_rows else "nat"
    held_two, (three[key],) = tie(held_two, three[key])
    held_three = begin(three)
    held_two = joined_total(held_two)
    count = len(held_two)
    both, (dq,) = tie(held_two + held_three, three.dq)
    held_three = both[count:]
    last_two = last_step(both[:count])
    handed_three = {**{k: three[k] for k in handed}, "dq": dq}
    held_three = advance(held_three, 1)
    three_in = dict(xc=centers[0], ge=two_grads.gel, **halves_of("leaves", "edges"))
    three_grads = inputs_of(
        params[0], three_in, handed_three, joined("xl", "el"), own_rows, F32, "first_inputs"
    )
    late = [x for x, _ in last_two[0][1:]]
    held_three, (gxc, yc, *late) = tie(held_three, three_grads.gxc, two.yc, *late)
    last_two = (last_two[0][:1] + [(x, 0) for x in late], last_two[1])
    center_rows = jnp.where(star_own, jnp.concatenate([yc, gxc], axis=1), 0.0)
    center_rows = center_rows + exchange(center_rows, ("leaf", 0, 1), 1, sizes)
    held_three = advance(held_three, 2) if n_steps > 3 else held_three
    for n in range(3, n_steps - 1):
        held_three = advance(held_three, n)
    held_three, (gxl, gel, yl, en, center_rows) = tie(
        held_three, three_grads.gxl, three_grads.gel, two.yl, two.en, center_rows
    )
    for bit in range(1, leaf_bits):
        center_rows = center_rows + exchange(center_rows, ("leaf", bit, 1), 1, sizes)
    centers_out, grad_centers = center_rows[:, :D].astype(BF), center_rows[:, D:]
    lasts, _ = tie([last_step(joined_total(held_three)), last_two])
    grad_total = jnp.stack([end(x) for x in lasts])
    first_new = BETA_ONE * first_moment + (1.0 - BETA_ONE) * grad_total
    second_new = BETA_TWO * second_moment + (1.0 - BETA_TWO) * grad_total * grad_total
    step_one = first_new / (1.0 - BETA_ONE**STEP)
    step_two = second_new / (1.0 - BETA_TWO**STEP)
    weights_new = weights - RATE * (step_one / (jnp.sqrt(step_two) + EPS_ADAM) + DECAY * weights)
    return (
        centers_out[None],
        yl[None],
        en[None],
        grad_centers[None],
        gxl[None],
        gel[None],
        first_new,
        second_new,
        weights_new,
        weights_new.astype(BF),
        grad_total,
    )


def solution(mesh):
    both = ("graph", "leaf")
    return jax.shard_map(
        local,
        mesh=mesh,
        in_specs=(
            P(None, both),
            P(None, both),
            P(None, both),
            P("graph", None, None),
            P("graph", "leaf", None),
            P("graph", "leaf", None),
            P("graph", None, None),
            P("graph", "leaf", None),
            P("graph", "leaf", None),
            P("graph", "leaf"),
            P("graph", None),
            P("graph", "leaf"),
            P(),
        ),
        out_specs=(
            P("graph", None, None),
            P("graph", "leaf", None),
            P("graph", "leaf", None),
            P("graph", None, None),
            P("graph", "leaf", None),
            P("graph", "leaf", None),
            P(None, both),
            P(None, both),
            P(None, both),
            P(None, both),
            P(None, both),
        ),
        check_vma=False,
    )
```
